32 devices in a mesh: dp: 4 (over y, x), expert: 8 (over z, core).
Axes of the slice: x: 2, y: 2, z: 4, core: 2. Of those that a mesh axis runs over, the one named last changes fastest.
Arguments:
- tokens: bfloat16 [1024, 2048], P('expert'), may hold values from -4 to 4
- norm_gain: bfloat16 [2048], replicated, may hold values from 0.5 to 1.5
- routing_projection_matrix: bfloat16 [2048, 8], replicated, may hold values from -0.125 to 0.125
- experts: int32 [1024, 8], P('expert'), may hold values from 0 to 7, as said below
- replica_key: int32 [1024, 8], P('expert'), may hold values from 0 to 1048575
- slot_expert: int32 [16], replicated, may hold values from 0 to 7, as said below
- capacity: int32 [16], replicated, may hold values from 4 to 16, as said below
- slot_gate_up_weight: bfloat16 [16, 2048, 2, 1024], P('expert', None, None, 'dp'), may hold values from -0.125 to 0.125
- down_weight: bfloat16 [16, 1024, 2048], P('expert', 'dp'), may hold values from -0.1875 to 0.1875
Outputs:
- mixed: bfloat16 [1024, 2048], P('expert', 'dp')
The draws below stay inside these ranges and needn't reach their ends.
Inputs may be any that keep to these rules, and one draw needn't show every extreme that they name: Each row names 8 different experts. `slot_expert`: every expert occupies at least one slot. `capacity`: for every j the capacities of slots 2 * j and 2 * j + 1 sum to at most 24, and to exactly 24 for some j.
All inputs are finite; a program needn't handle non-finite values.
Results may differ from the reference program's by a relative error of at most 0.012.
Values may be sent and summed in bfloat16 or wider, within the bound.
No kernel may reach another device: no remote copies, remote signals or barrier semaphores. Data moves between devices by JAX's collectives and lax.ppermute only.
A program may use at most 128 MiB of HBM per device.

```python
import jax
import jax.numpy as jnp
from jax import lax

D = 2048
FF = 1024
TOP = 8
SPECIALIST_COUNT = 8
SLOT_DEV = 2
SLOTS = 16
UNITS = 256
TOK_DEV = 128
TOKENS = 1024
CAPACITY_HIGH = 16
CAP_LO = 4
CAP_DEV = 24
N_EXPERT = 8


def plan(key):
    device_count = SLOTS // SLOT_DEV
    hot_count = max(SPECIALIST_COUNT // 8, 1)
    order = jax.random.permutation(jax.random.fold_in(key, 11), SPECIALIST_COUNT).astype(jnp.int32)
    hottest = order[:hot_count]
    extra = hottest[jax.random.randint(jax.random.fold_in(key, 12), (SLOTS - SPECIALIST_COUNT,), 0, hot_count)]
    table = jnp.concatenate([order, extra])
    table = table[jax.random.permutation(jax.random.fold_in(key, 13), SLOTS)].astype(jnp.int32)
    first = jax.random.randint(jax.random.fold_in(key, 14), (device_count,), CAP_LO, CAPACITY_HIGH + 1)
    upper = jnp.minimum(CAP_DEV - first, CAPACITY_HIGH)
    second = CAP_LO + jax.random.randint(jax.random.fold_in(key, 15), (device_count,), 0, 1 << 20) % (upper - CAP_LO + 1)
    special = jax.random.randint(jax.random.fold_in(key, 16), (), 0, device_count)
    devices = jnp.arange(device_count)
    first = jnp.where(devices == special, CAPACITY_HIGH, first)
    second = jnp.where(devices == special, CAP_DEV - CAPACITY_HIGH, second)
    lowest = (special + 1) % device_count
    second = jnp.where(devices == lowest, CAP_LO, second)
    capacity = jnp.stack([first, second], axis=1).reshape(SLOTS).astype(jnp.int32)
    selected_specialists = table[2 * special]
    holders = table == selected_specialists
    copies = jnp.sum(holders.astype(jnp.int32))
    before = jnp.sum((holders & (jnp.arange(SLOTS) < 2 * special)).astype(jnp.int32))
    is_hot = jnp.any(jnp.arange(SPECIALIST_COUNT)[:, None] == hottest[None, :], axis=1).astype(jnp.int32)
    minimal_share = jax.random.randint(jax.random.fold_in(key, 17), (TOKENS, SPECIALIST_COUNT), 0, 1 << 16) + (1 << 15) * is_hot[None, :]
    noise = jax.random.randint(jax.random.fold_in(key, 18), (TOKENS // TOK_DEV, TOK_DEV), 0, 1 << 20)
    distinct = noise * TOK_DEV + jnp.arange(TOK_DEV)[None, :]
    ranks = jnp.argsort(jnp.argsort(distinct, axis=1), axis=1)
    pinned_selection = (ranks < CAPACITY_HIGH).reshape(TOKENS)
    leftover_share = (pinned_selection[:, None] & (jnp.arange(SPECIALIST_COUNT)[None, :] == selected_specialists)).astype(jnp.int32) * (1 << 17)
    routing_logit_matrix = (minimal_share + leftover_share) * SPECIALIST_COUNT + jnp.arange(SPECIALIST_COUNT)[None, :]
    _, experts = lax.top_k(routing_logit_matrix, TOP)
    experts = experts.astype(jnp.int32)
    keyed = jax.random.randint(jax.random.fold_in(key, 19), (TOKENS, TOP), 0, 1 << 20)
    steer = pinned_selection[:, None] & (experts == selected_specialists)
    keyed = jnp.where(steer, before + copies * (keyed % 4096), keyed)
    topmost = (ranks.reshape(TOKENS) == TOK_DEV - 1) & (jnp.arange(TOKENS) < TOK_DEV)
    marked = topmost[:, None] & (jnp.arange(TOP)[None, :] == 0)
    keyed = jnp.where(marked, (1 << 20) - 1, keyed).astype(jnp.int32)
    return (table, capacity, experts, keyed)


def draw_experts(key, part):
    return plan(key)[2]


def draw_replica_key(key, part):
    return plan(key)[3]


def draw_slot_expert(key, part):
    return plan(key)[0]


def draw_capacity(key, part):
    return plan(key)[1]


def levels(key, extent, shards, least, high):
    level = 1.0
    for dim, parts in shards:
        steps = jax.random.uniform(jax.random.fold_in(jax.random.fold_in(key, 6), dim), (parts,), jnp.float32, least / len(shards), high / len(shards))
        level = level * jnp.repeat(jnp.exp(steps), extent[dim] // parts).reshape((-1,) + (1,) * (len(extent) - 1 - dim))
    return level


def bell_draw(stream_key, dims, scale, reach, pieces=(), kind=jnp.bfloat16):
    loudness = levels(stream_key, dims, pieces, -0.22, 0.18) if pieces else 1.0
    values = jax.random.normal(stream_key, dims, jnp.float32) * scale * loudness
    return jnp.minimum(jnp.maximum(values, -reach), reach).astype(kind)


def setup_inputs(seed: int = 0) -> dict:
    splits = jax.random.split(jax.random.key(seed), 10)
    return {
        "tokens": bell_draw(splits[0], (TOKENS, D), 0.5, 4.0, ((0, 8),)),
        "norm_gain": jnp.clip(1.0 + 0.1 * jax.random.normal(splits[1], (D,), jnp.float32), 0.5, 1.5).astype(jnp.bfloat16),
        "routing_projection_matrix": bell_draw(splits[2], (D, SPECIALIST_COUNT), D ** -0.5, 0.125),
        "experts": draw_experts(jax.random.fold_in(splits[9], 71), 0),
        "replica_key": draw_replica_key(jax.random.fold_in(splits[9], 71), 0),
        "slot_expert": draw_slot_expert(jax.random.fold_in(splits[9], 71), 0),
        "capacity": draw_capacity(jax.random.fold_in(splits[9], 71), 0),
        "slot_gate_up_weight": bell_draw(splits[7], (SLOTS, D, 2, FF), D ** -0.5, 0.125, ((0, 8), (3, 4))),
        "down_weight": bell_draw(splits[8], (SLOTS, FF, D), FF ** -0.5, 0.1875, ((0, 8), (1, 4))),
    }


def assign_slots(experts, replica_key, slot_expert):
    flat_experts = experts.reshape(-1)
    holders = (flat_experts[:, None] == slot_expert[None, :]).astype(jnp.int32)
    copies = lax.optimization_barrier(jnp.sum(holders, axis=1))
    earlier = jnp.cumsum(holders, axis=1) - holders
    wanted = replica_key.reshape(-1) % copies
    matched = holders * (earlier == wanted[:, None]).astype(jnp.int32)
    numbers = jnp.arange(slot_expert.shape[0], dtype=jnp.int32)
    return lax.optimization_barrier(jnp.sum(matched * numbers[None, :], axis=1)).astype(jnp.int32)

def block_positions(slot_ids):
    onehot = (slot_ids[:, None] == jnp.arange(SLOTS, dtype=jnp.int32)[None, :]).astype(jnp.int32)
    return lax.optimization_barrier(jnp.sum((jnp.cumsum(onehot, axis=0) - onehot) * onehot, axis=1)).astype(jnp.int32)

def reference(tokens, norm_gain, routing_projection_matrix, experts, replica_key, slot_expert, capacity, slot_gate_up_weight, down_weight):
    hidden = tokens.astype(jnp.float32)
    scale = lax.rsqrt(lax.optimization_barrier(jnp.mean(hidden * hidden, axis=-1, keepdims=True)) + 1e-06)
    normed = (hidden * scale * norm_gain.astype(jnp.float32)).astype(jnp.bfloat16)
    logits = jnp.dot(normed, routing_projection_matrix, preferred_element_type=jnp.float32)
    routing_logit_matrix = jax.nn.sigmoid(jnp.take_along_axis(logits, experts, axis=1)).reshape(-1)
    slot_ids = assign_slots(experts, replica_key, slot_expert)
    position = jax.vmap(block_positions)(slot_ids.reshape(N_EXPERT, TOK_DEV * TOP)).reshape(-1)
    kept_mask = position < capacity[slot_ids]
    pair_rows = jnp.arange(TOKENS * TOP, dtype=jnp.int32) // TOP
    blocks = pair_rows // TOK_DEV
    total = SLOTS * N_EXPERT * CAPACITY_HIGH
    target = jnp.where(kept_mask, (slot_ids * N_EXPERT + blocks) * CAPACITY_HIGH + position, total).astype(jnp.int32)
    row_table = jnp.zeros((total + 1,), jnp.int32).at[target].set(pair_rows)[:-1].reshape(SLOTS, N_EXPERT * CAPACITY_HIGH)
    kept_scores = jnp.where(kept_mask, routing_logit_matrix, jnp.float32(0.0))
    weight_table = jnp.zeros((total + 1,), jnp.float32).at[target].set(kept_scores)[:-1].reshape(SLOTS, N_EXPERT * CAPACITY_HIGH)

    def slot_step(mixture, inputs):
        rows, row_weights, gate_up_one, down_one = inputs
        picked = normed[rows]
        gate_up_out = jnp.dot(picked, gate_up_one.reshape(D, 2 * FF), preferred_element_type=jnp.float32)
        activated = (jax.nn.silu(gate_up_out[:, :FF]) * gate_up_out[:, FF:]).astype(jnp.bfloat16)
        result = jnp.zeros((rows.shape[0], D), jnp.float32)
        for section in range(FF // UNITS):
            lower = section * UNITS
            piece = jnp.dot(activated[:, lower:lower + UNITS], down_one[lower:lower + UNITS], preferred_element_type=jnp.float32)
            rounded = lax.optimization_barrier(piece.astype(jnp.bfloat16))
            result = result + rounded.astype(jnp.float32)
        mixture = mixture.at[rows].add(row_weights[:, None] * result)
        return (mixture, None)
    mixture, _ = lax.scan(slot_step, jnp.zeros((TOKENS, D), jnp.float32), (row_table, weight_table, slot_gate_up_weight, down_weight))
    return (hidden + mixture).astype(jnp.bfloat16)
```

```python
import functools

import jax
import jax.numpy as jnp
from jax import lax
from jax.experimental import pallas as pl
from jax.experimental.pallas import tpu as pltpu
from jax.sharding import PartitionSpec as P

CAP_DEV = 24


def to_column(row):
    n = row.shape[1]
    eye = lax.broadcasted_iota(jnp.int32, (n, n), 0) == lax.broadcasted_iota(
        jnp.int32, (n, n), 1
    )
    wide = jnp.where(eye, jnp.broadcast_to(row, (n, n)).astype(jnp.float32), 0.0)
    return jnp.sum(wide, axis=1, keepdims=True)


def place_rows(experts_t, keys_t, slot_row, cap_row, per_device):
    slots = slot_row.shape[1]
    picks, rows = experts_t.shape
    slot_f = slot_row.astype(jnp.float32)
    cap_f = cap_row.astype(jnp.float32)
    slot_col = to_column(slot_row)
    cap_col = to_column(cap_row)
    here = lax.broadcasted_iota(jnp.int32, (slots, slots), 0)
    other = lax.broadcasted_iota(jnp.int32, (slots, slots), 1)
    same = jnp.where(slot_f == slot_col, 1.0, 0.0)
    copies = jnp.sum(same, axis=1, keepdims=True)
    earlier = other < here
    place = jnp.sum(jnp.where(earlier, same, 0.0), axis=1, keepdims=True)
    together = (here // per_device) == (other // per_device)
    offset = jnp.sum(jnp.where(earlier & together, cap_f, 0.0), axis=1, keepdims=True)
    hit = jnp.zeros((slots, rows), jnp.float32)
    key = jnp.zeros((slots, rows), jnp.float32)
    experts_f = experts_t.astype(jnp.float32)
    keys_f = keys_t.astype(jnp.float32)
    for k in range(picks):
        match = experts_f[k : k + 1, :] == slot_col
        hit = jnp.where(match, 1.0, hit)
        key = jnp.where(match, keys_f[k : k + 1, :], key)
    rest = key - jnp.floor(key * (1.0 / copies)) * copies
    rest = jnp.where(rest < 0.0, rest + copies, rest)
    rest = jnp.where(rest >= copies, rest - copies, rest)
    chosen = (hit > 0.0) & (rest == place)
    before = lax.broadcasted_iota(jnp.int32, (rows, rows), 0) < lax.broadcasted_iota(
        jnp.int32, (rows, rows), 1
    )
    position = jnp.dot(
        jnp.where(chosen, 1.0, 0.0).astype(jnp.bfloat16),
        jnp.where(before, 1.0, 0.0).astype(jnp.bfloat16),
        preferred_element_type=jnp.float32,
    )
    return jnp.where(chosen & (position < cap_col), position + offset, -1.0)


def row_scale(hidden):
    return lax.rsqrt(jnp.mean(hidden * hidden, axis=-1, keepdims=True) + 1e-06)


def dispatch_kernel(
    per_device,
    tokens_ref,
    gain_ref,
    experts_ref,
    keys_ref,
    slot_ref,
    cap_ref,
    out_ref,
    local_ref,
):
    slots = slot_ref.shape[1]
    rows = tokens_ref.shape[0]
    width = out_ref.shape[1]
    hidden = tokens_ref[...].astype(jnp.float32)
    scale = row_scale(hidden)
    start = pl.multiple_of(lax.axis_index("dp") * width, width)
    part = tokens_ref[:, pl.ds(start, width)].astype(jnp.float32)
    gain = gain_ref[:, pl.ds(start, width)].astype(jnp.float32)
    normed = (part * scale * gain).astype(jnp.bfloat16)
    local = place_rows(
        experts_ref[...], keys_ref[...], slot_ref[...], cap_ref[...], per_device
    )
    local_ref[...] = local
    number = lax.broadcasted_iota(jnp.int32, (CAP_DEV, rows), 0).astype(jnp.float32)
    blocks = []
    for device in range(slots // per_device):
        block = jnp.zeros((CAP_DEV, rows), jnp.float32)
        for slot in range(device * per_device, (device + 1) * per_device):
            block = jnp.where(local[slot : slot + 1, :] == number, 1.0, block)
        blocks.append(block)
    pick = jnp.concatenate(blocks, axis=0).astype(jnp.bfloat16)
    out_ref[...] = jnp.dot(pick, normed, preferred_element_type=jnp.float32).astype(
        jnp.bfloat16
    )


def weight_kernel(
    per_device, tokens_ref, gain_ref, route_ref, slot_ref, local_ref, out_ref
):
    slots = slot_ref.shape[1]
    rows = tokens_ref.shape[0]
    hidden = tokens_ref[...].astype(jnp.float32)
    normed = (hidden * row_scale(hidden) * gain_ref[...].astype(jnp.float32)).astype(
        jnp.bfloat16
    )
    logits = lax.dot_general(
        route_ref[...],
        normed,
        (((1,), (1,)), ((), ())),
        preferred_element_type=jnp.float32,
    )
    score = 1.0 / (1.0 + jnp.exp(-logits))
    slot_col = to_column(slot_ref[...])
    by_slot = jnp.zeros((slots, rows), jnp.float32)
    for expert in range(route_ref.shape[0]):
        by_slot = jnp.where(slot_col == expert, score[expert : expert + 1, :], by_slot)
    local = local_ref[...]
    number = lax.broadcasted_iota(jnp.int32, (CAP_DEV, rows), 0).astype(jnp.float32)
    blocks = []
    for device in range(slots // per_device):
        block = jnp.zeros((CAP_DEV, rows), jnp.float32)
        for slot in range(device * per_device, (device + 1) * per_device):
            block = jnp.where(
                local[slot : slot + 1, :] == number, by_slot[slot : slot + 1, :], block
            )
        blocks.append(block)
    out_ref[...] = jnp.concatenate(blocks, axis=0).astype(jnp.bfloat16)


def on_device(
    tokens,
    norm_gain,
    routing_projection_matrix,
    experts,
    replica_key,
    slot_expert,
    capacity,
    slot_gate_up_weight,
    down_weight,
):
    peers = lax.axis_size("expert")
    groups = lax.axis_size("dp")
    group = lax.axis_index("dp")
    rows, width = tokens.shape
    slots = slot_expert.shape[0]
    per_device = slots // peers
    units = slot_gate_up_weight.shape[3]
    quarter = width // groups
    total = peers * CAP_DEV

    gain = norm_gain.reshape(1, width)
    slot_row = slot_expert.reshape(1, slots)
    cap_row = capacity.reshape(1, slots)
    outgoing, local = pl.pallas_call(
        functools.partial(dispatch_kernel, per_device),
        out_shape=(
            jax.ShapeDtypeStruct((total, quarter), jnp.bfloat16),
            jax.ShapeDtypeStruct((slots, rows), jnp.float32),
        ),
        name="dispatch",
    )(tokens, gain, experts.T, replica_key.T, slot_row, cap_row)
    weights = pl.pallas_call(
        functools.partial(weight_kernel, per_device),
        out_shape=jax.ShapeDtypeStruct((total, rows), jnp.bfloat16),
        name="combine_weights",
    )(tokens, gain, routing_projection_matrix.T, slot_row, local)

    def swap(value, step):
        return lax.ppermute(value, "dp", [(i, i ^ step) for i in range(groups)])

    def exchange(value):
        return lax.all_to_all(
            value.reshape(peers, CAP_DEV, quarter), "expert", 0, 0, tiled=True
        ).reshape(total, quarter)

    own = exchange(outgoing)
    gate_up = None
    for step in range(groups):
        rows_in = own if step == 0 else swap(own, step)
        start = (group ^ step) * quarter
        part = lax.dynamic_slice_in_dim(slot_gate_up_weight, start, quarter, 1)
        part = part.transpose(1, 0, 2, 3).reshape(quarter, per_device * 2 * units)
        term = jnp.dot(rows_in, part, preferred_element_type=jnp.float32)
        gate_up = term if gate_up is None else gate_up + term

    expert = lax.axis_index("expert")
    caps = lax.dynamic_slice_in_dim(capacity, expert * per_device, per_device)
    ends = jnp.cumsum(caps)
    number = lax.broadcasted_iota(jnp.int32, (peers, CAP_DEV, 1), 1).reshape(total, 1)
    pieces = []
    for slot in range(per_device):
        gate = gate_up[:, 2 * slot * units : (2 * slot + 1) * units]
        up = gate_up[:, (2 * slot + 1) * units : (2 * slot + 2) * units]
        mine = (number >= ends[slot] - caps[slot]) & (number < ends[slot])
        pieces.append(jnp.where(mine, jax.nn.silu(gate) * up, 0.0).astype(jnp.bfloat16))
    activated = jnp.concatenate(pieces, axis=1)
    down = down_weight.reshape(per_device * units, width)
    summed = None
    for step in reversed(range(groups)):
        start = (group ^ step) * quarter
        part = lax.dynamic_slice_in_dim(down, start, quarter, 1)
        term = jnp.dot(activated, part, preferred_element_type=jnp.float32)
        term = term.astype(jnp.bfloat16)
        if step:
            term = swap(term, step)
        term = term.astype(jnp.float32)
        summed = term if summed is None else summed + term
    returned = exchange(summed.astype(jnp.bfloat16))
    mixture = lax.dot_general(
        weights, returned, (((0,), (0,)), ((), ())), preferred_element_type=jnp.float32
    )
    residual = lax.dynamic_slice_in_dim(tokens, group * quarter, quarter, 1)
    return (residual.astype(jnp.float32) + mixture).astype(jnp.bfloat16)


def solution(mesh):
    in_specs = (
        P("expert", None),
        P(),
        P(),
        P("expert", None),
        P("expert", None),
        P(),
        P(),
        P("expert", None, None, "dp"),
        P("expert", "dp", None),
    )
    return jax.shard_map(
        on_device,
        mesh=mesh,
        in_specs=in_specs,
        out_specs=P("expert", "dp"),
        check_vma=False,
    )
```

```python
import functools

import jax
import jax.numpy as jnp
from jax import lax
from jax.experimental import pallas as pl
from jax.experimental.pallas import tpu as pltpu
from jax.sharding import PartitionSpec as P

CAP_DEV = 24


def to_column(row):
    n = row.shape[1]
    eye = lax.broadcasted_iota(jnp.int32, (n, n), 0) == lax.broadcasted_iota(
        jnp.int32, (n, n), 1
    )
    wide = jnp.where(eye, jnp.broadcast_to(row, (n, n)).astype(jnp.float32), 0.0)
    return jnp.sum(wide, axis=1, keepdims=True)


def place_rows(experts_t, keys_t, slot_row, cap_row, per_device):
    slots = slot_row.shape[1]
    picks, rows = experts_t.shape
    slot_f = slot_row.astype(jnp.float32)
    cap_f = cap_row.astype(jnp.float32)
    slot_col = to_column(slot_row)
    cap_col = to_column(cap_row)
    here = lax.broadcasted_iota(jnp.int32, (slots, slots), 0)
    other = lax.broadcasted_iota(jnp.int32, (slots, slots), 1)
    same = jnp.where(slot_f == slot_col, 1.0, 0.0)
    copies = jnp.sum(same, axis=1, keepdims=True)
    earlier = other < here
    place = jnp.sum(jnp.where(earlier, same, 0.0), axis=1, keepdims=True)
    together = (here // per_device) == (other // per_device)
    offset = jnp.sum(jnp.where(earlier & together, cap_f, 0.0), axis=1, keepdims=True)
    hit = jnp.zeros((slots, rows), jnp.float32)
    key = jnp.zeros((slots, rows), jnp.float32)
    experts_f = experts_t.astype(jnp.float32)
    keys_f = keys_t.astype(jnp.float32)
    for k in range(picks):
        match = experts_f[k : k + 1, :] == slot_col
        hit = jnp.where(match, 1.0, hit)
        key = jnp.where(match, keys_f[k : k + 1, :], key)
    rest = key - jnp.floor(key * (1.0 / copies)) * copies
    rest = jnp.where(rest < 0.0, rest + copies, rest)
    rest = jnp.where(rest >= copies, rest - copies, rest)
    chosen = (hit > 0.0) & (rest == place)
    before = lax.broadcasted_iota(jnp.int32, (rows, rows), 0) < lax.broadcasted_iota(
        jnp.int32, (rows, rows), 1
    )
    position = jnp.dot(
        jnp.where(chosen, 1.0, 0.0).astype(jnp.bfloat16),
        jnp.where(before, 1.0, 0.0).astype(jnp.bfloat16),
        preferred_element_type=jnp.float32,
    )
    return jnp.where(chosen & (position < cap_col), position + offset, -1.0)


def row_scale(hidden):
    return lax.rsqrt(jnp.mean(hidden * hidden, axis=-1, keepdims=True) + 1e-06)


def apply_gain(scaled, gain_ref, first):
    gain = gain_ref[...].astype(jnp.float32)
    number = lax.broadcasted_iota(jnp.int32, gain.shape, 0)
    parts = []
    for index in range(scaled.shape[1] // 128):
        row = jnp.sum(
            jnp.where(number == first + index, gain, 0.0), axis=0, keepdims=True
        )
        parts.append(
            (scaled[:, index * 128 : (index + 1) * 128] * row).astype(jnp.bfloat16)
        )
    return jnp.concatenate(parts, axis=1)


def dispatch_kernel(
    per_device,
    tokens_ref,
    gain_ref,
    experts_ref,
    keys_ref,
    slot_ref,
    cap_ref,
    out_ref,
    local_ref,
):
    slots = slot_ref.shape[1]
    rows = tokens_ref.shape[0]
    width = out_ref.shape[1]
    hidden = tokens_ref[...].astype(jnp.float32)
    scale = row_scale(hidden)
    start = pl.multiple_of(lax.axis_index("dp") * width, width)
    part = tokens_ref[:, pl.ds(start, width)].astype(jnp.float32)
    normed = apply_gain(part * scale, gain_ref, lax.axis_index("dp") * (width // 128))
    local = place_rows(
        experts_ref[...], keys_ref[...], slot_ref[...], cap_ref[...], per_device
    )
    local_ref[...] = local
    number = lax.broadcasted_iota(jnp.int32, (CAP_DEV, rows), 0).astype(jnp.float32)
    blocks = []
    for device in range(slots // per_device):
        block = jnp.zeros((CAP_DEV, rows), jnp.float32)
        for slot in range(device * per_device, (device + 1) * per_device):
            block = jnp.where(local[slot : slot + 1, :] == number, 1.0, block)
        blocks.append(block)
    pick = jnp.concatenate(blocks, axis=0).astype(jnp.bfloat16)
    out_ref[...] = jnp.dot(pick, normed, preferred_element_type=jnp.float32).astype(
        jnp.bfloat16
    )


def weight_kernel(
    per_device,
    tokens_ref,
    gain_ref,
    route_ref,
    slot_ref,
    local_ref,
    out_ref,
    residual_ref,
):
    quarter = residual_ref.shape[1]
    start = pl.multiple_of(lax.axis_index("dp") * quarter, quarter)
    residual_ref[...] = tokens_ref[:, pl.ds(start, quarter)]
    slots = slot_ref.shape[1]
    rows = tokens_ref.shape[0]
    hidden = tokens_ref[...].astype(jnp.float32)
    normed = apply_gain(hidden * row_scale(hidden), gain_ref, 0)
    logits = lax.dot_general(
        route_ref[...],
        normed,
        (((1,), (1,)), ((), ())),
        preferred_element_type=jnp.float32,
    )
    score = 1.0 / (1.0 + jnp.exp(-logits))
    slot_col = to_column(slot_ref[...])
    by_slot = jnp.zeros((slots, rows), jnp.float32)
    for expert in range(route_ref.shape[0]):
        by_slot = jnp.where(slot_col == expert, score[expert : expert + 1, :], by_slot)
    local = local_ref[...]
    number = lax.broadcasted_iota(jnp.int32, (CAP_DEV, rows), 0).astype(jnp.float32)
    blocks = []
    for device in range(slots // per_device):
        block = jnp.zeros((CAP_DEV, rows), jnp.float32)
        for slot in range(device * per_device, (device + 1) * per_device):
            block = jnp.where(
                local[slot : slot + 1, :] == number, by_slot[slot : slot + 1, :], block
            )
        blocks.append(block)
    out_ref[...] = jnp.concatenate(blocks, axis=0).T.astype(jnp.bfloat16)


def split_kernel(halves, per_device, cap_ref, in_ref, out_ref, mask_ref):
    tile = 256
    kinds = 2 * halves
    per_tile = tile // kinds
    to_row = lax.broadcasted_iota(jnp.int32, (tile, tile), 0)
    from_row = lax.broadcasted_iota(jnp.int32, (tile, tile), 1)
    column = to_row // per_tile
    source = (to_row % per_tile) * kinds + (column % halves) * 2 + column // halves
    order = jnp.where(source == from_row, 1.0, 0.0).astype(jnp.bfloat16)
    for index in range(0, in_ref.shape[1] // tile, 2):
        low = index * tile
        pair = jnp.concatenate(
            [in_ref[0, low : low + tile, :], in_ref[0, low + tile : low + 2 * tile, :]],
            axis=1,
        )
        moved = jnp.dot(order, pair, preferred_element_type=jnp.float32)
        moved = moved.astype(jnp.bfloat16)
        for side in range(2):
            top = (index + side) * per_tile
            for kind in range(kinds):
                out_ref[0, top : top + per_tile, kind * 128 : (kind + 1) * 128] = moved[
                    kind * per_tile : (kind + 1) * per_tile,
                    side * 128 : (side + 1) * 128,
                ]

    @pl.when((pl.program_id(0) == 0) & (pl.program_id(1) == 0))
    def _():
        units = halves * 128
        first = lax.axis_index("expert") * per_device
        caps = cap_ref[...].astype(jnp.float32)
        lane = lax.broadcasted_iota(jnp.int32, caps.shape, 1)
        number = lax.broadcasted_iota(jnp.int32, (CAP_DEV, units), 0)
        number = number.astype(jnp.float32)
        end = jnp.zeros((1, 1), jnp.float32)
        parts = []
        for slot in range(per_device):
            begin = end
            cap = jnp.sum(
                jnp.where(lane == first + slot, caps, 0.0), axis=1, keepdims=True
            )
            end = begin + cap
            parts.append(jnp.where((number >= begin) & (number < end), 1.0, 0.0))
        block = jnp.concatenate(parts, axis=1)
        copies = mask_ref.shape[0] // CAP_DEV
        mask_ref[...] = jnp.concatenate([block] * copies, axis=0).astype(jnp.bfloat16)


def split_weights(weight, cap_row, groups, peers):
    slots, width, _, units = weight.shape
    halves = units // 128
    quarter = width // groups
    rows = weight.reshape(slots, width, 2, halves, 128).transpose(0, 1, 3, 2, 4)
    rows = rows.reshape(slots, width * 2 * halves, 128)
    return pl.pallas_call(
        functools.partial(split_kernel, halves, slots),
        grid=(groups, slots),
        in_specs=[
            pl.BlockSpec(cap_row.shape, lambda step, slot: (0, 0)),
            pl.BlockSpec(
                (1, quarter * 2 * halves, 128),
                lambda step, slot: (slot, lax.axis_index("dp") ^ step, 0),
            ),
        ],
        out_specs=(
            pl.BlockSpec((1, quarter, 2 * units), lambda step, slot: (step, 0, slot)),
            pl.BlockSpec((peers * CAP_DEV, slots * units), lambda step, slot: (0, 0)),
        ),
        out_shape=(
            jax.ShapeDtypeStruct((groups, quarter, slots * 2 * units), jnp.bfloat16),
            jax.ShapeDtypeStruct((peers * CAP_DEV, slots * units), jnp.bfloat16),
        ),
        cost_estimate=pl.CostEstimate(
            flops=2 * 256 * weight.size,
            bytes_accessed=4 * weight.size,
            transcendentals=0,
        ),
        name="split_gate_up",
    )(cap_row, rows)


def on_device(
    tokens,
    norm_gain,
    routing_projection_matrix,
    experts,
    replica_key,
    slot_expert,
    capacity,
    slot_gate_up_weight,
    down_weight,
):
    peers = lax.axis_size("expert")
    groups = lax.axis_size("dp")
    group = lax.axis_index("dp")
    rows, width = tokens.shape
    slots = slot_expert.shape[0]
    per_device = slots // peers
    units = slot_gate_up_weight.shape[3]
    quarter = width // groups
    total = peers * CAP_DEV

    gain = norm_gain.reshape(width // 128, 128)
    slot_row = slot_expert.reshape(1, slots)
    cap_row = capacity.reshape(1, slots)
    outgoing, local = pl.pallas_call(
        functools.partial(dispatch_kernel, per_device),
        out_shape=(
            jax.ShapeDtypeStruct((total, quarter), jnp.bfloat16),
            jax.ShapeDtypeStruct((slots, rows), jnp.float32),
        ),
        name="dispatch",
    )(tokens, gain, experts.T, replica_key.T, slot_row, cap_row)
    weights, residual = pl.pallas_call(
        functools.partial(weight_kernel, per_device),
        out_shape=(
            jax.ShapeDtypeStruct((rows, total), jnp.bfloat16),
            jax.ShapeDtypeStruct((rows, quarter), jnp.bfloat16),
        ),
        name="combine_weights",
    )(tokens, gain, routing_projection_matrix.T, slot_row, local)

    def swap(value, step):
        return lax.ppermute(value, "dp", [(i, i ^ step) for i in range(groups)])

    def exchange(value):
        return lax.all_to_all(
            value.reshape(peers, CAP_DEV, quarter), "expert", 0, 0, tiled=True
        ).reshape(total, quarter)

    own = exchange(outgoing)
    gate_up_parts, mask = split_weights(slot_gate_up_weight, cap_row, groups, peers)
    gate_up = None
    for step in range(groups):
        rows_in = own if step == 0 else swap(own, step)
        term = jnp.dot(rows_in, gate_up_parts[step], preferred_element_type=jnp.float32)
        gate_up = term if gate_up is None else gate_up + term

    pieces = []
    for slot in range(per_device):
        gate = gate_up[:, 2 * slot * units : (2 * slot + 1) * units]
        up = gate_up[:, (2 * slot + 1) * units : (2 * slot + 2) * units]
        pieces.append((jax.nn.silu(gate) * up).astype(jnp.bfloat16))
    activated = jnp.where(mask > 0, jnp.concatenate(pieces, axis=1), 0)
    down = down_weight.reshape(per_device * units, width)
    summed = None
    for step in reversed(range(groups)):
        start = (group ^ step) * quarter
        part = lax.dynamic_slice_in_dim(down, start, quarter, 1)
        term = jnp.dot(activated, part, preferred_element_type=jnp.float32)
        term = term.astype(jnp.bfloat16)
        if step:
            term = swap(term, step)
        term = term.astype(jnp.float32)
        summed = term if summed is None else summed + term
    returned = exchange(summed.astype(jnp.bfloat16))
    mixture = jnp.dot(weights, returned, preferred_element_type=jnp.float32)
    return (residual.astype(jnp.float32) + mixture).astype(jnp.bfloat16)


def solution(mesh):
    in_specs = (
        P("expert", None),
        P(),
        P(),
        P("expert", None),
        P("expert", None),
        P(),
        P(),
        P("expert", None, None, "dp"),
        P("expert", "dp", None),
    )
    return jax.shard_map(
        on_device,
        mesh=mesh,
        in_specs=in_specs,
        out_specs=P("expert", "dp"),
        check_vma=False,
    )
```

```python
import functools

import jax
import jax.numpy as jnp
from jax import lax
from jax.experimental import pallas as pl
from jax.experimental.pallas import tpu as pltpu
from jax.sharding import PartitionSpec as P

CAP_DEV = 24
NEAR = 4


def to_column(row):
    n = row.shape[1]
    eye = lax.broadcasted_iota(jnp.int32, (n, n), 0) == lax.broadcasted_iota(
        jnp.int32, (n, n), 1
    )
    wide = jnp.where(eye, jnp.broadcast_to(row, (n, n)).astype(jnp.float32), 0.0)
    return jnp.sum(wide, axis=1, keepdims=True)


def place_rows(experts_t, keys_t, slot_row, cap_row, per_device):
    slots = slot_row.shape[1]
    picks, rows = experts_t.shape
    slot_f = slot_row.astype(jnp.float32)
    cap_f = cap_row.astype(jnp.float32)
    slot_col = to_column(slot_row)
    cap_col = to_column(cap_row)
    here = lax.broadcasted_iota(jnp.int32, (slots, slots), 0)
    other = lax.broadcasted_iota(jnp.int32, (slots, slots), 1)
    same = jnp.where(slot_f == slot_col, 1.0, 0.0)
    copies = jnp.sum(same, axis=1, keepdims=True)
    earlier = other < here
    place = jnp.sum(jnp.where(earlier, same, 0.0), axis=1, keepdims=True)
    together = (here // per_device) == (other // per_device)
    offset = jnp.sum(jnp.where(earlier & together, cap_f, 0.0), axis=1, keepdims=True)
    hit = jnp.zeros((slots, rows), jnp.float32)
    key = jnp.zeros((slots, rows), jnp.float32)
    experts_f = experts_t.astype(jnp.float32)
    keys_f = keys_t.astype(jnp.float32)
    for k in range(picks):
        match = experts_f[k : k + 1, :] == slot_col
        hit = jnp.where(match, 1.0, hit)
        key = jnp.where(match, keys_f[k : k + 1, :], key)
    rest = key - jnp.floor(key * (1.0 / copies)) * copies
    rest = jnp.where(rest < 0.0, rest + copies, rest)
    rest = jnp.where(rest >= copies, rest - copies, rest)
    chosen = (hit > 0.0) & (rest == place)
    before = lax.broadcasted_iota(jnp.int32, (rows, rows), 0) < lax.broadcasted_iota(
        jnp.int32, (rows, rows), 1
    )
    position = jnp.dot(
        jnp.where(chosen, 1.0, 0.0).astype(jnp.bfloat16),
        jnp.where(before, 1.0, 0.0).astype(jnp.bfloat16),
        preferred_element_type=jnp.float32,
    )
    return jnp.where(chosen & (position < cap_col), position + offset, -1.0)


def row_scale(hidden):
    return lax.rsqrt(jnp.mean(hidden * hidden, axis=-1, keepdims=True) + 1e-06)


def apply_gain(scaled, gain, first):
    number = lax.broadcasted_iota(jnp.int32, gain.shape, 0)
    parts = []
    for index in range(scaled.shape[1] // 128):
        row = jnp.sum(
            jnp.where(number == first + index, gain, 0.0), axis=0, keepdims=True
        )
        parts.append(
            (scaled[:, index * 128 : (index + 1) * 128] * row).astype(jnp.bfloat16)
        )
    return jnp.concatenate(parts, axis=1)


def pick_rows(local_ref, value_ref, steps, per_device):
    rows = local_ref.shape[1]
    me = lax.axis_index("expert")
    number = lax.broadcasted_iota(jnp.int32, (CAP_DEV, rows), 0).astype(jnp.float32)
    blocks = []
    for step in steps:
        block = jnp.zeros((CAP_DEV, rows), jnp.float32)
        for index in range(per_device):
            slot = (me ^ step) * per_device + index
            value = 1.0 if value_ref is None else value_ref[pl.ds(slot, 1), :]
            block = jnp.where(local_ref[pl.ds(slot, 1), :] == number, value, block)
        blocks.append(block)
    return jnp.concatenate(blocks, axis=0)


def store_blocks(refs, value):
    for index, ref in enumerate(refs):
        ref[...] = value[index * CAP_DEV : (index + 1) * CAP_DEV, :].astype(ref.dtype)


def load_blocks(refs):
    return jnp.concatenate([ref[...].astype(jnp.float32) for ref in refs], axis=0)


def dispatch_kernel(per_device, steps, *refs):
    tokens_hbm, *small_hbm = refs[:6]
    tokens_ref, gain_ref, local_ref, *out_refs = refs[6 : 9 + len(steps)]
    experts_ref, keys_ref, slot_ref, cap_ref, arrived = refs[9 + len(steps) :]
    small_refs = (experts_ref, keys_ref, slot_ref, cap_ref, gain_ref)
    copies = [
        pltpu.make_async_copy(source, target, arrived.at[index])
        for index, (source, target) in enumerate(
            zip((*small_hbm, tokens_hbm), (*small_refs, tokens_ref))
        )
    ]
    for copy in copies:
        copy.start()
    for copy in copies[:-1]:
        copy.wait()
    local_ref[...] = place_rows(
        experts_ref[...], keys_ref[...], slot_ref[...], cap_ref[...], per_device
    )
    pick = pick_rows(local_ref, None, steps, per_device).astype(jnp.bfloat16)
    gain = gain_ref[...].astype(jnp.float32)
    width = out_refs[0].shape[1]
    group = lax.axis_index("dp")
    copies[-1].wait()
    scale = row_scale(tokens_ref[...].astype(jnp.float32))
    start = pl.multiple_of(group * width, width)
    part = tokens_ref[:, pl.ds(start, width)].astype(jnp.float32)
    normed = apply_gain(part * scale, gain, group * (width // 128))
    store_blocks(out_refs, jnp.dot(pick, normed, preferred_element_type=jnp.float32))


def near_kernel(
    per_device, groups, steps, tokens_ref, gain_ref, local_ref, *out_refs
):
    gain = gain_ref[...].astype(jnp.float32)
    width = tokens_ref.shape[1] // groups
    group = lax.axis_index("dp")
    scale = row_scale(tokens_ref[...].astype(jnp.float32))
    pick = pick_rows(local_ref, None, steps, per_device).astype(jnp.bfloat16)
    for step in range(groups):
        start = pl.multiple_of((group ^ step) * width, width)
        part = tokens_ref[:, pl.ds(start, width)].astype(jnp.float32)
        normed = apply_gain(part * scale, gain, (group ^ step) * (width // 128))
        value = jnp.dot(pick, normed, preferred_element_type=jnp.float32)
        for index, ref in enumerate(out_refs):
            ref[:, step * width : (step + 1) * width] = value[
                index * CAP_DEV : (index + 1) * CAP_DEV, :
            ].astype(ref.dtype)


def weight_kernel(
    per_device,
    steps,
    tokens_ref,
    gain_ref,
    route_ref,
    slot_ref,
    local_ref,
    out_ref,
    residual_ref,
    score_ref,
):
    quarter = residual_ref.shape[1]
    start = pl.multiple_of(lax.axis_index("dp") * quarter, quarter)
    residual_ref[...] = tokens_ref[:, pl.ds(start, quarter)]
    slots = slot_ref.shape[1]
    rows = tokens_ref.shape[0]
    hidden = tokens_ref[...].astype(jnp.float32)
    gain = gain_ref[...].astype(jnp.float32)
    normed = apply_gain(hidden * row_scale(hidden), gain, 0)
    logits = lax.dot_general(
        route_ref[...],
        normed,
        (((1,), (1,)), ((), ())),
        preferred_element_type=jnp.float32,
    )
    score = 1.0 / (1.0 + jnp.exp(-logits))
    slot_col = to_column(slot_ref[...])
    by_slot = jnp.zeros((slots, rows), jnp.float32)
    for expert in range(route_ref.shape[0]):
        by_slot = jnp.where(slot_col == expert, score[expert : expert + 1, :], by_slot)
    score_ref[...] = by_slot
    weights = pick_rows(local_ref, score_ref, steps, per_device)
    out_ref[...] = weights.T.astype(jnp.bfloat16)


def split_kernel(halves, groups, in_hbm, out_ref, in_ref, arrived):
    tile = 256
    kinds = 2 * halves
    per_tile = tile // kinds
    slots, length, _ = in_hbm.shape
    part = length // groups
    group = lax.axis_index("dp")
    copies = []
    for step in range(groups):
        base = pl.multiple_of((group ^ step) * part, part)
        copies.append(
            pltpu.make_async_copy(
                in_hbm.at[:, pl.ds(base, part), :], in_ref.at[step], arrived.at[step]
            )
        )
        copies[-1].start()
    to_row = lax.broadcasted_iota(jnp.int32, (tile, tile), 0)
    from_row = lax.broadcasted_iota(jnp.int32, (tile, tile), 1)
    column = to_row // per_tile
    source = (to_row % per_tile) * kinds + (column % halves) * 2 + column // halves
    order = jnp.where(source == from_row, 1.0, 0.0).astype(jnp.bfloat16)
    for step in range(groups):
        copies[step].wait()
        for slot in range(slots):
            for index in range(0, part // tile, 2):
                low = index * tile
                pair = [
                    in_ref[step, slot, low + side * tile : low + (side + 1) * tile, :]
                    for side in range(2)
                ]
                moved = jnp.dot(
                    order,
                    jnp.concatenate(pair, axis=1),
                    preferred_element_type=jnp.float32,
                ).astype(jnp.bfloat16)
                for side in range(2):
                    top = (index + side) * per_tile
                    for kind in range(kinds):
                        left = (slot * kinds + kind) * 128
                        out_ref[step, top : top + per_tile, left : left + 128] = moved[
                            kind * per_tile : (kind + 1) * per_tile,
                            side * 128 : (side + 1) * 128,
                        ]


def slot_mask(cap_ref, per_device, units):
    first = lax.axis_index("expert") * per_device
    caps = cap_ref[...].astype(jnp.float32)
    lane = lax.broadcasted_iota(jnp.int32, caps.shape, 1)
    number = lax.broadcasted_iota(jnp.int32, (CAP_DEV, units), 0).astype(jnp.float32)
    end = jnp.zeros((1, 1), jnp.float32)
    parts = []
    for slot in range(per_device):
        begin = end
        end = begin + jnp.sum(
            jnp.where(lane == first + slot, caps, 0.0), axis=1, keepdims=True
        )
        parts.append(jnp.where((number >= begin) & (number < end), 1.0, 0.0))
    return jnp.concatenate(parts, axis=1)


def finish_rows(gate_up, cap_ref, down_ref, out_refs, per_device):
    units = down_ref.shape[0] // per_device
    mask = slot_mask(cap_ref, per_device, units)
    mask = jnp.concatenate([mask] * (gate_up.shape[0] // CAP_DEV), axis=0)
    pieces = []
    for slot in range(per_device):
        left = 2 * slot * units
        gate = gate_up[:, left : left + units]
        up = gate_up[:, left + units : left + 2 * units]
        pieces.append(gate / (1.0 + jnp.exp(-gate)) * up)
    activated = jnp.where(mask > 0.0, jnp.concatenate(pieces, axis=1), 0.0)
    activated = activated.astype(jnp.bfloat16)
    group = lax.axis_index("dp")
    for step, ref in enumerate(out_refs):
        width = ref.shape[1]
        start = pl.multiple_of((group ^ step) * width, width)
        ref[...] = jnp.dot(
            activated,
            down_ref[:, pl.ds(start, width)],
            preferred_element_type=jnp.float32,
        ).astype(ref.dtype)


def far_kernel(
    per_device, sum_ref, last_ref, weight_ref, cap_ref, down_ref, *out_refs
):
    gate_up = sum_ref[...] + jnp.dot(
        last_ref[...],
        weight_ref[weight_ref.shape[0] - 1],
        preferred_element_type=jnp.float32,
    )
    finish_rows(gate_up, cap_ref, down_ref, out_refs, per_device)


def near_expert_kernel(per_device, count, *refs):
    row_refs, (weight_ref, cap_ref, down_ref, *out_refs) = refs[:count], refs[count:]
    rows = load_blocks(row_refs).astype(jnp.bfloat16)
    width = weight_ref.shape[1]
    gate_up = None
    for step in range(weight_ref.shape[0]):
        term = jnp.dot(
            rows[:, step * width : (step + 1) * width],
            weight_ref[step],
            preferred_element_type=jnp.float32,
        )
        gate_up = term if gate_up is None else gate_up + term
    finish_rows(gate_up, cap_ref, down_ref, out_refs, per_device)


def join_kernel(*refs):
    refs[-1][...] = load_blocks(refs[:-1]).astype(refs[-1].dtype)


def sum_kernel(count, *refs):
    total = refs[0][...].astype(jnp.float32)
    for ref in refs[1:count]:
        total = total + ref[...].astype(jnp.float32)
    store_blocks(refs[count:], total)


def combine_kernel(count, weight_ref, residual_ref, *refs):
    rows = load_blocks(refs[:count]).astype(jnp.bfloat16)
    mixture = jnp.dot(weight_ref[...], rows, preferred_element_type=jnp.float32)
    refs[count][...] = (residual_ref[...].astype(jnp.float32) + mixture).astype(
        jnp.bfloat16
    )


def call(kernel, name, outs, *args, scratch=(), in_hbm=False, after=()):
    count = len(after)
    if in_hbm:
        args = [pltpu.with_memory_space_constraint(a, pltpu.HBM) for a in args]
    space = pltpu.HBM if in_hbm else pltpu.VMEM
    size = sum(a.size * a.dtype.itemsize for a in (*args, *outs))
    return pl.pallas_call(
        lambda *refs: kernel(*refs[count:]),
        in_specs=[pl.BlockSpec(memory_space=pl.ANY)] * count
        + [pl.BlockSpec(memory_space=space)] * len(args),
        out_specs=[pl.BlockSpec(memory_space=pltpu.VMEM)] * len(outs),
        out_shape=outs,
        scratch_shapes=scratch,
        compiler_params=pltpu.CompilerParams(vmem_limit_bytes=size + (8 << 20)),
        name=name,
    )(*after, *args)


def on_device(
    tokens,
    norm_gain,
    routing_projection_matrix,
    experts,
    replica_key,
    slot_expert,
    capacity,
    slot_gate_up_weight,
    down_weight,
):
    peers = lax.axis_size("expert")
    groups = lax.axis_size("dp")
    rows, width = tokens.shape
    slots = slot_expert.shape[0]
    per_device = slots // peers
    units = slot_gate_up_weight.shape[3]
    quarter = width // groups
    near = range(min(NEAR, peers))
    far = range(len(near), peers)

    def blocks(count, *shape, dtype=jnp.bfloat16):
        return [jax.ShapeDtypeStruct(shape, dtype)] * count

    def to_group(value, step):
        return lax.ppermute(value, "dp", [(i, i ^ step) for i in range(groups)])

    def to_peer(value, step):
        return lax.ppermute(value, "expert", [(i, i ^ step) for i in range(peers)])

    gain = norm_gain.reshape(width // 128, 128)
    slot_row = slot_expert.reshape(1, slots)
    cap_row = capacity.reshape(1, slots)
    down = down_weight.reshape(per_device * units, width)

    tokens_here, gain_here, local, *far_out = call(
        functools.partial(dispatch_kernel, per_device, far),
        "dispatch",
        blocks(1, rows, width)
        + blocks(1, *gain.shape)
        + blocks(1, slots, rows, dtype=jnp.float32)
        + blocks(len(far), CAP_DEV, quarter),
        tokens,
        experts.T,
        replica_key.T,
        slot_row,
        cap_row,
        gain,
        scratch=[
            pltpu.VMEM((experts.shape[1], rows), jnp.int32),
            pltpu.VMEM((experts.shape[1], rows), jnp.int32),
            pltpu.VMEM((1, slots), jnp.int32),
            pltpu.VMEM((1, slots), jnp.int32),
            pltpu.SemaphoreType.DMA((6,)),
        ],
        in_hbm=True,
    )
    far_in = [to_peer(value, step) for value, step in zip(far_out[::-1], far[::-1])]

    halves = units // 128
    split_in = slot_gate_up_weight.reshape(per_device, width, 2, halves, 128)
    split_in = split_in.transpose(0, 1, 3, 2, 4)
    split_in = split_in.reshape(per_device, width * halves * 2, 128)
    (gate_up,) = call(
        functools.partial(split_kernel, halves, groups),
        "split_gate_up",
        blocks(1, groups, quarter, per_device * 2 * units),
        split_in,
        scratch=[
            pltpu.VMEM(
                (groups, per_device, quarter * halves * 2, 128), jnp.bfloat16
            ),
            pltpu.SemaphoreType.DMA((groups,)),
        ],
        in_hbm=True,
        after=(local,),
    )

    (far_rows,) = call(
        join_kernel,
        "join_far",
        blocks(1, len(far) * CAP_DEV, quarter),
        *far_in[::-1],
        after=(gate_up,),
    )
    near_out = call(
        functools.partial(near_kernel, per_device, groups, near),
        "dispatch_near",
        blocks(len(near), CAP_DEV, width),
        tokens_here,
        gain_here,
        local,
        after=(far_rows,),
    )
    near_in = [near_out[0]] + [to_peer(near_out[step], step) for step in near[1:]]

    far_parts = [far_rows] + [to_group(far_rows, step) for step in range(1, groups)]
    far_sum = None
    for step in range(groups - 1):
        term = jnp.dot(
            far_parts[step], gate_up[step], preferred_element_type=jnp.float32
        )
        far_sum = term if far_sum is None else far_sum + term
    far_partials = call(
        functools.partial(far_kernel, per_device),
        "expert_far",
        blocks(groups, len(far) * CAP_DEV, quarter),
        far_sum,
        far_parts[-1],
        gate_up,
        cap_row,
        down,
    )
    near_partials = call(
        functools.partial(near_expert_kernel, per_device, len(near)),
        "expert_near",
        blocks(groups, len(near) * CAP_DEV, quarter),
        *near_in,
        gate_up,
        cap_row,
        down,
        after=(far_partials[1],),
    )

    def reduce_groups(partials, name, count, after=()):
        received = [to_group(partials[step], step) for step in range(1, groups)]
        return call(
            functools.partial(sum_kernel, groups),
            name,
            blocks(count, CAP_DEV, quarter),
            partials[0],
            *received,
            after=after,
        )

    far_back = reduce_groups(far_partials, "sum_far", len(far))
    near_back = reduce_groups(near_partials, "sum_near", len(near), far_back[:1])
    far_back = [to_peer(value, step) for value, step in zip(far_back[::-1], far[::-1])]
    near_back = [near_back[0]] + [to_peer(near_back[step], step) for step in near[1:]]

    weights, residual = call(
        functools.partial(weight_kernel, per_device, range(peers)),
        "combine_weights",
        blocks(1, rows, peers * CAP_DEV) + blocks(1, rows, quarter),
        tokens_here,
        gain_here,
        routing_projection_matrix.T,
        slot_row,
        local,
        scratch=[pltpu.VMEM((slots, rows), jnp.float32)],
    )
    (mixed,) = call(
        functools.partial(combine_kernel, peers),
        "combine",
        blocks(1, rows, quarter),
        weights,
        residual,
        *near_back,
        *far_back[::-1],
    )
    return mixed


def solution(mesh):
    in_specs = (
        P("expert", None),
        P(),
        P(),
        P("expert", None),
        P("expert", None),
        P(),
        P(),
        P("expert", None, None, "dp"),
        P("expert", "dp", None),
    )
    return jax.shard_map(
        on_device,
        mesh=mesh,
        in_specs=in_specs,
        out_specs=P("expert", "dp"),
        check_vma=False,
    )
```

```python
import functools

import jax
import jax.numpy as jnp
from jax import lax
from jax.experimental import pallas as pl
from jax.experimental.pallas import tpu as pltpu
from jax.sharding import PartitionSpec as P

CAP_DEV = 24
NEAR = 4


def to_column(row):
    n = row.shape[1]
    eye = lax.broadcasted_iota(jnp.int32, (n, n), 0) == lax.broadcasted_iota(
        jnp.int32, (n, n), 1
    )
    wide = jnp.where(eye, jnp.broadcast_to(row, (n, n)).astype(jnp.float32), 0.0)
    return jnp.sum(wide, axis=1, keepdims=True)


def place_rows(experts_t, keys_t, slot_row, cap_row, per_device):
    slots = slot_row.shape[1]
    picks, rows = experts_t.shape
    slot_f = slot_row.astype(jnp.float32)
    cap_f = cap_row.astype(jnp.float32)
    slot_col = to_column(slot_row)
    cap_col = to_column(cap_row)
    here = lax.broadcasted_iota(jnp.int32, (slots, slots), 0)
    other = lax.broadcasted_iota(jnp.int32, (slots, slots), 1)
    same = jnp.where(slot_f == slot_col, 1.0, 0.0)
    copies = jnp.sum(same, axis=1, keepdims=True)
    earlier = other < here
    place = jnp.sum(jnp.where(earlier, same, 0.0), axis=1, keepdims=True)
    together = (here // per_device) == (other // per_device)
    offset = jnp.sum(jnp.where(earlier & together, cap_f, 0.0), axis=1, keepdims=True)
    hit = jnp.zeros((slots, rows), jnp.float32)
    key = jnp.zeros((slots, rows), jnp.float32)
    experts_f = experts_t.astype(jnp.float32)
    keys_f = keys_t.astype(jnp.float32)
    for k in range(picks):
        match = experts_f[k : k + 1, :] == slot_col
        hit = jnp.where(match, 1.0, hit)
        key = jnp.where(match, keys_f[k : k + 1, :], key)
    rest = key - jnp.floor(key * (1.0 / copies)) * copies
    rest = jnp.where(rest < 0.0, rest + copies, rest)
    rest = jnp.where(rest >= copies, rest - copies, rest)
    chosen = (hit > 0.0) & (rest == place)
    before = lax.broadcasted_iota(jnp.int32, (rows, rows), 0) < lax.broadcasted_iota(
        jnp.int32, (rows, rows), 1
    )
    position = jnp.dot(
        jnp.where(chosen, 1.0, 0.0).astype(jnp.bfloat16),
        jnp.where(before, 1.0, 0.0).astype(jnp.bfloat16),
        preferred_element_type=jnp.float32,
    )
    return jnp.where(chosen & (position < cap_col), position + offset, -1.0)


def row_scale(hidden):
    return lax.rsqrt(jnp.mean(hidden * hidden, axis=-1, keepdims=True) + 1e-06)


def apply_gain(scaled, gain, first):
    number = lax.broadcasted_iota(jnp.int32, gain.shape, 0)
    parts = []
    for index in range(scaled.shape[1] // 128):
        row = jnp.sum(
            jnp.where(number == first + index, gain, 0.0), axis=0, keepdims=True
        )
        parts.append(
            (scaled[:, index * 128 : (index + 1) * 128] * row).astype(jnp.bfloat16)
        )
    return jnp.concatenate(parts, axis=1)


def pick_rows(local_ref, value_ref, steps, per_device):
    rows = local_ref.shape[1]
    me = lax.axis_index("expert")
    number = lax.broadcasted_iota(jnp.int32, (CAP_DEV, rows), 0).astype(jnp.float32)
    blocks = []
    for step in steps:
        block = jnp.zeros((CAP_DEV, rows), jnp.float32)
        for index in range(per_device):
            slot = (me ^ step) * per_device + index
            value = 1.0 if value_ref is None else value_ref[pl.ds(slot, 1), :]
            block = jnp.where(local_ref[pl.ds(slot, 1), :] == number, value, block)
        blocks.append(block)
    return jnp.concatenate(blocks, axis=0)


def store_blocks(refs, value):
    top = 0
    for ref in refs:
        ref[...] = value[top : top + ref.shape[0], :].astype(ref.dtype)
        top += ref.shape[0]


def load_blocks(refs, half=None):
    values = [ref[...].astype(jnp.float32) for ref in refs]
    if half is not None:
        values = [v[half * CAP_DEV : (half + 1) * CAP_DEV, :] for v in values]
    return jnp.concatenate(values, axis=0)


def dispatch_kernel(per_device, steps, *refs):
    tokens_hbm, *small_hbm = refs[:6]
    tokens_ref, gain_ref, local_ref, *out_refs = refs[6:11]
    experts_ref, keys_ref, slot_ref, cap_ref, arrived = refs[11:]
    small_refs = (experts_ref, keys_ref, slot_ref, cap_ref, gain_ref)
    copies = [
        pltpu.make_async_copy(source, target, arrived.at[index])
        for index, (source, target) in enumerate(
            zip((*small_hbm, tokens_hbm), (*small_refs, tokens_ref))
        )
    ]
    for copy in copies:
        copy.start()
    for copy in copies[:-1]:
        copy.wait()
    local_ref[...] = place_rows(
        experts_ref[...], keys_ref[...], slot_ref[...], cap_ref[...], per_device
    )
    pick = pick_rows(local_ref, None, steps, per_device).astype(jnp.bfloat16)
    gain = gain_ref[...].astype(jnp.float32)
    width = out_refs[0].shape[1]
    group = lax.axis_index("dp")
    copies[-1].wait()
    scale = row_scale(tokens_ref[...].astype(jnp.float32))
    start = pl.multiple_of(group * width, width)
    part = tokens_ref[:, pl.ds(start, width)].astype(jnp.float32)
    normed = apply_gain(part * scale, gain, group * (width // 128))
    store_blocks(out_refs, jnp.dot(pick, normed, preferred_element_type=jnp.float32))


def near_kernel(per_device, groups, steps, tokens_ref, gain_ref, local_ref, *out_refs):
    gain = gain_ref[...].astype(jnp.float32)
    width = tokens_ref.shape[1] // groups
    group = lax.axis_index("dp")
    scale = row_scale(tokens_ref[...].astype(jnp.float32))
    pick = pick_rows(local_ref, None, sum(steps, ()), per_device).astype(jnp.bfloat16)
    for step in range(groups):
        start = pl.multiple_of((group ^ step) * width, width)
        part = tokens_ref[:, pl.ds(start, width)].astype(jnp.float32)
        normed = apply_gain(part * scale, gain, (group ^ step) * (width // 128))
        value = jnp.dot(pick, normed, preferred_element_type=jnp.float32)
        top = 0
        for ref in out_refs:
            ref[:, step * width : (step + 1) * width] = value[
                top : top + ref.shape[0], :
            ].astype(ref.dtype)
            top += ref.shape[0]


def weight_kernel(
    per_device,
    steps,
    tokens_ref,
    gain_ref,
    route_ref,
    slot_ref,
    local_ref,
    out_ref,
    residual_ref,
    score_ref,
):
    quarter = residual_ref.shape[1]
    start = pl.multiple_of(lax.axis_index("dp") * quarter, quarter)
    residual_ref[...] = tokens_ref[:, pl.ds(start, quarter)]
    slots = slot_ref.shape[1]
    rows = tokens_ref.shape[0]
    hidden = tokens_ref[...].astype(jnp.float32)
    gain = gain_ref[...].astype(jnp.float32)
    normed = apply_gain(hidden * row_scale(hidden), gain, 0)
    logits = lax.dot_general(
        route_ref[...],
        normed,
        (((1,), (1,)), ((), ())),
        preferred_element_type=jnp.float32,
    )
    score = 1.0 / (1.0 + jnp.exp(-logits))
    slot_col = to_column(slot_ref[...])
    by_slot = jnp.zeros((slots, rows), jnp.float32)
    for expert in range(route_ref.shape[0]):
        by_slot = jnp.where(slot_col == expert, score[expert : expert + 1, :], by_slot)
    score_ref[...] = by_slot
    weights = pick_rows(local_ref, score_ref, steps, per_device)
    out_ref[...] = weights.T.astype(jnp.bfloat16)


def split_kernel(halves, groups, steps, in_hbm, out_ref, in_ref, arrived):
    tile = 256
    kinds = 2 * halves
    per_tile = tile // kinds
    slots, length, _ = in_hbm.shape
    part = length // groups
    group = lax.axis_index("dp")
    copies = []
    for place, step in enumerate(steps):
        base = pl.multiple_of((group ^ step) * part, part)
        copies.append(
            pltpu.make_async_copy(
                in_hbm.at[:, pl.ds(base, part), :], in_ref.at[place], arrived.at[place]
            )
        )
        copies[-1].start()
    to_row = lax.broadcasted_iota(jnp.int32, (tile, tile), 0)
    from_row = lax.broadcasted_iota(jnp.int32, (tile, tile), 1)
    column = to_row // per_tile
    source = (to_row % per_tile) * kinds + (column % halves) * 2 + column // halves
    order = jnp.where(source == from_row, 1.0, 0.0).astype(jnp.bfloat16)
    for place in range(len(steps)):
        copies[place].wait()
        for slot in range(slots):
            for index in range(0, part // tile, 2):
                low = index * tile
                pair = [
                    in_ref[place, slot, low + side * tile : low + (side + 1) * tile, :]
                    for side in range(2)
                ]
                moved = jnp.dot(
                    order,
                    jnp.concatenate(pair, axis=1),
                    preferred_element_type=jnp.float32,
                ).astype(jnp.bfloat16)
                for side in range(2):
                    top = (index + side) * per_tile
                    for kind in range(kinds):
                        left = (slot * kinds + kind) * 128
                        out_ref[place, top : top + per_tile, left : left + 128] = moved[
                            kind * per_tile : (kind + 1) * per_tile,
                            side * 128 : (side + 1) * 128,
                        ]


def slot_mask(cap_ref, per_device, units):
    first = lax.axis_index("expert") * per_device
    caps = cap_ref[...].astype(jnp.float32)
    lane = lax.broadcasted_iota(jnp.int32, caps.shape, 1)
    number = lax.broadcasted_iota(jnp.int32, (CAP_DEV, units), 0).astype(jnp.float32)
    end = jnp.zeros((1, 1), jnp.float32)
    parts = []
    for slot in range(per_device):
        begin = end
        end = begin + jnp.sum(
            jnp.where(lane == first + slot, caps, 0.0), axis=1, keepdims=True
        )
        parts.append(jnp.where((number >= begin) & (number < end), 1.0, 0.0))
    return jnp.concatenate(parts, axis=1)


def finish_rows(gate_up, cap_ref, down_ref, out_refs, per_device):
    units = down_ref.shape[0] // per_device
    mask = slot_mask(cap_ref, per_device, units)
    mask = jnp.concatenate([mask] * (gate_up.shape[0] // CAP_DEV), axis=0)
    pieces = []
    for slot in range(per_device):
        left = 2 * slot * units
        gate = gate_up[:, left : left + units]
        up = gate_up[:, left + units : left + 2 * units]
        pieces.append(gate / (1.0 + jnp.exp(-gate)) * up)
    activated = jnp.where(mask > 0.0, jnp.concatenate(pieces, axis=1), 0.0)
    activated = activated.astype(jnp.bfloat16)
    group = lax.axis_index("dp")
    for step, ref in enumerate(out_refs):
        width = ref.shape[1]
        start = pl.multiple_of((group ^ step) * width, width)
        ref[...] = jnp.dot(
            activated,
            down_ref[:, pl.ds(start, width)],
            preferred_element_type=jnp.float32,
        ).astype(ref.dtype)


def product_kernel(index, rows_ref, weight_ref, *refs):
    value = jnp.dot(
        rows_ref[...], weight_ref[index], preferred_element_type=jnp.float32
    )
    for ref in refs[:-1]:
        value = value + ref[...]
    refs[-1][...] = value


def far_kernel(per_device, sum_ref, last_ref, weight_ref, cap_ref, down_ref, *out_refs):
    gate_up = sum_ref[...] + jnp.dot(
        last_ref[...],
        weight_ref[weight_ref.shape[0] - 1],
        preferred_element_type=jnp.float32,
    )
    finish_rows(gate_up, cap_ref, down_ref, out_refs, per_device)


def near_expert_kernel(
    per_device, own_ref, core_ref, chip_ref, first_ref, second_ref, cap_ref, down_ref, *out_refs
):
    rows = jnp.concatenate(
        [load_blocks([own_ref]), load_blocks([core_ref], 0), load_blocks([chip_ref])],
        axis=0,
    ).astype(jnp.bfloat16)
    width = first_ref.shape[1]
    gate_up = None
    for index in range(first_ref.shape[0] + second_ref.shape[0]):
        weight = (
            first_ref[index]
            if index < first_ref.shape[0]
            else second_ref[index - first_ref.shape[0]]
        )
        term = jnp.dot(
            rows[:, index * width : (index + 1) * width],
            weight,
            preferred_element_type=jnp.float32,
        )
        gate_up = term if gate_up is None else gate_up + term
    finish_rows(gate_up, cap_ref, down_ref, out_refs, per_device)


def join_kernel(*refs):
    refs[-1][...] = load_blocks(refs[:-1]).astype(refs[-1].dtype)


def pair_kernel(same_ref, core_ref, *out_refs):
    same, core = load_blocks([same_ref]), load_blocks([core_ref])
    for index, ref in enumerate(out_refs):
        rows = slice(index * CAP_DEV, (index + 1) * CAP_DEV)
        ref[...] = jnp.concatenate([same[rows], core[rows]], axis=0).astype(ref.dtype)


def forward_kernel(same_ref, core_ref, out_ref):
    out_ref[...] = jnp.concatenate(
        [load_blocks([same_ref]), load_blocks([core_ref], 1)], axis=0
    ).astype(out_ref.dtype)


def flip_kernel(*refs):
    refs[-1][...] = load_blocks(refs[:-1], 1).astype(refs[-1].dtype)


def sum_kernel(count, *refs):
    total = refs[0][...].astype(jnp.float32)
    for ref in refs[1:count]:
        total = total + ref[...].astype(jnp.float32)
    store_blocks(refs[count:], total)


def combine_kernel(weight_ref, residual_ref, *refs):
    rows = load_blocks(refs[:-1], 0).astype(jnp.bfloat16)
    mixture = jnp.dot(
        weight_ref[:, : rows.shape[0]], rows, preferred_element_type=jnp.float32
    )
    refs[-1][...] = residual_ref[...].astype(jnp.float32) + mixture


def finish_kernel(weight_ref, sum_ref, core_ref, out_ref):
    mixture = jnp.dot(
        weight_ref[:, core_ref.shape[0] :],
        core_ref[...],
        preferred_element_type=jnp.float32,
    )
    out_ref[...] = (sum_ref[...] + mixture).astype(jnp.bfloat16)


def call(kernel, name, outs, *args, scratch=(), in_hbm=False, after=()):
    count = len(after)
    if in_hbm:
        args = [pltpu.with_memory_space_constraint(a, pltpu.HBM) for a in args]
    space = pltpu.HBM if in_hbm else pltpu.VMEM
    size = sum(a.size * a.dtype.itemsize for a in (*args, *outs))
    return pl.pallas_call(
        lambda *refs: kernel(*refs[count:]),
        in_specs=[pl.BlockSpec(memory_space=pl.ANY)] * count
        + [pl.BlockSpec(memory_space=space)] * len(args),
        out_specs=[pl.BlockSpec(memory_space=pltpu.VMEM)] * len(outs),
        out_shape=outs,
        scratch_shapes=scratch,
        compiler_params=pltpu.CompilerParams(vmem_limit_bytes=size + (8 << 20)),
        cost_estimate=pl.CostEstimate(flops=1, bytes_accessed=1, transcendentals=0),
        name=name,
    )(*after, *args)


def on_device(
    tokens,
    norm_gain,
    routing_projection_matrix,
    experts,
    replica_key,
    slot_expert,
    capacity,
    slot_gate_up_weight,
    down_weight,
):
    peers = lax.axis_size("expert")
    groups = lax.axis_size("dp")
    rows, width = tokens.shape
    slots = slot_expert.shape[0]
    per_device = slots // peers
    units = slot_gate_up_weight.shape[3]
    quarter = width // groups
    chips = peers // 2

    def blocks(count, *shape, dtype=jnp.bfloat16):
        return [jax.ShapeDtypeStruct(shape, dtype)] * count

    def to_group(value, step):
        return lax.ppermute(value, "dp", [(i, i ^ step) for i in range(groups)])

    def to_peer(value, step):
        return lax.ppermute(value, "expert", [(i, i ^ step) for i in range(peers)])

    gain = norm_gain.reshape(width // 128, 128)
    slot_row = slot_expert.reshape(1, slots)
    cap_row = capacity.reshape(1, slots)
    down = down_weight.reshape(per_device * units, width)

    tokens_here, gain_here, local, far_same, far_flip = call(
        functools.partial(
            dispatch_kernel, per_device, [*range(4, peers, 2), *range(5, peers, 2)]
        ),
        "dispatch",
        blocks(1, rows, width)
        + blocks(1, *gain.shape)
        + blocks(1, slots, rows, dtype=jnp.float32)
        + blocks(2, (chips - 2) * CAP_DEV, quarter),
        tokens,
        experts.T,
        replica_key.T,
        slot_row,
        cap_row,
        gain,
        scratch=[
            pltpu.VMEM((experts.shape[1], rows), jnp.int32),
            pltpu.VMEM((experts.shape[1], rows), jnp.int32),
            pltpu.VMEM((1, slots), jnp.int32),
            pltpu.VMEM((1, slots), jnp.int32),
            pltpu.SemaphoreType.DMA((6,)),
        ],
        in_hbm=True,
    )
    core_far = to_peer(far_flip, 1)
    own_rows, same_rows, flip_rows = call(
        functools.partial(near_kernel, per_device, groups, ((0,), (2,), (1, 3))),
        "dispatch_near",
        blocks(2, CAP_DEV, width) + blocks(1, 2 * CAP_DEV, width),
        tokens_here,
        gain_here,
        local,
    )
    core_rows = to_peer(flip_rows, 1)
    far_out = call(
        pair_kernel,
        "pair_far",
        blocks(chips - 2, 2 * CAP_DEV, quarter),
        far_same,
        core_far,
    )
    far_in = [
        to_peer(value, 2 * chip) for chip, value in reversed([*enumerate(far_out, 2)])
    ]
    (chip_rows,) = call(
        forward_kernel,
        "forward_near",
        blocks(1, 2 * CAP_DEV, width),
        same_rows,
        core_rows,
        after=(far_out[0],),
    )
    near_ready = chip_rows
    chip_rows = to_peer(chip_rows, 2)

    halves = units // 128
    split_in = slot_gate_up_weight.reshape(per_device, width, 2, halves, 128)
    split_in = split_in.transpose(0, 1, 3, 2, 4)
    split_in = split_in.reshape(per_device, width * halves * 2, 128)
    half = groups // 2

    def split(steps, after):
        return call(
            functools.partial(split_kernel, halves, groups, steps),
            "split_gate_up",
            blocks(1, len(steps), quarter, per_device * 2 * units),
            split_in,
            scratch=[
                pltpu.VMEM(
                    (len(steps), per_device, quarter * halves * 2, 128), jnp.bfloat16
                ),
                pltpu.SemaphoreType.DMA((len(steps),)),
            ],
            in_hbm=True,
            after=after,
        )[0]

    first_weights = split(range(half), (near_ready,))
    (far_rows,) = call(
        join_kernel,
        "join_far",
        blocks(1, (peers - NEAR) * CAP_DEV, quarter),
        *far_in[::-1],
        after=(first_weights,),
    )
    second_weights = split(range(half, groups), (far_rows,))

    far_parts = [far_rows] + [to_group(far_rows, step) for step in range(1, groups)]
    far_sum = ()
    for step in range(groups - 1):
        weights, index = (
            (first_weights, step) if step < half else (second_weights, step - half)
        )
        far_sum = call(
            functools.partial(product_kernel, index),
            "product_far",
            blocks(
                1, far_rows.shape[0], per_device * 2 * units, dtype=jnp.float32
            ),
            far_parts[step],
            weights,
            *far_sum,
        )
    far_partials = call(
        functools.partial(far_kernel, per_device),
        "expert_far",
        blocks(groups, (peers - NEAR) * CAP_DEV, quarter),
        *far_sum,
        far_parts[-1],
        second_weights,
        cap_row,
        down,
    )
    near_partials = call(
        functools.partial(near_expert_kernel, per_device),
        "expert_near",
        blocks(groups, NEAR * CAP_DEV, quarter),
        own_rows,
        core_rows,
        chip_rows,
        first_weights,
        second_weights,
        cap_row,
        down,
        after=(far_partials[1],),
    )

    def reduce_groups(partials, name, count, after=()):
        received = [to_group(partials[step], step) for step in range(1, groups)]
        return call(
            functools.partial(sum_kernel, groups),
            name,
            blocks(count, 2 * CAP_DEV, quarter),
            partials[0],
            *received,
            after=after,
        )

    far_back = reduce_groups(far_partials, "sum_far", chips - 2)
    near_back = reduce_groups(near_partials, "sum_near", 2, far_back[:1])
    far_back = [
        to_peer(value, 2 * chip) for chip, value in reversed([*enumerate(far_back, 2)])
    ]
    back = [near_back[0], to_peer(near_back[1], 2), *far_back[::-1]]
    (flip_back,) = call(
        flip_kernel, "flip_back", blocks(1, chips * CAP_DEV, quarter), *back
    )
    core_back = to_peer(flip_back, 1)

    order = [*range(0, peers, 2), *range(1, peers, 2)]
    weights, residual = call(
        functools.partial(weight_kernel, per_device, order),
        "combine_weights",
        blocks(1, rows, peers * CAP_DEV) + blocks(1, rows, quarter),
        tokens_here,
        gain_here,
        routing_projection_matrix.T,
        slot_row,
        local,
        scratch=[pltpu.VMEM((slots, rows), jnp.float32)],
    )
    (mixed_half,) = call(
        combine_kernel,
        "combine",
        blocks(1, rows, quarter, dtype=jnp.float32),
        weights,
        residual,
        *back,
    )
    (mixed,) = call(
        finish_kernel, "finish", blocks(1, rows, quarter), weights, mixed_half, core_back
    )
    return mixed


def solution(mesh):
    in_specs = (
        P("expert", None),
        P(),
        P(),
        P("expert", None),
        P("expert", None),
        P(),
        P(),
        P("expert", None, None, "dp"),
        P("expert", "dp", None),
    )
    return jax.shard_map(
        on_device,
        mesh=mesh,
        in_specs=in_specs,
        out_specs=P("expert", "dp"),
        check_vma=False,
    )
```

```python
import functools

import jax
import jax.numpy as jnp
from jax import lax
from jax.experimental import pallas as pl
from jax.experimental.pallas import tpu as pltpu
from jax.sharding import PartitionSpec as P

CAP_DEV = 24
NEAR = 4


def to_column(row):
    n = row.shape[1]
    eye = lax.broadcasted_iota(jnp.int32, (n, n), 0) == lax.broadcasted_iota(
        jnp.int32, (n, n), 1
    )
    wide = jnp.where(eye, jnp.broadcast_to(row, (n, n)).astype(jnp.float32), 0.0)
    return jnp.sum(wide, axis=1, keepdims=True)


def place_rows(experts_t, keys_t, slot_row, cap_row, per_device):
    slots = slot_row.shape[1]
    picks, rows = experts_t.shape
    slot_f = slot_row.astype(jnp.float32)
    cap_f = cap_row.astype(jnp.float32)
    slot_col = to_column(slot_row)
    cap_col = to_column(cap_row)
    here = lax.broadcasted_iota(jnp.int32, (slots, slots), 0)
    other = lax.broadcasted_iota(jnp.int32, (slots, slots), 1)
    same = jnp.where(slot_f == slot_col, 1.0, 0.0)
    copies = jnp.sum(same, axis=1, keepdims=True)
    earlier = other < here
    place = jnp.sum(jnp.where(earlier, same, 0.0), axis=1, keepdims=True)
    together = (here // per_device) == (other // per_device)
    offset = jnp.sum(jnp.where(earlier & together, cap_f, 0.0), axis=1, keepdims=True)
    hit = jnp.zeros((slots, rows), jnp.float32)
    key = jnp.zeros((slots, rows), jnp.float32)
    experts_f = experts_t.astype(jnp.float32)
    keys_f = keys_t.astype(jnp.float32)
    for k in range(picks):
        match = experts_f[k : k + 1, :] == slot_col
        hit = jnp.where(match, 1.0, hit)
        key = jnp.where(match, keys_f[k : k + 1, :], key)
    rest = key - jnp.floor(key * (1.0 / copies)) * copies
    rest = jnp.where(rest < 0.0, rest + copies, rest)
    rest = jnp.where(rest >= copies, rest - copies, rest)
    chosen = (hit > 0.0) & (rest == place)
    before = lax.broadcasted_iota(jnp.int32, (rows, rows), 0) < lax.broadcasted_iota(
        jnp.int32, (rows, rows), 1
    )
    position = jnp.dot(
        jnp.where(chosen, 1.0, 0.0).astype(jnp.bfloat16),
        jnp.where(before, 1.0, 0.0).astype(jnp.bfloat16),
        preferred_element_type=jnp.float32,
    )
    return jnp.where(chosen & (position < cap_col), position + offset, -1.0)


def row_scale(hidden):
    return lax.rsqrt(jnp.mean(hidden * hidden, axis=-1, keepdims=True) + 1e-06)


def apply_gain(scaled, gain, first):
    number = lax.broadcasted_iota(jnp.int32, gain.shape, 0)
    parts = []
    for index in range(scaled.shape[1] // 128):
        row = jnp.sum(
            jnp.where(number == first + index, gain, 0.0), axis=0, keepdims=True
        )
        parts.append(
            (scaled[:, index * 128 : (index + 1) * 128] * row).astype(jnp.bfloat16)
        )
    return jnp.concatenate(parts, axis=1)


def pick_rows(local_ref, value_ref, steps, per_device):
    rows = local_ref.shape[1]
    me = lax.axis_index("expert")
    number = lax.broadcasted_iota(jnp.int32, (CAP_DEV, rows), 0).astype(jnp.float32)
    blocks = []
    for step in steps:
        block = jnp.zeros((CAP_DEV, rows), jnp.float32)
        for index in range(per_device):
            slot = (me ^ step) * per_device + index
            value = 1.0 if value_ref is None else value_ref[pl.ds(slot, 1), :]
            block = jnp.where(local_ref[pl.ds(slot, 1), :] == number, value, block)
        blocks.append(block)
    return jnp.concatenate(blocks, axis=0)


def store_blocks(refs, value):
    top = 0
    for ref in refs:
        ref[...] = value[top : top + ref.shape[0], :].astype(ref.dtype)
        top += ref.shape[0]


def load_blocks(refs, half=None):
    values = [ref[...].astype(jnp.float32) for ref in refs]
    if half is not None:
        values = [v[half * CAP_DEV : (half + 1) * CAP_DEV, :] for v in values]
    return jnp.concatenate(values, axis=0)


def dispatch_kernel(per_device, steps, *refs):
    tokens_hbm, *small_hbm = refs[:6]
    tokens_ref, gain_ref, slot_ref, cap_ref, local_ref, *out_refs = refs[6:13]
    experts_ref, keys_ref, arrived = refs[13:]
    small_refs = (experts_ref, keys_ref, gain_ref, slot_ref, cap_ref)
    copies = [
        pltpu.make_async_copy(source, target, arrived.at[index])
        for index, (source, target) in enumerate(
            zip((*small_hbm, tokens_hbm), (*small_refs, tokens_ref))
        )
    ]
    for copy in copies:
        copy.start()
    for copy in copies[:-1]:
        copy.wait()
    local_ref[...] = place_rows(
        experts_ref[...], keys_ref[...], slot_ref[...], cap_ref[...], per_device
    )
    pick = pick_rows(local_ref, None, steps, per_device).astype(jnp.bfloat16)
    gain = gain_ref[...].astype(jnp.float32)
    width = out_refs[0].shape[1]
    group = lax.axis_index("dp")
    copies[-1].wait()
    scale = row_scale(tokens_ref[...].astype(jnp.float32))
    start = pl.multiple_of(group * width, width)
    part = tokens_ref[:, pl.ds(start, width)].astype(jnp.float32)
    normed = apply_gain(part * scale, gain, group * (width // 128))
    store_blocks(out_refs, jnp.dot(pick, normed, preferred_element_type=jnp.float32))


def near_kernel(per_device, meet, steps, tokens_ref, gain_ref, local_ref, *out_refs):
    gain = gain_ref[...].astype(jnp.float32)
    width = tokens_ref.shape[1] // len(meet)
    group = lax.axis_index("dp")
    scale = row_scale(tokens_ref[...].astype(jnp.float32))
    pick = pick_rows(local_ref, None, sum(steps, ()), per_device).astype(jnp.bfloat16)
    for place, step in enumerate(meet):
        start = pl.multiple_of((group ^ step) * width, width)
        part = tokens_ref[:, pl.ds(start, width)].astype(jnp.float32)
        normed = apply_gain(part * scale, gain, (group ^ step) * (width // 128))
        value = jnp.dot(pick, normed, preferred_element_type=jnp.float32)
        top = 0
        for ref in out_refs:
            ref[:, place * width : (place + 1) * width] = value[
                top : top + ref.shape[0], :
            ].astype(ref.dtype)
            top += ref.shape[0]


def weight_kernel(
    per_device,
    steps,
    tokens_ref,
    gain_ref,
    route_ref,
    slot_ref,
    local_ref,
    out_ref,
    residual_ref,
    score_ref,
):
    quarter = residual_ref.shape[1]
    start = pl.multiple_of(lax.axis_index("dp") * quarter, quarter)
    residual_ref[...] = tokens_ref[:, pl.ds(start, quarter)]
    slots = slot_ref.shape[1]
    rows = tokens_ref.shape[0]
    hidden = tokens_ref[...].astype(jnp.float32)
    gain = gain_ref[...].astype(jnp.float32)
    normed = apply_gain(hidden * row_scale(hidden), gain, 0)
    logits = lax.dot_general(
        route_ref[...],
        normed,
        (((1,), (1,)), ((), ())),
        preferred_element_type=jnp.float32,
    )
    score = 1.0 / (1.0 + jnp.exp(-logits))
    slot_col = to_column(slot_ref[...])
    by_slot = jnp.zeros((slots, rows), jnp.float32)
    for expert in range(route_ref.shape[0]):
        by_slot = jnp.where(slot_col == expert, score[expert : expert + 1, :], by_slot)
    score_ref[...] = by_slot
    weights = pick_rows(local_ref, score_ref, steps, per_device)
    out_ref[...] = weights.T.astype(jnp.bfloat16)


def split_rows(halves, in_ref, out_ref):
    tile = 256
    kinds = 2 * halves
    per_tile = tile // kinds
    slots, length, _ = in_ref.shape
    to_row = lax.broadcasted_iota(jnp.int32, (tile, tile), 0)
    from_row = lax.broadcasted_iota(jnp.int32, (tile, tile), 1)
    column = to_row // per_tile
    source = (to_row % per_tile) * kinds + (column % halves) * 2 + column // halves
    order = jnp.where(source == from_row, 1.0, 0.0).astype(jnp.bfloat16)
    for slot in range(slots):
        for index in range(0, length // tile, 2):
            low = index * tile
            pair = [
                in_ref[slot, low + side * tile : low + (side + 1) * tile, :]
                for side in range(2)
            ]
            moved = jnp.dot(
                order,
                jnp.concatenate(pair, axis=1),
                preferred_element_type=jnp.float32,
            ).astype(jnp.bfloat16)
            for side in range(2):
                top = (index + side) * per_tile
                for kind in range(kinds):
                    left = (slot * kinds + kind) * 128
                    out_ref[top : top + per_tile, left : left + 128] = moved[
                        kind * per_tile : (kind + 1) * per_tile,
                        side * 128 : (side + 1) * 128,
                    ]


def split_first_kernel(halves, meet, in_hbm, out_ref, rest_ref, in_ref, arrived):
    first, second = out_ref.shape[0], rest_ref.shape[0]
    part = in_hbm.shape[1] // (first + second)
    group = lax.axis_index("dp")
    copies = []
    for step in range(first + second):
        base = pl.multiple_of((group ^ meet[step]) * part, part)
        target = in_ref.at[step] if step < first else rest_ref.at[step - first]
        copies.append(
            pltpu.make_async_copy(
                in_hbm.at[:, pl.ds(base, part), :], target, arrived.at[step]
            )
        )
        copies[-1].start()
    for step in range(first):
        copies[step].wait()
        split_rows(halves, in_ref.at[step], out_ref.at[step])
    for copy in copies[first:]:
        copy.wait()


def split_second_kernel(halves, down_hbm, in_ref, out_ref, down_ref, arrived):
    copy = pltpu.make_async_copy(down_hbm, down_ref, arrived)
    copy.start()
    for index in range(in_ref.shape[0]):
        split_rows(halves, in_ref.at[index], out_ref.at[index])
    copy.wait()


def slot_mask(cap_ref, per_device, units):
    first = lax.axis_index("expert") * per_device
    caps = cap_ref[...].astype(jnp.float32)
    lane = lax.broadcasted_iota(jnp.int32, caps.shape, 1)
    number = lax.broadcasted_iota(jnp.int32, (CAP_DEV, units), 0).astype(jnp.float32)
    end = jnp.zeros((1, 1), jnp.float32)
    parts = []
    for slot in range(per_device):
        begin = end
        end = begin + jnp.sum(
            jnp.where(lane == first + slot, caps, 0.0), axis=1, keepdims=True
        )
        parts.append(jnp.where((number >= begin) & (number < end), 1.0, 0.0))
    return jnp.concatenate(parts, axis=1)


def finish_rows(gate_up, cap_ref, down_ref, out_refs, per_device):
    units = down_ref.shape[0] // per_device
    mask = slot_mask(cap_ref, per_device, units)
    mask = jnp.concatenate([mask] * (gate_up.shape[0] // CAP_DEV), axis=0)
    pieces = []
    for slot in range(per_device):
        left = 2 * slot * units
        gate = gate_up[:, left : left + units]
        up = gate_up[:, left + units : left + 2 * units]
        pieces.append(gate / (1.0 + jnp.exp(-gate)) * up)
    activated = jnp.where(mask > 0.0, jnp.concatenate(pieces, axis=1), 0.0)
    activated = activated.astype(jnp.bfloat16)
    group = lax.axis_index("dp")
    for step, ref in enumerate(out_refs):
        width = ref.shape[1]
        start = pl.multiple_of((group ^ step) * width, width)
        ref[...] = jnp.dot(
            activated,
            down_ref[:, pl.ds(start, width)],
            preferred_element_type=jnp.float32,
        ).astype(ref.dtype)


def product_kernel(index, rows_ref, weight_ref, *refs):
    value = jnp.dot(
        rows_ref[...], weight_ref[index], preferred_element_type=jnp.float32
    )
    for ref in refs[:-1]:
        value = value + ref[...]
    refs[-1][...] = value


def far_kernel(per_device, sum_ref, last_ref, weight_ref, cap_ref, down_ref, *out_refs):
    gate_up = sum_ref[...] + jnp.dot(
        last_ref[...],
        weight_ref[weight_ref.shape[0] - 1],
        preferred_element_type=jnp.float32,
    )
    finish_rows(gate_up, cap_ref, down_ref, out_refs, per_device)


def near_expert_kernel(
    per_device, own_ref, core_ref, chip_ref, first_ref, second_ref, cap_ref, down_ref, *out_refs
):
    rows = jnp.concatenate(
        [load_blocks([own_ref]), load_blocks([core_ref], 0), load_blocks([chip_ref])],
        axis=0,
    ).astype(jnp.bfloat16)
    width = first_ref.shape[1]
    gate_up = None
    for index in range(first_ref.shape[0] + second_ref.shape[0]):
        weight = (
            first_ref[index]
            if index < first_ref.shape[0]
            else second_ref[index - first_ref.shape[0]]
        )
        term = jnp.dot(
            rows[:, index * width : (index + 1) * width],
            weight,
            preferred_element_type=jnp.float32,
        )
        gate_up = term if gate_up is None else gate_up + term
    finish_rows(gate_up, cap_ref, down_ref, out_refs, per_device)


def join_kernel(*refs):
    refs[-1][...] = load_blocks(refs[:-1]).astype(refs[-1].dtype)


def pair_kernel(same_ref, core_ref, *out_refs):
    same, core = load_blocks([same_ref]), load_blocks([core_ref])
    for index, ref in enumerate(out_refs):
        rows = slice(index * CAP_DEV, (index + 1) * CAP_DEV)
        ref[...] = jnp.concatenate([same[rows], core[rows]], axis=0).astype(ref.dtype)


def forward_kernel(same_ref, core_ref, out_ref):
    out_ref[...] = jnp.concatenate(
        [load_blocks([same_ref]), load_blocks([core_ref], 1)], axis=0
    ).astype(out_ref.dtype)


def flip_kernel(*refs):
    refs[-1][...] = load_blocks(refs[:-1], 1).astype(refs[-1].dtype)


def sum_kernel(count, *refs):
    total = refs[0][...].astype(jnp.float32)
    for ref in refs[1:count]:
        total = total + ref[...].astype(jnp.float32)
    store_blocks(refs[count:], total)


def combine_kernel(weight_ref, residual_ref, *refs):
    rows = load_blocks(refs[:-1], 0).astype(jnp.bfloat16)
    mixture = jnp.dot(
        weight_ref[:, : rows.shape[0]], rows, preferred_element_type=jnp.float32
    )
    refs[-1][...] = residual_ref[...].astype(jnp.float32) + mixture


def finish_kernel(weight_ref, sum_ref, core_ref, out_ref):
    mixture = jnp.dot(
        weight_ref[:, core_ref.shape[0] :],
        core_ref[...],
        preferred_element_type=jnp.float32,
    )
    out_ref[...] = (sum_ref[...] + mixture).astype(jnp.bfloat16)


def call(kernel, name, outs, *args, scratch=(), hbm=(), after=()):
    count = len(after)
    hbm = [pltpu.with_memory_space_constraint(a, pltpu.HBM) for a in hbm]
    size = sum(a.size * a.dtype.itemsize for a in (*args, *outs))
    return pl.pallas_call(
        lambda *refs: kernel(*refs[count:]),
        in_specs=[pl.BlockSpec(memory_space=pl.ANY)] * count
        + [pl.BlockSpec(memory_space=pltpu.HBM)] * len(hbm)
        + [pl.BlockSpec(memory_space=pltpu.VMEM)] * len(args),
        out_specs=[pl.BlockSpec(memory_space=pltpu.VMEM)] * len(outs),
        out_shape=outs,
        scratch_shapes=scratch,
        compiler_params=pltpu.CompilerParams(vmem_limit_bytes=size + (8 << 20)),
        cost_estimate=pl.CostEstimate(flops=1, bytes_accessed=1, transcendentals=0),
        name=name,
    )(*after, *hbm, *args)


def on_device(
    tokens,
    norm_gain,
    routing_projection_matrix,
    experts,
    replica_key,
    slot_expert,
    capacity,
    slot_gate_up_weight,
    down_weight,
):
    peers = lax.axis_size("expert")
    groups = lax.axis_size("dp")
    rows, width = tokens.shape
    slots = slot_expert.shape[0]
    per_device = slots // peers
    units = slot_gate_up_weight.shape[3]
    quarter = width // groups
    chips = peers // 2
    far = range(2, chips)[::-1]
    meet = [0, groups - 1, *range(1, groups - 1)]

    def blocks(count, *shape, dtype=jnp.bfloat16):
        return [jax.ShapeDtypeStruct(shape, dtype)] * count

    def to_group(value, step):
        return lax.ppermute(value, "dp", [(i, i ^ step) for i in range(groups)])

    def to_peer(value, step):
        return lax.ppermute(value, "expert", [(i, i ^ step) for i in range(peers)])

    gain = norm_gain.reshape(width // 128, 128)
    slot_row = slot_expert.reshape(1, slots)
    cap_row = capacity.reshape(1, slots)
    down = down_weight.reshape(per_device * units, width)

    (
        tokens_here, gain_here, slot_here, cap_here, local, far_same, far_flip
    ) = call(
        functools.partial(
            dispatch_kernel, per_device, [2 * c for c in far] + [2 * c + 1 for c in far]
        ),
        "dispatch",
        blocks(1, rows, width)
        + blocks(1, *gain.shape)
        + blocks(2, 1, slots, dtype=jnp.int32)
        + blocks(1, slots, rows, dtype=jnp.float32)
        + blocks(2, (chips - 2) * CAP_DEV, quarter),
        hbm=[tokens, experts.T, replica_key.T, gain, slot_row, cap_row],
        scratch=[
            pltpu.VMEM((experts.shape[1], rows), jnp.int32),
            pltpu.VMEM((experts.shape[1], rows), jnp.int32),
            pltpu.SemaphoreType.DMA((6,)),
        ],
    )
    core_far = to_peer(far_flip, 1)
    own_rows, same_rows, flip_rows = call(
        functools.partial(near_kernel, per_device, meet, ((0,), (2,), (1, 3))),
        "dispatch_near",
        blocks(2, CAP_DEV, width) + blocks(1, 2 * CAP_DEV, width),
        tokens_here,
        gain_here,
        local,
    )
    core_rows = to_peer(flip_rows, 1)
    far_out = call(
        pair_kernel,
        "pair_far",
        blocks(chips - 2, 2 * CAP_DEV, quarter),
        far_same,
        core_far,
    )
    far_in = [to_peer(value, 2 * chip) for chip, value in zip(far, far_out)]
    (chip_rows,) = call(
        forward_kernel,
        "forward_near",
        blocks(1, 2 * CAP_DEV, width),
        same_rows,
        core_rows,
        after=(far_out[0],),
    )
    near_ready = chip_rows
    chip_rows = to_peer(chip_rows, 2)

    halves = units // 128
    split_in = slot_gate_up_weight.reshape(per_device, width, 2, halves, 128)
    split_in = split_in.transpose(0, 1, 3, 2, 4)
    split_in = split_in.reshape(per_device, width * halves * 2, 128)
    half = groups // 2

    part = (per_device, quarter * halves * 2, 128)
    out = (quarter, per_device * 2 * units)
    first_weights, rest = call(
        functools.partial(split_first_kernel, halves, meet),
        "split_first",
        blocks(1, half, *out) + blocks(1, groups - half, *part),
        hbm=[split_in],
        scratch=[
            pltpu.VMEM((half, *part), jnp.bfloat16),
            pltpu.SemaphoreType.DMA((groups,)),
        ],
        after=(near_ready,),
    )
    (far_rows,) = call(
        join_kernel,
        "join_far",
        blocks(1, (peers - NEAR) * CAP_DEV, quarter),
        *far_in,
        after=(first_weights,),
    )
    second_weights, down_here = call(
        functools.partial(split_second_kernel, halves),
        "split_second",
        blocks(1, groups - half, *out) + blocks(1, *down.shape),
        rest,
        hbm=[down],
        scratch=[pltpu.SemaphoreType.DMA],
        after=(far_rows,),
    )

    far_parts = [far_rows] + [to_group(far_rows, step) for step in meet[1:]]
    far_sum = ()
    for step in range(groups - 1):
        weights, index = (
            (first_weights, step) if step < half else (second_weights, step - half)
        )
        far_sum = call(
            functools.partial(product_kernel, index),
            "product_far",
            blocks(
                1, far_rows.shape[0], per_device * 2 * units, dtype=jnp.float32
            ),
            far_parts[step],
            weights,
            *far_sum,
        )
    far_partials = call(
        functools.partial(far_kernel, per_device),
        "expert_far",
        blocks(groups, (peers - NEAR) * CAP_DEV, quarter),
        *far_sum,
        far_parts[-1],
        second_weights,
        cap_here,
        down_here,
    )
    near_partials = call(
        functools.partial(near_expert_kernel, per_device),
        "expert_near",
        blocks(groups, NEAR * CAP_DEV, quarter),
        own_rows,
        core_rows,
        chip_rows,
        first_weights,
        second_weights,
        cap_here,
        down_here,
        after=(far_partials[1],),
    )

    def reduce_groups(partials, name, count, after=()):
        received = [
            to_group(partials[step], step) for step in meet[1:]
        ]
        return call(
            functools.partial(sum_kernel, groups),
            name,
            blocks(count, 2 * CAP_DEV, quarter),
            partials[0],
            *received,
            after=after,
        )

    far_back = reduce_groups(far_partials, "sum_far", chips - 2)
    near_back = reduce_groups(near_partials, "sum_near", 2, far_back[:1])
    far_back = [to_peer(value, 2 * chip) for chip, value in zip(far, far_back)]
    back = [*far_back, near_back[0], to_peer(near_back[1], 2)]
    (flip_back,) = call(
        flip_kernel, "flip_back", blocks(1, chips * CAP_DEV, quarter), *back
    )
    core_back = to_peer(flip_back, 1)

    order = [2 * c for c in (*far, 0, 1)]
    order += [step + 1 for step in order]
    weights, residual = call(
        functools.partial(weight_kernel, per_device, order),
        "combine_weights",
        blocks(1, rows, peers * CAP_DEV) + blocks(1, rows, quarter),
        tokens_here,
        gain_here,
        routing_projection_matrix.T,
        slot_here,
        local,
        scratch=[pltpu.VMEM((slots, rows), jnp.float32)],
    )
    (mixed_half,) = call(
        combine_kernel,
        "combine",
        blocks(1, rows, quarter, dtype=jnp.float32),
        weights,
        residual,
        *back,
    )
    (mixed,) = call(
        finish_kernel, "finish", blocks(1, rows, quarter), weights, mixed_half, core_back
    )
    return mixed


def solution(mesh):
    in_specs = (
        P("expert", None),
        P(),
        P(),
        P("expert", None),
        P("expert", None),
        P(),
        P(),
        P("expert", None, None, "dp"),
        P("expert", "dp", None),
    )
    return jax.shard_map(
        on_device,
        mesh=mesh,
        in_specs=in_specs,
        out_specs=P("expert", "dp"),
        check_vma=False,
    )
```

```python
import functools

import jax
import jax.numpy as jnp
from jax import lax
from jax.experimental import pallas as pl
from jax.experimental.pallas import tpu as pltpu
from jax.sharding import PartitionSpec as P

CAP_DEV = 24
NEAR = 4


def to_column(row):
    n = row.shape[1]
    eye = lax.broadcasted_iota(jnp.int32, (n, n), 0) == lax.broadcasted_iota(
        jnp.int32, (n, n), 1
    )
    wide = jnp.where(eye, jnp.broadcast_to(row, (n, n)).astype(jnp.float32), 0.0)
    return jnp.sum(wide, axis=1, keepdims=True)


def place_rows(experts_t, keys_t, slot_row, cap_row, per_device):
    slots = slot_row.shape[1]
    picks, rows = experts_t.shape
    slot_f = slot_row.astype(jnp.float32)
    cap_f = cap_row.astype(jnp.float32)
    slot_col = to_column(slot_row)
    cap_col = to_column(cap_row)
    here = lax.broadcasted_iota(jnp.int32, (slots, slots), 0)
    other = lax.broadcasted_iota(jnp.int32, (slots, slots), 1)
    same = jnp.where(slot_f == slot_col, 1.0, 0.0)
    copies = jnp.sum(same, axis=1, keepdims=True)
    earlier = other < here
    place = jnp.sum(jnp.where(earlier, same, 0.0), axis=1, keepdims=True)
    together = (here // per_device) == (other // per_device)
    offset = jnp.sum(jnp.where(earlier & together, cap_f, 0.0), axis=1, keepdims=True)
    hit = jnp.zeros((slots, rows), jnp.float32)
    key = jnp.zeros((slots, rows), jnp.float32)
    experts_f = experts_t.astype(jnp.float32)
    keys_f = keys_t.astype(jnp.float32)
    for k in range(picks):
        match = experts_f[k : k + 1, :] == slot_col
        hit = jnp.where(match, 1.0, hit)
        key = jnp.where(match, keys_f[k : k + 1, :], key)
    rest = key - jnp.floor(key * (1.0 / copies)) * copies
    rest = jnp.where(rest < 0.0, rest + copies, rest)
    rest = jnp.where(rest >= copies, rest - copies, rest)
    chosen = (hit > 0.0) & (rest == place)
    before = lax.broadcasted_iota(jnp.int32, (rows, rows), 0) < lax.broadcasted_iota(
        jnp.int32, (rows, rows), 1
    )
    position = jnp.dot(
        jnp.where(chosen, 1.0, 0.0).astype(jnp.bfloat16),
        jnp.where(before, 1.0, 0.0).astype(jnp.bfloat16),
        preferred_element_type=jnp.float32,
    )
    return jnp.where(chosen & (position < cap_col), position + offset, -1.0)


def row_scale(hidden):
    return lax.rsqrt(jnp.mean(hidden * hidden, axis=-1, keepdims=True) + 1e-06)


def apply_gain(scaled, gain, first):
    number = lax.broadcasted_iota(jnp.int32, gain.shape, 0)
    parts = []
    for index in range(scaled.shape[1] // 128):
        row = jnp.sum(
            jnp.where(number == first + index, gain, 0.0), axis=0, keepdims=True
        )
        parts.append(
            (scaled[:, index * 128 : (index + 1) * 128] * row).astype(jnp.bfloat16)
        )
    return jnp.concatenate(parts, axis=1)


def pick_rows(local_ref, value_ref, steps, per_device):
    rows = local_ref.shape[1]
    me = lax.axis_index("expert")
    number = lax.broadcasted_iota(jnp.int32, (CAP_DEV, rows), 0).astype(jnp.float32)
    blocks = []
    for step in steps:
        block = jnp.zeros((CAP_DEV, rows), jnp.float32)
        for index in range(per_device):
            slot = (me ^ step) * per_device + index
            value = 1.0 if value_ref is None else value_ref[pl.ds(slot, 1), :]
            block = jnp.where(local_ref[pl.ds(slot, 1), :] == number, value, block)
        blocks.append(block)
    return jnp.concatenate(blocks, axis=0)


def store_blocks(refs, value):
    top = 0
    for ref in refs:
        ref[...] = value[top : top + ref.shape[0], :].astype(ref.dtype)
        top += ref.shape[0]


def load_blocks(refs, half=None):
    values = [ref[...].astype(jnp.float32) for ref in refs]
    if half is not None:
        values = [v[half * CAP_DEV : (half + 1) * CAP_DEV, :] for v in values]
    return jnp.concatenate(values, axis=0)


def normed_part(tokens_ref, gain, start, width):
    scale = row_scale(tokens_ref[...].astype(jnp.float32))
    left = pl.multiple_of(start * width, width)
    part = tokens_ref[:, pl.ds(left, width)].astype(jnp.float32)
    return apply_gain(part * scale, gain, start * (width // 128))


def place_kernel(per_device, *refs):
    in_refs, out_refs, scratch = refs[:6], refs[6:11], refs[11:]
    tokens_ref, gain_ref, slot_ref, cap_ref, local_ref = out_refs
    experts_ref, keys_ref, arrived = scratch
    targets = (tokens_ref, experts_ref, keys_ref, gain_ref, slot_ref, cap_ref)
    copies = [
        pltpu.make_async_copy(source, target, arrived.at[index])
        for index, (source, target) in enumerate(zip(in_refs, targets))
    ]
    for copy in copies:
        copy.start()
    for copy in copies[1:]:
        copy.wait()
    local_ref[...] = place_rows(
        experts_ref[...], keys_ref[...], slot_ref[...], cap_ref[...], per_device
    )
    copies[0].wait()


def dispatch_kernel(
    per_device,
    steps,
    tokens_ref,
    core_ref,
    gain_ref,
    local_ref,
    experts_ref,
    keys_ref,
    slot_ref,
    cap_ref,
    core_local_ref,
    *out_refs,
):
    core_local_ref[...] = place_rows(
        experts_ref[...], keys_ref[...], slot_ref[...], cap_ref[...], per_device
    )
    gain = gain_ref[...].astype(jnp.float32)
    width = out_refs[0].shape[1]
    group = lax.axis_index("dp")
    rows = []
    for here, places in ((tokens_ref, local_ref), (core_ref, core_local_ref)):
        pick = pick_rows(places, None, steps, per_device).astype(jnp.bfloat16)
        normed = normed_part(here, gain, group, width)
        rows.append(jnp.dot(pick, normed, preferred_element_type=jnp.float32))
    for index, ref in enumerate(out_refs):
        block = slice(index * CAP_DEV, (index + 1) * CAP_DEV)
        ref[...] = jnp.concatenate([r[block] for r in rows], axis=0).astype(ref.dtype)


def near_kernel(
    per_device,
    meet,
    steps,
    tokens_ref,
    core_ref,
    gain_ref,
    local_ref,
    core_local_ref,
    *out_refs,
):
    gain = gain_ref[...].astype(jnp.float32)
    width = tokens_ref.shape[1] // len(meet)
    group = lax.axis_index("dp")
    sources = ((tokens_ref, local_ref), (core_ref, core_local_ref))
    for side, (here, places) in enumerate(sources):
        pick = pick_rows(places, None, steps, per_device).astype(jnp.bfloat16)
        scale = row_scale(here[...].astype(jnp.float32))
        for place, step in enumerate(meet):
            start = pl.multiple_of((group ^ step) * width, width)
            part = here[:, pl.ds(start, width)].astype(jnp.float32)
            normed = apply_gain(part * scale, gain, (group ^ step) * (width // 128))
            value = jnp.dot(pick, normed, preferred_element_type=jnp.float32)
            for index, ref in enumerate(out_refs):
                ref[
                    side * CAP_DEV : (side + 1) * CAP_DEV,
                    place * width : (place + 1) * width,
                ] = value[index * CAP_DEV : (index + 1) * CAP_DEV, :].astype(ref.dtype)


def weight_kernel(
    per_device,
    steps,
    tokens_ref,
    gain_ref,
    route_ref,
    slot_ref,
    local_ref,
    out_ref,
    residual_ref,
    score_ref,
):
    quarter = residual_ref.shape[1]
    start = pl.multiple_of(lax.axis_index("dp") * quarter, quarter)
    residual_ref[...] = tokens_ref[:, pl.ds(start, quarter)]
    slots = slot_ref.shape[1]
    rows = tokens_ref.shape[0]
    hidden = tokens_ref[...].astype(jnp.float32)
    gain = gain_ref[...].astype(jnp.float32)
    normed = apply_gain(hidden * row_scale(hidden), gain, 0)
    logits = lax.dot_general(
        route_ref[...],
        normed,
        (((1,), (1,)), ((), ())),
        preferred_element_type=jnp.float32,
    )
    score = 1.0 / (1.0 + jnp.exp(-logits))
    slot_col = to_column(slot_ref[...])
    by_slot = jnp.zeros((slots, rows), jnp.float32)
    for expert in range(route_ref.shape[0]):
        by_slot = jnp.where(slot_col == expert, score[expert : expert + 1, :], by_slot)
    score_ref[...] = by_slot
    weights = pick_rows(local_ref, score_ref, steps, per_device)
    out_ref[...] = weights.T.astype(jnp.bfloat16)


def split_rows(halves, in_ref, out_ref):
    tile = 256
    kinds = 2 * halves
    per_tile = tile // kinds
    slots, length, _ = in_ref.shape
    to_row = lax.broadcasted_iota(jnp.int32, (tile, tile), 0)
    from_row = lax.broadcasted_iota(jnp.int32, (tile, tile), 1)
    column = to_row // per_tile
    source = (to_row % per_tile) * kinds + (column % halves) * 2 + column // halves
    order = jnp.where(source == from_row, 1.0, 0.0).astype(jnp.bfloat16)
    for slot in range(slots):
        for index in range(0, length // tile, 2):
            low = index * tile
            pair = [
                in_ref[slot, low + side * tile : low + (side + 1) * tile, :]
                for side in range(2)
            ]
            moved = jnp.dot(
                order,
                jnp.concatenate(pair, axis=1),
                preferred_element_type=jnp.float32,
            ).astype(jnp.bfloat16)
            for side in range(2):
                top = (index + side) * per_tile
                for kind in range(kinds):
                    left = (slot * kinds + kind) * 128
                    out_ref[top : top + per_tile, left : left + 128] = moved[
                        kind * per_tile : (kind + 1) * per_tile,
                        side * 128 : (side + 1) * 128,
                    ]


def split_first_kernel(halves, meet, in_hbm, out_ref, rest_ref, in_ref, arrived):
    first, second = out_ref.shape[0], rest_ref.shape[0]
    part = in_hbm.shape[1] // (first + second)
    group = lax.axis_index("dp")
    copies = []
    for step in range(first + second):
        base = pl.multiple_of((group ^ meet[step]) * part, part)
        target = in_ref.at[step] if step < first else rest_ref.at[step - first]
        copies.append(
            pltpu.make_async_copy(
                in_hbm.at[:, pl.ds(base, part), :], target, arrived.at[step]
            )
        )
        copies[-1].start()
    for step in range(first):
        copies[step].wait()
        split_rows(halves, in_ref.at[step], out_ref.at[step])
    for copy in copies[first:]:
        copy.wait()


def split_second_kernel(halves, down_hbm, in_ref, out_ref, down_ref, arrived):
    copy = pltpu.make_async_copy(down_hbm, down_ref, arrived)
    copy.start()
    for index in range(in_ref.shape[0]):
        split_rows(halves, in_ref.at[index], out_ref.at[index])
    copy.wait()


def slot_mask(cap_ref, per_device, units):
    first = lax.axis_index("expert") * per_device
    caps = cap_ref[...].astype(jnp.float32)
    lane = lax.broadcasted_iota(jnp.int32, caps.shape, 1)
    number = lax.broadcasted_iota(jnp.int32, (CAP_DEV, units), 0).astype(jnp.float32)
    end = jnp.zeros((1, 1), jnp.float32)
    parts = []
    for slot in range(per_device):
        begin = end
        end = begin + jnp.sum(
            jnp.where(lane == first + slot, caps, 0.0), axis=1, keepdims=True
        )
        parts.append(jnp.where((number >= begin) & (number < end), 1.0, 0.0))
    return jnp.concatenate(parts, axis=1)


def finish_rows(gate_up, cap_ref, down_ref, out_refs, per_device):
    units = down_ref.shape[0] // per_device
    mask = slot_mask(cap_ref, per_device, units)
    mask = jnp.concatenate([mask] * (gate_up.shape[0] // CAP_DEV), axis=0)
    pieces = []
    for slot in range(per_device):
        left = 2 * slot * units
        gate = gate_up[:, left : left + units]
        up = gate_up[:, left + units : left + 2 * units]
        pieces.append(gate / (1.0 + jnp.exp(-gate)) * up)
    activated = jnp.where(mask > 0.0, jnp.concatenate(pieces, axis=1), 0.0)
    activated = activated.astype(jnp.bfloat16)
    group = lax.axis_index("dp")
    for step, ref in enumerate(out_refs):
        width = ref.shape[1]
        start = pl.multiple_of((group ^ step) * width, width)
        ref[...] = jnp.dot(
            activated,
            down_ref[:, pl.ds(start, width)],
            preferred_element_type=jnp.float32,
        ).astype(ref.dtype)


def product_kernel(index, rows_ref, weight_ref, *refs):
    value = jnp.dot(
        rows_ref[...], weight_ref[index], preferred_element_type=jnp.float32
    )
    for ref in refs[:-1]:
        value = value + ref[...]
    refs[-1][...] = value


def far_kernel(per_device, sum_ref, last_ref, weight_ref, cap_ref, down_ref, *out_refs):
    gate_up = sum_ref[...] + jnp.dot(
        last_ref[...],
        weight_ref[weight_ref.shape[0] - 1],
        preferred_element_type=jnp.float32,
    )
    finish_rows(gate_up, cap_ref, down_ref, out_refs, per_device)


def near_expert_kernel(
    per_device, here_ref, chip_ref, first_ref, second_ref, cap_ref, down_ref, *out_refs
):
    rows = jnp.concatenate([here_ref[...], chip_ref[...]], axis=0)
    width = first_ref.shape[1]
    gate_up = None
    for index in range(first_ref.shape[0] + second_ref.shape[0]):
        weight = (
            first_ref[index]
            if index < first_ref.shape[0]
            else second_ref[index - first_ref.shape[0]]
        )
        term = jnp.dot(
            rows[:, index * width : (index + 1) * width],
            weight,
            preferred_element_type=jnp.float32,
        )
        gate_up = term if gate_up is None else gate_up + term
    finish_rows(gate_up, cap_ref, down_ref, out_refs, per_device)


def join_kernel(*refs):
    refs[-1][...] = load_blocks(refs[:-1]).astype(refs[-1].dtype)


def flip_kernel(*refs):
    refs[-1][...] = load_blocks(refs[:-1], 1).astype(refs[-1].dtype)


def sum_kernel(count, *refs):
    total = refs[0][...].astype(jnp.float32)
    for ref in refs[1:count]:
        total = total + ref[...].astype(jnp.float32)
    store_blocks(refs[count:], total)


def combine_kernel(weight_ref, residual_ref, *refs):
    rows = load_blocks(refs[:-1], 0).astype(jnp.bfloat16)
    mixture = jnp.dot(
        weight_ref[:, : rows.shape[0]], rows, preferred_element_type=jnp.float32
    )
    refs[-1][...] = residual_ref[...].astype(jnp.float32) + mixture


def finish_kernel(weight_ref, sum_ref, core_ref, out_ref):
    mixture = jnp.dot(
        weight_ref[:, core_ref.shape[0] :],
        core_ref[...],
        preferred_element_type=jnp.float32,
    )
    out_ref[...] = (sum_ref[...] + mixture).astype(jnp.bfloat16)


def call(kernel, name, outs, *args, scratch=(), hbm=(), after=()):
    count = len(after)
    hbm = [pltpu.with_memory_space_constraint(a, pltpu.HBM) for a in hbm]
    size = sum(a.size * a.dtype.itemsize for a in (*args, *outs))
    return pl.pallas_call(
        lambda *refs: kernel(*refs[count:]),
        in_specs=[pl.BlockSpec(memory_space=pl.ANY)] * count
        + [pl.BlockSpec(memory_space=pltpu.HBM)] * len(hbm)
        + [pl.BlockSpec(memory_space=pltpu.VMEM)] * len(args),
        out_specs=[pl.BlockSpec(memory_space=pltpu.VMEM)] * len(outs),
        out_shape=outs,
        scratch_shapes=scratch,
        compiler_params=pltpu.CompilerParams(vmem_limit_bytes=size + (8 << 20)),
        cost_estimate=pl.CostEstimate(flops=1, bytes_accessed=1, transcendentals=0),
        name=name,
    )(*after, *hbm, *args)


def on_device(
    tokens,
    norm_gain,
    routing_projection_matrix,
    experts,
    replica_key,
    slot_expert,
    capacity,
    slot_gate_up_weight,
    down_weight,
):
    peers = lax.axis_size("expert")
    groups = lax.axis_size("dp")
    rows, width = tokens.shape
    slots = slot_expert.shape[0]
    per_device = slots // peers
    units = slot_gate_up_weight.shape[3]
    quarter = width // groups
    chips = peers // 2
    far = range(2, chips)[::-1]
    meet = [0, groups - 1, *range(1, groups - 1)]

    def blocks(count, *shape, dtype=jnp.bfloat16):
        return [jax.ShapeDtypeStruct(shape, dtype)] * count

    def to_group(value, step):
        return lax.ppermute(value, "dp", [(i, i ^ step) for i in range(groups)])

    def to_peer(value, step):
        return lax.ppermute(value, "expert", [(i, i ^ step) for i in range(peers)])

    gain = norm_gain.reshape(width // 128, 128)
    slot_row = slot_expert.reshape(1, slots)
    cap_row = capacity.reshape(1, slots)
    down = down_weight.reshape(per_device * units, width)

    core_tokens, core_experts, core_keys = (
        to_peer(value, 1) for value in (tokens, experts.T, replica_key.T)
    )
    tokens_here, gain_here, slot_here, cap_here, local = call(
        functools.partial(place_kernel, per_device),
        "place",
        blocks(1, rows, width)
        + blocks(1, *gain.shape)
        + blocks(2, 1, slots, dtype=jnp.int32)
        + blocks(1, slots, rows, dtype=jnp.float32),
        hbm=[tokens, experts.T, replica_key.T, gain, slot_row, cap_row],
        scratch=[
            pltpu.VMEM((experts.shape[1], rows), jnp.int32),
            pltpu.VMEM((experts.shape[1], rows), jnp.int32),
            pltpu.SemaphoreType.DMA((6,)),
        ],
    )
    core_local, *far_out = call(
        functools.partial(dispatch_kernel, per_device, [2 * c for c in far]),
        "dispatch",
        blocks(1, slots, rows, dtype=jnp.float32)
        + blocks(len(far), 2 * CAP_DEV, quarter),
        tokens_here,
        core_tokens,
        gain_here,
        local,
        core_experts,
        core_keys,
        slot_here,
        cap_here,
    )
    far_in = [to_peer(value, 2 * chip) for chip, value in zip(far, far_out)]
    here_rows, chip_rows = call(
        functools.partial(near_kernel, per_device, meet, (0, 2)),
        "dispatch_near",
        blocks(2, 2 * CAP_DEV, width),
        tokens_here,
        core_tokens,
        gain_here,
        local,
        core_local,
        after=(far_out[0],),
    )
    near_ready = chip_rows
    chip_rows = to_peer(chip_rows, 2)

    halves = units // 128
    split_in = slot_gate_up_weight.reshape(per_device, width, 2, halves, 128)
    split_in = split_in.transpose(0, 1, 3, 2, 4)
    split_in = split_in.reshape(per_device, width * halves * 2, 128)
    half = groups // 2

    part = (per_device, quarter * halves * 2, 128)
    out = (quarter, per_device * 2 * units)
    first_weights, rest = call(
        functools.partial(split_first_kernel, halves, meet),
        "split_first",
        blocks(1, half, *out) + blocks(1, groups - half, *part),
        hbm=[split_in],
        scratch=[
            pltpu.VMEM((half, *part), jnp.bfloat16),
            pltpu.SemaphoreType.DMA((groups,)),
        ],
        after=(near_ready,),
    )
    (far_rows,) = call(
        join_kernel,
        "join_far",
        blocks(1, (peers - NEAR) * CAP_DEV, quarter),
        *far_in,
        after=(first_weights,),
    )
    second_weights, down_here = call(
        functools.partial(split_second_kernel, halves),
        "split_second",
        blocks(1, groups - half, *out) + blocks(1, *down.shape),
        rest,
        hbm=[down],
        scratch=[pltpu.SemaphoreType.DMA],
        after=(far_rows,),
    )

    far_parts = [far_rows] + [to_group(far_rows, step) for step in meet[1:]]
    far_sum = ()
    for step in range(groups - 1):
        weights, index = (
            (first_weights, step) if step < half else (second_weights, step - half)
        )
        far_sum = call(
            functools.partial(product_kernel, index),
            "product_far",
            blocks(
                1, far_rows.shape[0], per_device * 2 * units, dtype=jnp.float32
            ),
            far_parts[step],
            weights,
            *far_sum,
        )
    far_partials = call(
        functools.partial(far_kernel, per_device),
        "expert_far",
        blocks(groups, (peers - NEAR) * CAP_DEV, quarter),
        *far_sum,
        far_parts[-1],
        second_weights,
        cap_here,
        down_here,
    )
    near_partials = call(
        functools.partial(near_expert_kernel, per_device),
        "expert_near",
        blocks(groups, NEAR * CAP_DEV, quarter),
        here_rows,
        chip_rows,
        first_weights,
        second_weights,
        cap_here,
        down_here,
        after=(far_partials[1],),
    )

    def reduce_groups(partials, name, count, after=()):
        received = [
            to_group(partials[step], step) for step in meet[1:]
        ]
        return call(
            functools.partial(sum_kernel, groups),
            name,
            blocks(count, 2 * CAP_DEV, quarter),
            partials[0],
            *received,
            after=after,
        )

    far_back = reduce_groups(far_partials, "sum_far", chips - 2)
    near_back = reduce_groups(near_partials, "sum_near", 2, far_back[:1])
    far_back = [to_peer(value, 2 * chip) for chip, value in zip(far, far_back)]
    back = [*far_back, near_back[0], to_peer(near_back[1], 2)]
    (flip_back,) = call(
        flip_kernel, "flip_back", blocks(1, chips * CAP_DEV, quarter), *back
    )
    core_back = to_peer(flip_back, 1)

    order = [2 * c for c in (*far, 0, 1)]
    order += [step + 1 for step in order]
    weights, residual = call(
        functools.partial(weight_kernel, per_device, order),
        "combine_weights",
        blocks(1, rows, peers * CAP_DEV) + blocks(1, rows, quarter),
        tokens_here,
        gain_here,
        routing_projection_matrix.T,
        slot_here,
        local,
        scratch=[pltpu.VMEM((slots, rows), jnp.float32)],
    )
    (mixed_half,) = call(
        combine_kernel,
        "combine",
        blocks(1, rows, quarter, dtype=jnp.float32),
        weights,
        residual,
        *back,
    )
    (mixed,) = call(
        finish_kernel, "finish", blocks(1, rows, quarter), weights, mixed_half, core_back
    )
    return mixed


def solution(mesh):
    in_specs = (
        P("expert", None),
        P(),
        P(),
        P("expert", None),
        P("expert", None),
        P(),
        P(),
        P("expert", None, None, "dp"),
        P("expert", "dp", None),
    )
    return jax.shard_map(
        on_device,
        mesh=mesh,
        in_specs=in_specs,
        out_specs=P("expert", "dp"),
        check_vma=False,
    )
```

```python
import functools

import jax
import jax.numpy as jnp
from jax import lax
from jax.experimental import pallas as pl
from jax.experimental.pallas import tpu as pltpu
from jax.sharding import PartitionSpec as P

CAP_DEV = 24
NEAR = 4


def to_column(row):
    n = row.shape[1]
    eye = lax.broadcasted_iota(jnp.int32, (n, n), 0) == lax.broadcasted_iota(
        jnp.int32, (n, n), 1
    )
    wide = jnp.where(eye, jnp.broadcast_to(row, (n, n)).astype(jnp.float32), 0.0)
    return jnp.sum(wide, axis=1, keepdims=True)


def place_rows(experts_t, keys_t, slot_row, cap_row, per_device):
    slots = slot_row.shape[1]
    picks, rows = experts_t.shape
    slot_f = slot_row.astype(jnp.float32)
    cap_f = cap_row.astype(jnp.float32)
    slot_col = to_column(slot_row)
    cap_col = to_column(cap_row)
    here = lax.broadcasted_iota(jnp.int32, (slots, slots), 0)
    other = lax.broadcasted_iota(jnp.int32, (slots, slots), 1)
    same = jnp.where(slot_f == slot_col, 1.0, 0.0)
    copies = jnp.sum(same, axis=1, keepdims=True)
    earlier = other < here
    place = jnp.sum(jnp.where(earlier, same, 0.0), axis=1, keepdims=True)
    together = (here // per_device) == (other // per_device)
    offset = jnp.sum(jnp.where(earlier & together, cap_f, 0.0), axis=1, keepdims=True)
    hit = jnp.zeros((slots, rows), jnp.float32)
    key = jnp.zeros((slots, rows), jnp.float32)
    experts_f = experts_t.astype(jnp.float32)
    keys_f = keys_t.astype(jnp.float32)
    for k in range(picks):
        match = experts_f[k : k + 1, :] == slot_col
        hit = jnp.where(match, 1.0, hit)
        key = jnp.where(match, keys_f[k : k + 1, :], key)
    rest = key - jnp.floor(key * (1.0 / copies)) * copies
    rest = jnp.where(rest < 0.0, rest + copies, rest)
    rest = jnp.where(rest >= copies, rest - copies, rest)
    chosen = (hit > 0.0) & (rest == place)
    before = lax.broadcasted_iota(jnp.int32, (rows, rows), 0) < lax.broadcasted_iota(
        jnp.int32, (rows, rows), 1
    )
    position = jnp.dot(
        jnp.where(chosen, 1.0, 0.0).astype(jnp.bfloat16),
        jnp.where(before, 1.0, 0.0).astype(jnp.bfloat16),
        preferred_element_type=jnp.float32,
    )
    return jnp.where(chosen & (position < cap_col), position + offset, -1.0)


def row_scale(hidden):
    return lax.rsqrt(jnp.mean(hidden * hidden, axis=-1, keepdims=True) + 1e-06)


def apply_gain(scaled, gain, first):
    number = lax.broadcasted_iota(jnp.int32, gain.shape, 0)
    parts = []
    for index in range(scaled.shape[1] // 128):
        row = jnp.sum(
            jnp.where(number == first + index, gain, 0.0), axis=0, keepdims=True
        )
        parts.append(
            (scaled[:, index * 128 : (index + 1) * 128] * row).astype(jnp.bfloat16)
        )
    return jnp.concatenate(parts, axis=1)


def pick_rows(local_ref, value_ref, steps, per_device):
    rows = local_ref.shape[1]
    me = lax.axis_index("expert")
    number = lax.broadcasted_iota(jnp.int32, (CAP_DEV, rows), 0).astype(jnp.float32)
    blocks = []
    for step in steps:
        block = jnp.zeros((CAP_DEV, rows), jnp.float32)
        for index in range(per_device):
            slot = (me ^ step) * per_device + index
            value = 1.0 if value_ref is None else value_ref[pl.ds(slot, 1), :]
            block = jnp.where(local_ref[pl.ds(slot, 1), :] == number, value, block)
        blocks.append(block)
    return jnp.concatenate(blocks, axis=0)


def store_blocks(refs, value):
    top = 0
    for ref in refs:
        ref[...] = value[top : top + ref.shape[0], :].astype(ref.dtype)
        top += ref.shape[0]


def load_blocks(refs, half=None):
    values = [ref[...].astype(jnp.float32) for ref in refs]
    if half is not None:
        values = [v[half * CAP_DEV : (half + 1) * CAP_DEV, :] for v in values]
    return jnp.concatenate(values, axis=0)


def normed_part(tokens_ref, gain, start, width):
    scale = row_scale(tokens_ref[...].astype(jnp.float32))
    left = pl.multiple_of(start * width, width)
    part = tokens_ref[:, pl.ds(left, width)].astype(jnp.float32)
    return apply_gain(part * scale, gain, start * (width // 128))


def place_kernel(per_device, *refs):
    in_refs, out_refs, scratch = refs[:6], refs[6:11], refs[11:]
    tokens_ref, gain_ref, slot_ref, cap_ref, local_ref = out_refs
    experts_ref, keys_ref, arrived = scratch
    targets = (tokens_ref, experts_ref, keys_ref, gain_ref, slot_ref, cap_ref)
    copies = [
        pltpu.make_async_copy(source, target, arrived.at[index])
        for index, (source, target) in enumerate(zip(in_refs, targets))
    ]
    for copy in copies:
        copy.start()
    for copy in copies[1:]:
        copy.wait()
    local_ref[...] = place_rows(
        experts_ref[...], keys_ref[...], slot_ref[...], cap_ref[...], per_device
    )
    copies[0].wait()


def dispatch_kernel(
    per_device,
    steps,
    tokens_ref,
    core_ref,
    gain_ref,
    local_ref,
    experts_ref,
    keys_ref,
    slot_ref,
    cap_ref,
    core_local_ref,
    *out_refs,
):
    core_local_ref[...] = place_rows(
        experts_ref[...], keys_ref[...], slot_ref[...], cap_ref[...], per_device
    )
    gain = gain_ref[...].astype(jnp.float32)
    width = out_refs[0].shape[1]
    group = lax.axis_index("dp")
    rows = []
    for here, places in ((tokens_ref, local_ref), (core_ref, core_local_ref)):
        pick = pick_rows(places, None, steps, per_device).astype(jnp.bfloat16)
        normed = normed_part(here, gain, group, width)
        rows.append(jnp.dot(pick, normed, preferred_element_type=jnp.float32))
    for index, ref in enumerate(out_refs):
        block = slice(index * CAP_DEV, (index + 1) * CAP_DEV)
        ref[...] = jnp.concatenate([r[block] for r in rows], axis=0).astype(ref.dtype)


def near_kernel(
    per_device,
    meet,
    steps,
    tokens_ref,
    core_ref,
    gain_ref,
    local_ref,
    core_local_ref,
    *out_refs,
):
    gain = gain_ref[...].astype(jnp.float32)
    width = tokens_ref.shape[1] // len(meet)
    group = lax.axis_index("dp")
    sources = []
    for here, places in ((tokens_ref, local_ref), (core_ref, core_local_ref)):
        pick = pick_rows(places, None, steps, per_device).astype(jnp.bfloat16)
        sources.append((here, pick, row_scale(here[...].astype(jnp.float32))))
    for place, step in enumerate(meet):
        start = pl.multiple_of((group ^ step) * width, width)
        values = []
        for here, pick, scale in sources:
            part = here[:, pl.ds(start, width)].astype(jnp.float32)
            normed = apply_gain(part * scale, gain, (group ^ step) * (width // 128))
            values.append(jnp.dot(pick, normed, preferred_element_type=jnp.float32))
        for index, ref in enumerate(out_refs):
            block = slice(index * CAP_DEV, (index + 1) * CAP_DEV)
            ref[:, place * width : (place + 1) * width] = jnp.concatenate(
                [value[block] for value in values], axis=0
            ).astype(ref.dtype)


def weight_kernel(
    per_device,
    steps,
    tokens_ref,
    gain_ref,
    route_ref,
    slot_ref,
    local_ref,
    out_ref,
    residual_ref,
    score_ref,
):
    quarter = residual_ref.shape[1]
    start = pl.multiple_of(lax.axis_index("dp") * quarter, quarter)
    residual_ref[...] = tokens_ref[:, pl.ds(start, quarter)]
    slots = slot_ref.shape[1]
    rows = tokens_ref.shape[0]
    hidden = tokens_ref[...].astype(jnp.float32)
    gain = gain_ref[...].astype(jnp.float32)
    normed = apply_gain(hidden * row_scale(hidden), gain, 0)
    logits = lax.dot_general(
        route_ref[...],
        normed,
        (((1,), (1,)), ((), ())),
        preferred_element_type=jnp.float32,
    )
    score = 1.0 / (1.0 + jnp.exp(-logits))
    slot_col = to_column(slot_ref[...])
    by_slot = jnp.zeros((slots, rows), jnp.float32)
    for expert in range(route_ref.shape[0]):
        by_slot = jnp.where(slot_col == expert, score[expert : expert + 1, :], by_slot)
    score_ref[...] = by_slot
    weights = pick_rows(local_ref, score_ref, steps, per_device)
    out_ref[...] = weights.T.astype(jnp.bfloat16)


def split_rows(halves, in_ref, out_ref):
    tile = 256
    kinds = 2 * halves
    per_tile = tile // kinds
    slots, length, _ = in_ref.shape
    to_row = lax.broadcasted_iota(jnp.int32, (tile, tile), 0)
    from_row = lax.broadcasted_iota(jnp.int32, (tile, tile), 1)
    column = to_row // per_tile
    source = (to_row % per_tile) * kinds + (column % halves) * 2 + column // halves
    order = jnp.where(source == from_row, 1.0, 0.0).astype(jnp.bfloat16)
    for slot in range(slots):
        for index in range(0, length // tile, 2):
            low = index * tile
            pair = [
                in_ref[slot, low + side * tile : low + (side + 1) * tile, :]
                for side in range(2)
            ]
            moved = jnp.dot(
                order,
                jnp.concatenate(pair, axis=1),
                preferred_element_type=jnp.float32,
            ).astype(jnp.bfloat16)
            for side in range(2):
                top = (index + side) * per_tile
                for kind in range(kinds):
                    left = (slot * kinds + kind) * 128
                    out_ref[top : top + per_tile, left : left + 128] = moved[
                        kind * per_tile : (kind + 1) * per_tile,
                        side * 128 : (side + 1) * 128,
                    ]


def split_first_kernel(halves, meet, in_hbm, out_ref, rest_ref, in_ref, arrived):
    first, second = out_ref.shape[0], rest_ref.shape[0]
    part = in_hbm.shape[1] // (first + second)
    group = lax.axis_index("dp")
    copies = []
    for step in range(first + second):
        base = pl.multiple_of((group ^ meet[step]) * part, part)
        target = in_ref.at[step] if step < first else rest_ref.at[step - first]
        copies.append(
            pltpu.make_async_copy(
                in_hbm.at[:, pl.ds(base, part), :], target, arrived.at[step]
            )
        )
        copies[-1].start()
    for step in range(first):
        copies[step].wait()
        split_rows(halves, in_ref.at[step], out_ref.at[step])
    for copy in copies[first:]:
        copy.wait()


def split_second_kernel(halves, down_hbm, in_ref, out_ref, down_ref, arrived):
    copy = pltpu.make_async_copy(down_hbm, down_ref, arrived)
    copy.start()
    for index in range(in_ref.shape[0]):
        split_rows(halves, in_ref.at[index], out_ref.at[index])
    copy.wait()


def slot_mask(cap_ref, per_device, units):
    first = lax.axis_index("expert") * per_device
    caps = cap_ref[...].astype(jnp.float32)
    lane = lax.broadcasted_iota(jnp.int32, caps.shape, 1)
    number = lax.broadcasted_iota(jnp.int32, (CAP_DEV, units), 0).astype(jnp.float32)
    end = jnp.zeros((1, 1), jnp.float32)
    parts = []
    for slot in range(per_device):
        begin = end
        end = begin + jnp.sum(
            jnp.where(lane == first + slot, caps, 0.0), axis=1, keepdims=True
        )
        parts.append(jnp.where((number >= begin) & (number < end), 1.0, 0.0))
    return jnp.concatenate(parts, axis=1)


def finish_rows(gate_up, cap_ref, down_ref, out_refs, per_device):
    units = down_ref.shape[0] // per_device
    mask = slot_mask(cap_ref, per_device, units)
    mask = jnp.concatenate([mask] * (gate_up.shape[0] // CAP_DEV), axis=0)
    pieces = []
    for slot in range(per_device):
        left = 2 * slot * units
        gate = gate_up[:, left : left + units]
        up = gate_up[:, left + units : left + 2 * units]
        pieces.append(gate / (1.0 + jnp.exp(-gate)) * up)
    activated = jnp.where(mask > 0.0, jnp.concatenate(pieces, axis=1), 0.0)
    activated = activated.astype(jnp.bfloat16)
    group = lax.axis_index("dp")
    for step, ref in enumerate(out_refs):
        width = ref.shape[1]
        start = pl.multiple_of((group ^ step) * width, width)
        ref[...] = jnp.dot(
            activated,
            down_ref[:, pl.ds(start, width)],
            preferred_element_type=jnp.float32,
        ).astype(ref.dtype)


def product_kernel(index, rows_ref, weight_ref, *refs):
    value = jnp.dot(
        rows_ref[...], weight_ref[index], preferred_element_type=jnp.float32
    )
    for ref in refs[:-1]:
        value = value + ref[...]
    refs[-1][...] = value


def far_kernel(per_device, sum_ref, last_ref, weight_ref, cap_ref, down_ref, *out_refs):
    gate_up = sum_ref[...] + jnp.dot(
        last_ref[...],
        weight_ref[weight_ref.shape[0] - 1],
        preferred_element_type=jnp.float32,
    )
    finish_rows(gate_up, cap_ref, down_ref, out_refs, per_device)


def near_expert_kernel(
    per_device, here_ref, chip_ref, first_ref, second_ref, cap_ref, down_ref, *out_refs
):
    rows = jnp.concatenate([here_ref[...], chip_ref[...]], axis=0)
    width = first_ref.shape[1]
    gate_up = None
    for index in range(first_ref.shape[0] + second_ref.shape[0]):
        weight = (
            first_ref[index]
            if index < first_ref.shape[0]
            else second_ref[index - first_ref.shape[0]]
        )
        term = jnp.dot(
            rows[:, index * width : (index + 1) * width],
            weight,
            preferred_element_type=jnp.float32,
        )
        gate_up = term if gate_up is None else gate_up + term
    finish_rows(gate_up, cap_ref, down_ref, out_refs, per_device)


def join_kernel(*refs):
    refs[-1][...] = load_blocks(refs[:-1]).astype(refs[-1].dtype)


def flip_kernel(*refs):
    refs[-1][...] = load_blocks(refs[:-1], 1).astype(refs[-1].dtype)


def sum_kernel(count, *refs):
    total = refs[0][...].astype(jnp.float32)
    for ref in refs[1:count]:
        total = total + ref[...].astype(jnp.float32)
    store_blocks(refs[count:], total)


def combine_kernel(weight_ref, residual_ref, *refs):
    rows = load_blocks(refs[:-1], 0).astype(jnp.bfloat16)
    mixture = jnp.dot(
        weight_ref[:, : rows.shape[0]], rows, preferred_element_type=jnp.float32
    )
    refs[-1][...] = residual_ref[...].astype(jnp.float32) + mixture


def finish_kernel(weight_ref, sum_ref, core_ref, out_ref):
    mixture = jnp.dot(
        weight_ref[:, core_ref.shape[0] :],
        core_ref[...],
        preferred_element_type=jnp.float32,
    )
    out_ref[...] = (sum_ref[...] + mixture).astype(jnp.bfloat16)


def call(kernel, name, outs, *args, scratch=(), hbm=(), after=()):
    count = len(after)
    hbm = [pltpu.with_memory_space_constraint(a, pltpu.HBM) for a in hbm]
    size = sum(a.size * a.dtype.itemsize for a in (*args, *outs))
    return pl.pallas_call(
        lambda *refs: kernel(*refs[count:]),
        in_specs=[pl.BlockSpec(memory_space=pl.ANY)] * count
        + [pl.BlockSpec(memory_space=pltpu.HBM)] * len(hbm)
        + [pl.BlockSpec(memory_space=pltpu.VMEM)] * len(args),
        out_specs=[pl.BlockSpec(memory_space=pltpu.VMEM)] * len(outs),
        out_shape=outs,
        scratch_shapes=scratch,
        compiler_params=pltpu.CompilerParams(vmem_limit_bytes=size + (8 << 20)),
        cost_estimate=pl.CostEstimate(flops=1, bytes_accessed=1, transcendentals=0),
        name=name,
    )(*after, *hbm, *args)


def on_device(
    tokens,
    norm_gain,
    routing_projection_matrix,
    experts,
    replica_key,
    slot_expert,
    capacity,
    slot_gate_up_weight,
    down_weight,
):
    peers = lax.axis_size("expert")
    groups = lax.axis_size("dp")
    rows, width = tokens.shape
    slots = slot_expert.shape[0]
    per_device = slots // peers
    units = slot_gate_up_weight.shape[3]
    quarter = width // groups
    chips = peers // 2
    far = range(2, chips)[::-1]
    meet = [0, groups - 1, *range(1, groups - 1)]

    def blocks(count, *shape, dtype=jnp.bfloat16):
        return [jax.ShapeDtypeStruct(shape, dtype)] * count

    def to_group(value, step):
        return lax.ppermute(value, "dp", [(i, i ^ step) for i in range(groups)])

    def to_peer(value, step):
        return lax.ppermute(value, "expert", [(i, i ^ step) for i in range(peers)])

    gain = norm_gain.reshape(width // 128, 128)
    slot_row = slot_expert.reshape(1, slots)
    cap_row = capacity.reshape(1, slots)
    down = down_weight.reshape(per_device * units, width)

    core_tokens, core_experts, core_keys = (
        to_peer(value, 1) for value in (tokens, experts.T, replica_key.T)
    )
    tokens_here, gain_here, slot_here, cap_here, local = call(
        functools.partial(place_kernel, per_device),
        "place",
        blocks(1, rows, width)
        + blocks(1, *gain.shape)
        + blocks(2, 1, slots, dtype=jnp.int32)
        + blocks(1, slots, rows, dtype=jnp.float32),
        hbm=[tokens, experts.T, replica_key.T, gain, slot_row, cap_row],
        scratch=[
            pltpu.VMEM((experts.shape[1], rows), jnp.int32),
            pltpu.VMEM((experts.shape[1], rows), jnp.int32),
            pltpu.SemaphoreType.DMA((6,)),
        ],
    )
    core_local, *far_out = call(
        functools.partial(dispatch_kernel, per_device, [2 * c for c in far]),
        "dispatch",
        blocks(1, slots, rows, dtype=jnp.float32)
        + blocks(len(far), 2 * CAP_DEV, quarter),
        tokens_here,
        core_tokens,
        gain_here,
        local,
        core_experts,
        core_keys,
        slot_here,
        cap_here,
    )
    far_in = [to_peer(value, 2 * chip) for chip, value in zip(far, far_out)]
    here_rows, chip_rows = call(
        functools.partial(near_kernel, per_device, meet, (0, 2)),
        "dispatch_near",
        blocks(2, 2 * CAP_DEV, width),
        tokens_here,
        core_tokens,
        gain_here,
        local,
        core_local,
        after=(far_out[0],),
    )
    near_ready = chip_rows
    chip_rows = to_peer(chip_rows, 2)

    halves = units // 128
    split_in = slot_gate_up_weight.reshape(per_device, width, 2, halves, 128)
    split_in = split_in.transpose(0, 1, 3, 2, 4)
    split_in = split_in.reshape(per_device, width * halves * 2, 128)
    half = groups // 2

    part = (per_device, quarter * halves * 2, 128)
    out = (quarter, per_device * 2 * units)
    first_weights, rest = call(
        functools.partial(split_first_kernel, halves, meet),
        "split_first",
        blocks(1, half, *out) + blocks(1, groups - half, *part),
        hbm=[split_in],
        scratch=[
            pltpu.VMEM((half, *part), jnp.bfloat16),
            pltpu.SemaphoreType.DMA((groups,)),
        ],
        after=(near_ready,),
    )
    (far_rows,) = call(
        join_kernel,
        "join_far",
        blocks(1, (peers - NEAR) * CAP_DEV, quarter),
        *far_in,
        after=(first_weights,),
    )
    second_weights, down_here = call(
        functools.partial(split_second_kernel, halves),
        "split_second",
        blocks(1, groups - half, *out) + blocks(1, *down.shape),
        rest,
        hbm=[down],
        scratch=[pltpu.SemaphoreType.DMA],
        after=(far_rows,),
    )

    far_parts = [far_rows] + [to_group(far_rows, step) for step in meet[1:]]
    far_sum = ()
    for step in range(groups - 1):
        weights, index = (
            (first_weights, step) if step < half else (second_weights, step - half)
        )
        far_sum = call(
            functools.partial(product_kernel, index),
            "product_far",
            blocks(
                1, far_rows.shape[0], per_device * 2 * units, dtype=jnp.float32
            ),
            far_parts[step],
            weights,
            *far_sum,
        )
    far_partials = call(
        functools.partial(far_kernel, per_device),
        "expert_far",
        blocks(groups, (peers - NEAR) * CAP_DEV, quarter),
        *far_sum,
        far_parts[-1],
        second_weights,
        cap_here,
        down_here,
    )
    near_partials = call(
        functools.partial(near_expert_kernel, per_device),
        "expert_near",
        blocks(groups, NEAR * CAP_DEV, quarter),
        here_rows,
        chip_rows,
        first_weights,
        second_weights,
        cap_here,
        down_here,
        after=(far_partials[1],),
    )

    def reduce_groups(partials, name, count, after=()):
        received = [
            to_group(partials[step], step) for step in meet[1:]
        ]
        return call(
            functools.partial(sum_kernel, groups),
            name,
            blocks(count, 2 * CAP_DEV, quarter),
            partials[0],
            *received,
            after=after,
        )

    far_back = reduce_groups(far_partials, "sum_far", chips - 2)
    near_back = reduce_groups(near_partials, "sum_near", 2, far_back[:1])
    far_back = [to_peer(value, 2 * chip) for chip, value in zip(far, far_back)]
    back = [*far_back, near_back[0], to_peer(near_back[1], 2)]
    (flip_back,) = call(
        flip_kernel, "flip_back", blocks(1, chips * CAP_DEV, quarter), *back
    )
    core_back = to_peer(flip_back, 1)

    order = [2 * c for c in (*far, 0, 1)]
    order += [step + 1 for step in order]
    weights, residual = call(
        functools.partial(weight_kernel, per_device, order),
        "combine_weights",
        blocks(1, rows, peers * CAP_DEV) + blocks(1, rows, quarter),
        tokens_here,
        gain_here,
        routing_projection_matrix.T,
        slot_here,
        local,
        scratch=[pltpu.VMEM((slots, rows), jnp.float32)],
    )
    (mixed_half,) = call(
        combine_kernel,
        "combine",
        blocks(1, rows, quarter, dtype=jnp.float32),
        weights,
        residual,
        *back,
    )
    (mixed,) = call(
        finish_kernel, "finish", blocks(1, rows, quarter), weights, mixed_half, core_back
    )
    return mixed


def solution(mesh):
    in_specs = (
        P("expert", None),
        P(),
        P(),
        P("expert", None),
        P("expert", None),
        P(),
        P(),
        P("expert", None, None, "dp"),
        P("expert", "dp", None),
    )
    return jax.shard_map(
        on_device,
        mesh=mesh,
        in_specs=in_specs,
        out_specs=P("expert", "dp"),
        check_vma=False,
    )
```

```python
import functools

import jax
import jax.numpy as jnp
from jax import lax
from jax.experimental import pallas as pl
from jax.experimental.pallas import tpu as pltpu
from jax.sharding import PartitionSpec as P

CAP_DEV = 24
NEAR = 4


def to_column(row):
    n = row.shape[1]
    eye = lax.broadcasted_iota(jnp.int32, (n, n), 0) == lax.broadcasted_iota(
        jnp.int32, (n, n), 1
    )
    wide = jnp.where(eye, jnp.broadcast_to(row, (n, n)).astype(jnp.float32), 0.0)
    return jnp.sum(wide, axis=1, keepdims=True)


def place_rows(experts_t, keys_t, slot_row, cap_row, per_device):
    slots = slot_row.shape[1]
    picks, rows = experts_t.shape
    slot_f = slot_row.astype(jnp.float32)
    cap_f = cap_row.astype(jnp.float32)
    slot_col = to_column(slot_row)
    cap_col = to_column(cap_row)
    here = lax.broadcasted_iota(jnp.int32, (slots, slots), 0)
    other = lax.broadcasted_iota(jnp.int32, (slots, slots), 1)
    same = jnp.where(slot_f == slot_col, 1.0, 0.0)
    copies = jnp.sum(same, axis=1, keepdims=True)
    earlier = other < here
    place = jnp.sum(jnp.where(earlier, same, 0.0), axis=1, keepdims=True)
    together = (here // per_device) == (other // per_device)
    offset = jnp.sum(jnp.where(earlier & together, cap_f, 0.0), axis=1, keepdims=True)
    hit = jnp.zeros((slots, rows), jnp.float32)
    key = jnp.zeros((slots, rows), jnp.float32)
    experts_f = experts_t.astype(jnp.float32)
    keys_f = keys_t.astype(jnp.float32)
    for k in range(picks):
        match = experts_f[k : k + 1, :] == slot_col
        hit = jnp.where(match, 1.0, hit)
        key = jnp.where(match, keys_f[k : k + 1, :], key)
    rest = key - jnp.floor(key * (1.0 / copies)) * copies
    rest = jnp.where(rest < 0.0, rest + copies, rest)
    rest = jnp.where(rest >= copies, rest - copies, rest)
    chosen = (hit > 0.0) & (rest == place)
    before = lax.broadcasted_iota(jnp.int32, (rows, rows), 0) < lax.broadcasted_iota(
        jnp.int32, (rows, rows), 1
    )
    position = jnp.dot(
        jnp.where(chosen, 1.0, 0.0).astype(jnp.bfloat16),
        jnp.where(before, 1.0, 0.0).astype(jnp.bfloat16),
        preferred_element_type=jnp.float32,
    )
    return jnp.where(chosen & (position < cap_col), position + offset, -1.0)


def row_scale(hidden):
    return lax.rsqrt(jnp.mean(hidden * hidden, axis=-1, keepdims=True) + 1e-06)


def apply_gain(scaled, gain, first):
    number = lax.broadcasted_iota(jnp.int32, gain.shape, 0)
    parts = []
    for index in range(scaled.shape[1] // 128):
        row = jnp.sum(
            jnp.where(number == first + index, gain, 0.0), axis=0, keepdims=True
        )
        parts.append(
            (scaled[:, index * 128 : (index + 1) * 128] * row).astype(jnp.bfloat16)
        )
    return jnp.concatenate(parts, axis=1)


def pick_rows(local_ref, value_ref, steps, per_device):
    rows = local_ref.shape[1]
    me = lax.axis_index("expert")
    number = lax.broadcasted_iota(jnp.int32, (CAP_DEV, rows), 0).astype(jnp.float32)
    blocks = []
    for step in steps:
        block = jnp.zeros((CAP_DEV, rows), jnp.float32)
        for index in range(per_device):
            slot = (me ^ step) * per_device + index
            value = 1.0 if value_ref is None else value_ref[pl.ds(slot, 1), :]
            block = jnp.where(local_ref[pl.ds(slot, 1), :] == number, value, block)
        blocks.append(block)
    return jnp.concatenate(blocks, axis=0)


def pick_pairs(local_ref, core_local_ref, steps, per_device):
    own = pick_rows(local_ref, None, steps, per_device)
    core = pick_rows(core_local_ref, None, steps, per_device)
    blocks = []
    for index in range(len(steps)):
        block = slice(index * CAP_DEV, (index + 1) * CAP_DEV)
        none = jnp.zeros_like(own[block])
        blocks.append(jnp.concatenate([own[block], none], axis=1))
        blocks.append(jnp.concatenate([none, core[block]], axis=1))
    return jnp.concatenate(blocks, axis=0).astype(jnp.bfloat16)


def store_blocks(refs, value):
    top = 0
    for ref in refs:
        ref[...] = value[top : top + ref.shape[0], :].astype(ref.dtype)
        top += ref.shape[0]


def load_blocks(refs, half=None):
    values = [ref[...].astype(jnp.float32) for ref in refs]
    if half is not None:
        values = [v[half * CAP_DEV : (half + 1) * CAP_DEV, :] for v in values]
    return jnp.concatenate(values, axis=0)


def normed_part(tokens_ref, gain, start, width):
    scale = row_scale(tokens_ref[...].astype(jnp.float32))
    left = pl.multiple_of(start * width, width)
    part = tokens_ref[:, pl.ds(left, width)].astype(jnp.float32)
    return apply_gain(part * scale, gain, start * (width // 128))


def place_kernel(per_device, *refs):
    in_refs, out_refs, scratch = refs[:6], refs[6:11], refs[11:]
    tokens_ref, gain_ref, slot_ref, cap_ref, local_ref = out_refs
    experts_ref, keys_ref, arrived = scratch
    targets = (tokens_ref, experts_ref, keys_ref, gain_ref, slot_ref, cap_ref)
    copies = [
        pltpu.make_async_copy(source, target, arrived.at[index])
        for index, (source, target) in enumerate(zip(in_refs, targets))
    ]
    for copy in copies:
        copy.start()
    for copy in copies[1:]:
        copy.wait()
    local_ref[...] = place_rows(
        experts_ref[...], keys_ref[...], slot_ref[...], cap_ref[...], per_device
    )
    copies[0].wait()


def dispatch_kernel(
    per_device,
    steps,
    tokens_ref,
    core_ref,
    gain_ref,
    local_ref,
    experts_ref,
    keys_ref,
    slot_ref,
    cap_ref,
    core_local_ref,
    *out_refs,
):
    core_local_ref[...] = place_rows(
        experts_ref[...], keys_ref[...], slot_ref[...], cap_ref[...], per_device
    )
    gain = gain_ref[...].astype(jnp.float32)
    width = out_refs[0].shape[1]
    group = lax.axis_index("dp")
    pick = pick_pairs(local_ref, core_local_ref, steps, per_device)
    normed = jnp.concatenate(
        [normed_part(here, gain, group, width) for here in (tokens_ref, core_ref)],
        axis=0,
    )
    store_blocks(out_refs, jnp.dot(pick, normed, preferred_element_type=jnp.float32))


def near_kernel(
    per_device,
    meet,
    steps,
    tokens_ref,
    core_ref,
    gain_ref,
    local_ref,
    core_local_ref,
    *out_refs,
):
    gain = gain_ref[...].astype(jnp.float32)
    width = tokens_ref.shape[1] // len(meet)
    group = lax.axis_index("dp")
    pick = pick_pairs(local_ref, core_local_ref, steps, per_device)
    scales = [row_scale(here[...].astype(jnp.float32)) for here in (tokens_ref, core_ref)]
    for place, step in enumerate(meet):
        start = pl.multiple_of((group ^ step) * width, width)
        parts = []
        for here, scale in zip((tokens_ref, core_ref), scales):
            part = here[:, pl.ds(start, width)].astype(jnp.float32)
            parts.append(apply_gain(part * scale, gain, (group ^ step) * (width // 128)))
        value = jnp.dot(
            pick, jnp.concatenate(parts, axis=0), preferred_element_type=jnp.float32
        )
        top = 0
        for ref in out_refs:
            ref[:, place * width : (place + 1) * width] = value[
                top : top + ref.shape[0], :
            ].astype(ref.dtype)
            top += ref.shape[0]


def weight_kernel(
    per_device,
    steps,
    tokens_ref,
    gain_ref,
    route_ref,
    slot_ref,
    local_ref,
    out_ref,
    residual_ref,
    score_ref,
):
    quarter = residual_ref.shape[1]
    start = pl.multiple_of(lax.axis_index("dp") * quarter, quarter)
    residual_ref[...] = tokens_ref[:, pl.ds(start, quarter)]
    slots = slot_ref.shape[1]
    rows = tokens_ref.shape[0]
    hidden = tokens_ref[...].astype(jnp.float32)
    gain = gain_ref[...].astype(jnp.float32)
    normed = apply_gain(hidden * row_scale(hidden), gain, 0)
    logits = lax.dot_general(
        route_ref[...],
        normed,
        (((1,), (1,)), ((), ())),
        preferred_element_type=jnp.float32,
    )
    score = 1.0 / (1.0 + jnp.exp(-logits))
    slot_col = to_column(slot_ref[...])
    by_slot = jnp.zeros((slots, rows), jnp.float32)
    for expert in range(route_ref.shape[0]):
        by_slot = jnp.where(slot_col == expert, score[expert : expert + 1, :], by_slot)
    score_ref[...] = by_slot
    weights = pick_rows(local_ref, score_ref, steps, per_device)
    out_ref[...] = weights.T.astype(jnp.bfloat16)


def split_rows(halves, in_ref, out_ref):
    tile = 256
    kinds = 2 * halves
    per_tile = tile // kinds
    slots, length, _ = in_ref.shape
    to_row = lax.broadcasted_iota(jnp.int32, (tile, tile), 0)
    from_row = lax.broadcasted_iota(jnp.int32, (tile, tile), 1)
    column = to_row // per_tile
    source = (to_row % per_tile) * kinds + (column % halves) * 2 + column // halves
    order = jnp.where(source == from_row, 1.0, 0.0).astype(jnp.bfloat16)
    for slot in range(slots):
        for index in range(0, length // tile, 2):
            low = index * tile
            pair = [
                in_ref[slot, low + side * tile : low + (side + 1) * tile, :]
                for side in range(2)
            ]
            moved = jnp.dot(
                order,
                jnp.concatenate(pair, axis=1),
                preferred_element_type=jnp.float32,
            ).astype(jnp.bfloat16)
            for side in range(2):
                top = (index + side) * per_tile
                for kind in range(kinds):
                    left = (slot * kinds + kind) * 128
                    out_ref[top : top + per_tile, left : left + 128] = moved[
                        kind * per_tile : (kind + 1) * per_tile,
                        side * 128 : (side + 1) * 128,
                    ]


def split_first_kernel(halves, meet, in_hbm, out_ref, rest_ref, in_ref, arrived):
    first, second = out_ref.shape[0], rest_ref.shape[0]
    part = in_hbm.shape[1] // (first + second)
    group = lax.axis_index("dp")
    copies = []
    for step in range(first + second):
        base = pl.multiple_of((group ^ meet[step]) * part, part)
        target = in_ref.at[step] if step < first else rest_ref.at[step - first]
        copies.append(
            pltpu.make_async_copy(
                in_hbm.at[:, pl.ds(base, part), :], target, arrived.at[step]
            )
        )
        copies[-1].start()
    for step in range(first):
        copies[step].wait()
        split_rows(halves, in_ref.at[step], out_ref.at[step])
    for copy in copies[first:]:
        copy.wait()


def split_second_kernel(halves, down_hbm, in_ref, out_ref, down_ref, arrived):
    copy = pltpu.make_async_copy(down_hbm, down_ref, arrived)
    copy.start()
    for index in range(in_ref.shape[0]):
        split_rows(halves, in_ref.at[index], out_ref.at[index])
    copy.wait()


def slot_mask(cap_ref, per_device, units):
    first = lax.axis_index("expert") * per_device
    caps = cap_ref[...].astype(jnp.float32)
    lane = lax.broadcasted_iota(jnp.int32, caps.shape, 1)
    number = lax.broadcasted_iota(jnp.int32, (CAP_DEV, units), 0).astype(jnp.float32)
    end = jnp.zeros((1, 1), jnp.float32)
    parts = []
    for slot in range(per_device):
        begin = end
        end = begin + jnp.sum(
            jnp.where(lane == first + slot, caps, 0.0), axis=1, keepdims=True
        )
        parts.append(jnp.where((number >= begin) & (number < end), 1.0, 0.0))
    return jnp.concatenate(parts, axis=1)


def finish_rows(gate_up, cap_ref, down_ref, out_refs, per_device):
    units = down_ref.shape[0] // per_device
    mask = slot_mask(cap_ref, per_device, units)
    mask = jnp.concatenate([mask] * (gate_up.shape[0] // CAP_DEV), axis=0)
    pieces = []
    for slot in range(per_device):
        left = 2 * slot * units
        gate = gate_up[:, left : left + units]
        up = gate_up[:, left + units : left + 2 * units]
        pieces.append(gate / (1.0 + jnp.exp(-gate)) * up)
    activated = jnp.where(mask > 0.0, jnp.concatenate(pieces, axis=1), 0.0)
    activated = activated.astype(jnp.bfloat16)
    group = lax.axis_index("dp")
    for step, ref in enumerate(out_refs):
        width = ref.shape[1]
        start = pl.multiple_of((group ^ step) * width, width)
        ref[...] = jnp.dot(
            activated,
            down_ref[:, pl.ds(start, width)],
            preferred_element_type=jnp.float32,
        ).astype(ref.dtype)


def product_kernel(index, rows_ref, weight_ref, *refs):
    value = jnp.dot(
        rows_ref[...], weight_ref[index], preferred_element_type=jnp.float32
    )
    for ref in refs[:-1]:
        value = value + ref[...]
    refs[-1][...] = value


def far_kernel(per_device, sum_ref, last_ref, weight_ref, cap_ref, down_ref, *out_refs):
    gate_up = sum_ref[...] + jnp.dot(
        last_ref[...],
        weight_ref[weight_ref.shape[0] - 1],
        preferred_element_type=jnp.float32,
    )
    finish_rows(gate_up, cap_ref, down_ref, out_refs, per_device)


def near_expert_kernel(
    per_device, here_ref, chip_ref, first_ref, second_ref, cap_ref, down_ref, *out_refs
):
    rows = jnp.concatenate([here_ref[...], chip_ref[...]], axis=0)
    width = first_ref.shape[1]
    gate_up = None
    for index in range(first_ref.shape[0] + second_ref.shape[0]):
        weight = (
            first_ref[index]
            if index < first_ref.shape[0]
            else second_ref[index - first_ref.shape[0]]
        )
        term = jnp.dot(
            rows[:, index * width : (index + 1) * width],
            weight,
            preferred_element_type=jnp.float32,
        )
        gate_up = term if gate_up is None else gate_up + term
    finish_rows(gate_up, cap_ref, down_ref, out_refs, per_device)


def join_kernel(*refs):
    refs[-1][...] = load_blocks(refs[:-1]).astype(refs[-1].dtype)


def flip_kernel(*refs):
    refs[-1][...] = load_blocks(refs[:-1], 1).astype(refs[-1].dtype)


def sum_kernel(count, *refs):
    total = refs[0][...].astype(jnp.float32)
    for ref in refs[1:count]:
        total = total + ref[...].astype(jnp.float32)
    store_blocks(refs[count:], total)


def combine_kernel(weight_ref, residual_ref, *refs):
    rows = load_blocks(refs[:-1], 0).astype(jnp.bfloat16)
    mixture = jnp.dot(
        weight_ref[:, : rows.shape[0]], rows, preferred_element_type=jnp.float32
    )
    refs[-1][...] = residual_ref[...].astype(jnp.float32) + mixture


def finish_kernel(weight_ref, sum_ref, core_ref, out_ref):
    mixture = jnp.dot(
        weight_ref[:, core_ref.shape[0] :],
        core_ref[...],
        preferred_element_type=jnp.float32,
    )
    out_ref[...] = (sum_ref[...] + mixture).astype(jnp.bfloat16)


def call(kernel, name, outs, *args, scratch=(), hbm=(), after=()):
    count = len(after)
    hbm = [pltpu.with_memory_space_constraint(a, pltpu.HBM) for a in hbm]
    size = sum(a.size * a.dtype.itemsize for a in (*args, *outs))
    return pl.pallas_call(
        lambda *refs: kernel(*refs[count:]),
        in_specs=[pl.BlockSpec(memory_space=pl.ANY)] * count
        + [pl.BlockSpec(memory_space=pltpu.HBM)] * len(hbm)
        + [pl.BlockSpec(memory_space=pltpu.VMEM)] * len(args),
        out_specs=[pl.BlockSpec(memory_space=pltpu.VMEM)] * len(outs),
        out_shape=outs,
        scratch_shapes=scratch,
        compiler_params=pltpu.CompilerParams(vmem_limit_bytes=size + (8 << 20)),
        cost_estimate=pl.CostEstimate(
            flops=10**8, bytes_accessed=10**5, transcendentals=0
        ),
        name=name,
    )(*after, *hbm, *args)


def on_device(
    tokens,
    norm_gain,
    routing_projection_matrix,
    experts,
    replica_key,
    slot_expert,
    capacity,
    slot_gate_up_weight,
    down_weight,
):
    peers = lax.axis_size("expert")
    groups = lax.axis_size("dp")
    rows, width = tokens.shape
    slots = slot_expert.shape[0]
    per_device = slots // peers
    units = slot_gate_up_weight.shape[3]
    quarter = width // groups
    chips = peers // 2
    far = range(2, chips)[::-1]
    meet = [0, groups - 1, *range(1, groups - 1)]

    def blocks(count, *shape, dtype=jnp.bfloat16):
        return [jax.ShapeDtypeStruct(shape, dtype)] * count

    def to_group(value, step):
        return lax.ppermute(value, "dp", [(i, i ^ step) for i in range(groups)])

    def to_peer(value, step):
        return lax.ppermute(value, "expert", [(i, i ^ step) for i in range(peers)])

    gain = norm_gain.reshape(width // 128, 128)
    slot_row = slot_expert.reshape(1, slots)
    cap_row = capacity.reshape(1, slots)
    down = down_weight.reshape(per_device * units, width)

    core_tokens, core_experts, core_keys = (
        to_peer(value, 1) for value in (tokens, experts.T, replica_key.T)
    )
    tokens_here, gain_here, slot_here, cap_here, local = call(
        functools.partial(place_kernel, per_device),
        "place",
        blocks(1, rows, width)
        + blocks(1, *gain.shape)
        + blocks(2, 1, slots, dtype=jnp.int32)
        + blocks(1, slots, rows, dtype=jnp.float32),
        hbm=[tokens, experts.T, replica_key.T, gain, slot_row, cap_row],
        scratch=[
            pltpu.VMEM((experts.shape[1], rows), jnp.int32),
            pltpu.VMEM((experts.shape[1], rows), jnp.int32),
            pltpu.SemaphoreType.DMA((6,)),
        ],
    )
    core_local, *far_out = call(
        functools.partial(dispatch_kernel, per_device, [2 * c for c in far]),
        "dispatch",
        blocks(1, slots, rows, dtype=jnp.float32)
        + blocks(len(far), 2 * CAP_DEV, quarter),
        tokens_here,
        core_tokens,
        gain_here,
        local,
        core_experts,
        core_keys,
        slot_here,
        cap_here,
    )
    far_in = [to_peer(value, 2 * chip) for chip, value in zip(far, far_out)]
    here_rows, chip_rows = call(
        functools.partial(near_kernel, per_device, meet, (0, 2)),
        "dispatch_near",
        blocks(2, 2 * CAP_DEV, width),
        tokens_here,
        core_tokens,
        gain_here,
        local,
        core_local,
        after=(far_out[0],),
    )
    near_ready = chip_rows
    chip_rows = to_peer(chip_rows, 2)

    halves = units // 128
    split_in = slot_gate_up_weight.reshape(per_device, width, 2, halves, 128)
    split_in = split_in.transpose(0, 1, 3, 2, 4)
    split_in = split_in.reshape(per_device, width * halves * 2, 128)
    half = groups // 2

    part = (per_device, quarter * halves * 2, 128)
    out = (quarter, per_device * 2 * units)
    first_weights, rest = call(
        functools.partial(split_first_kernel, halves, meet),
        "split_first",
        blocks(1, half, *out) + blocks(1, groups - half, *part),
        hbm=[split_in],
        scratch=[
            pltpu.VMEM((half, *part), jnp.bfloat16),
            pltpu.SemaphoreType.DMA((groups,)),
        ],
        after=(near_ready,),
    )
    (far_rows,) = call(
        join_kernel,
        "join_far",
        blocks(1, (peers - NEAR) * CAP_DEV, quarter),
        *far_in,
        after=(first_weights,),
    )
    second_weights, down_here = call(
        functools.partial(split_second_kernel, halves),
        "split_second",
        blocks(1, groups - half, *out) + blocks(1, *down.shape),
        rest,
        hbm=[down],
        scratch=[pltpu.SemaphoreType.DMA],
        after=(far_rows,),
    )

    far_parts = [far_rows] + [to_group(far_rows, step) for step in meet[1:]]
    far_sum = ()
    for step in range(groups - 1):
        weights, index = (
            (first_weights, step) if step < half else (second_weights, step - half)
        )
        far_sum = call(
            functools.partial(product_kernel, index),
            "product_far",
            blocks(
                1, far_rows.shape[0], per_device * 2 * units, dtype=jnp.float32
            ),
            far_parts[step],
            weights,
            *far_sum,
        )
    far_partials = call(
        functools.partial(far_kernel, per_device),
        "expert_far",
        blocks(groups, (peers - NEAR) * CAP_DEV, quarter),
        *far_sum,
        far_parts[-1],
        second_weights,
        cap_here,
        down_here,
    )
    near_partials = call(
        functools.partial(near_expert_kernel, per_device),
        "expert_near",
        blocks(groups, NEAR * CAP_DEV, quarter),
        here_rows,
        chip_rows,
        first_weights,
        second_weights,
        cap_here,
        down_here,
        after=(far_partials[1],),
    )

    def reduce_groups(partials, name, count, after=()):
        received = [
            to_group(partials[step], step) for step in meet[1:]
        ]
        return call(
            functools.partial(sum_kernel, groups),
            name,
            blocks(count, 2 * CAP_DEV, quarter),
            partials[0],
            *received,
            after=after,
        )

    far_back = reduce_groups(far_partials, "sum_far", chips - 2)
    near_back = reduce_groups(near_partials, "sum_near", 2, far_back[:1])
    far_back = [to_peer(value, 2 * chip) for chip, value in zip(far, far_back)]
    back = [*far_back, near_back[0], to_peer(near_back[1], 2)]
    (flip_back,) = call(
        flip_kernel, "flip_back", blocks(1, chips * CAP_DEV, quarter), *back
    )
    core_back = to_peer(flip_back, 1)

    order = [2 * c for c in (*far, 0, 1)]
    order += [step + 1 for step in order]
    weights, residual = call(
        functools.partial(weight_kernel, per_device, order),
        "combine_weights",
        blocks(1, rows, peers * CAP_DEV) + blocks(1, rows, quarter),
        tokens_here,
        gain_here,
        routing_projection_matrix.T,
        slot_here,
        local,
        scratch=[pltpu.VMEM((slots, rows), jnp.float32)],
    )
    (mixed_half,) = call(
        combine_kernel,
        "combine",
        blocks(1, rows, quarter, dtype=jnp.float32),
        weights,
        residual,
        *back,
    )
    (mixed,) = call(
        finish_kernel, "finish", blocks(1, rows, quarter), weights, mixed_half, core_back
    )
    return mixed


def solution(mesh):
    in_specs = (
        P("expert", None),
        P(),
        P(),
        P("expert", None),
        P("expert", None),
        P(),
        P(),
        P("expert", None, None, "dp"),
        P("expert", "dp", None),
    )
    return jax.shard_map(
        on_device,
        mesh=mesh,
        in_specs=in_specs,
        out_specs=P("expert", "dp"),
        check_vma=False,
    )
```

```python
import functools

import jax
import jax.numpy as jnp
from jax import lax
from jax.experimental import pallas as pl
from jax.experimental.pallas import tpu as pltpu
from jax.sharding import PartitionSpec as P

CAP_DEV = 24
NEAR = 4


def to_column(row):
    n = row.shape[1]
    eye = lax.broadcasted_iota(jnp.int32, (n, n), 0) == lax.broadcasted_iota(
        jnp.int32, (n, n), 1
    )
    wide = jnp.where(eye, jnp.broadcast_to(row, (n, n)).astype(jnp.float32), 0.0)
    return jnp.sum(wide, axis=1, keepdims=True)


def place_rows(experts_t, keys_t, slot_row, cap_row, per_device):
    slots = slot_row.shape[1]
    picks, rows = experts_t.shape
    slot_f = slot_row.astype(jnp.float32)
    cap_f = cap_row.astype(jnp.float32)
    slot_col = to_column(slot_row)
    cap_col = to_column(cap_row)
    here = lax.broadcasted_iota(jnp.int32, (slots, slots), 0)
    other = lax.broadcasted_iota(jnp.int32, (slots, slots), 1)
    same = jnp.where(slot_f == slot_col, 1.0, 0.0)
    copies = jnp.sum(same, axis=1, keepdims=True)
    earlier = other < here
    place = jnp.sum(jnp.where(earlier, same, 0.0), axis=1, keepdims=True)
    together = (here // per_device) == (other // per_device)
    offset = jnp.sum(jnp.where(earlier & together, cap_f, 0.0), axis=1, keepdims=True)
    hit = jnp.zeros((slots, rows), jnp.float32)
    key = jnp.zeros((slots, rows), jnp.float32)
    experts_f = experts_t.astype(jnp.float32)
    keys_f = keys_t.astype(jnp.float32)
    for k in range(picks):
        match = experts_f[k : k + 1, :] == slot_col
        hit = jnp.where(match, 1.0, hit)
        key = jnp.where(match, keys_f[k : k + 1, :], key)
    rest = key - jnp.floor(key * (1.0 / copies)) * copies
    rest = jnp.where(rest < 0.0, rest + copies, rest)
    rest = jnp.where(rest >= copies, rest - copies, rest)
    chosen = (hit > 0.0) & (rest == place)
    before = lax.broadcasted_iota(jnp.int32, (rows, rows), 0) < lax.broadcasted_iota(
        jnp.int32, (rows, rows), 1
    )
    position = jnp.dot(
        jnp.where(chosen, 1.0, 0.0).astype(jnp.bfloat16),
        jnp.where(before, 1.0, 0.0).astype(jnp.bfloat16),
        preferred_element_type=jnp.float32,
    )
    return jnp.where(chosen & (position < cap_col), position + offset, -1.0)


def row_scale(hidden):
    return lax.rsqrt(jnp.mean(hidden * hidden, axis=-1, keepdims=True) + 1e-06)


def apply_gain(scaled, gain, first):
    number = lax.broadcasted_iota(jnp.int32, gain.shape, 0)
    parts = []
    for index in range(scaled.shape[1] // 128):
        row = jnp.sum(
            jnp.where(number == first + index, gain, 0.0), axis=0, keepdims=True
        )
        parts.append(
            (scaled[:, index * 128 : (index + 1) * 128] * row).astype(jnp.bfloat16)
        )
    return jnp.concatenate(parts, axis=1)


def pick_rows(local_ref, value_ref, steps, per_device):
    rows = local_ref.shape[1]
    me = lax.axis_index("expert")
    number = lax.broadcasted_iota(jnp.int32, (CAP_DEV, rows), 0).astype(jnp.float32)
    blocks = []
    for step in steps:
        block = jnp.zeros((CAP_DEV, rows), jnp.float32)
        for index in range(per_device):
            slot = (me ^ step) * per_device + index
            value = 1.0 if value_ref is None else value_ref[pl.ds(slot, 1), :]
            block = jnp.where(local_ref[pl.ds(slot, 1), :] == number, value, block)
        blocks.append(block)
    return jnp.concatenate(blocks, axis=0)


def pick_pairs(local_ref, core_local_ref, steps, per_device):
    own = pick_rows(local_ref, None, steps, per_device)
    core = pick_rows(core_local_ref, None, steps, per_device)
    blocks = []
    for index in range(len(steps)):
        block = slice(index * CAP_DEV, (index + 1) * CAP_DEV)
        none = jnp.zeros_like(own[block])
        blocks.append(jnp.concatenate([own[block], none], axis=1))
        blocks.append(jnp.concatenate([none, core[block]], axis=1))
    return jnp.concatenate(blocks, axis=0).astype(jnp.bfloat16)


def store_blocks(refs, value):
    top = 0
    for ref in refs:
        ref[...] = value[top : top + ref.shape[0], :].astype(ref.dtype)
        top += ref.shape[0]


def load_blocks(refs, half=None):
    values = [ref[...].astype(jnp.float32) for ref in refs]
    if half is not None:
        values = [v[half * CAP_DEV : (half + 1) * CAP_DEV, :] for v in values]
    return jnp.concatenate(values, axis=0)


def normed_part(tokens_ref, gain, start, width):
    scale = row_scale(tokens_ref[...].astype(jnp.float32))
    left = pl.multiple_of(start * width, width)
    part = tokens_ref[:, pl.ds(left, width)].astype(jnp.float32)
    return apply_gain(part * scale, gain, start * (width // 128))


def place_kernel(per_device, *refs):
    in_refs, out_refs, scratch = refs[:6], refs[6:11], refs[11:]
    tokens_ref, gain_ref, slot_ref, cap_ref, local_ref = out_refs
    experts_ref, keys_ref, arrived = scratch
    targets = (tokens_ref, experts_ref, keys_ref, gain_ref, slot_ref, cap_ref)
    copies = [
        pltpu.make_async_copy(source, target, arrived.at[index])
        for index, (source, target) in enumerate(zip(in_refs, targets))
    ]
    for copy in (*copies[1:], copies[0]):
        copy.start()
    for copy in copies[1:]:
        copy.wait()
    local_ref[...] = place_rows(
        experts_ref[...], keys_ref[...], slot_ref[...], cap_ref[...], per_device
    )
    copies[0].wait()


def dispatch_kernel(
    per_device,
    steps,
    tokens_ref,
    core_ref,
    gain_ref,
    local_ref,
    experts_ref,
    keys_ref,
    slot_ref,
    cap_ref,
    core_local_ref,
    *out_refs,
):
    core_local_ref[...] = place_rows(
        experts_ref[...], keys_ref[...], slot_ref[...], cap_ref[...], per_device
    )
    gain = gain_ref[...].astype(jnp.float32)
    width = out_refs[0].shape[1]
    group = lax.axis_index("dp")
    pick = pick_pairs(local_ref, core_local_ref, steps, per_device)
    normed = jnp.concatenate(
        [normed_part(here, gain, group, width) for here in (tokens_ref, core_ref)],
        axis=0,
    )
    store_blocks(out_refs, jnp.dot(pick, normed, preferred_element_type=jnp.float32))


def near_kernel(
    per_device,
    meet,
    steps,
    tokens_ref,
    core_ref,
    gain_ref,
    local_ref,
    core_local_ref,
    *out_refs,
):
    gain = gain_ref[...].astype(jnp.float32)
    width = tokens_ref.shape[1] // len(meet)
    group = lax.axis_index("dp")
    pick = pick_pairs(local_ref, core_local_ref, steps, per_device)
    scales = [row_scale(here[...].astype(jnp.float32)) for here in (tokens_ref, core_ref)]
    for place, step in enumerate(meet):
        start = pl.multiple_of((group ^ step) * width, width)
        parts = []
        for here, scale in zip((tokens_ref, core_ref), scales):
            part = here[:, pl.ds(start, width)].astype(jnp.float32)
            parts.append(apply_gain(part * scale, gain, (group ^ step) * (width // 128)))
        value = jnp.dot(
            pick, jnp.concatenate(parts, axis=0), preferred_element_type=jnp.float32
        )
        top = 0
        for ref in out_refs:
            ref[:, place * width : (place + 1) * width] = value[
                top : top + ref.shape[0], :
            ].astype(ref.dtype)
            top += ref.shape[0]


def weight_kernel(
    per_device,
    steps,
    tokens_ref,
    gain_ref,
    route_ref,
    slot_ref,
    local_ref,
    out_ref,
    residual_ref,
    score_ref,
):
    quarter = residual_ref.shape[1]
    start = pl.multiple_of(lax.axis_index("dp") * quarter, quarter)
    residual_ref[...] = tokens_ref[:, pl.ds(start, quarter)]
    slots = slot_ref.shape[1]
    rows = tokens_ref.shape[0]
    hidden = tokens_ref[...].astype(jnp.float32)
    gain = gain_ref[...].astype(jnp.float32)
    normed = apply_gain(hidden * row_scale(hidden), gain, 0)
    logits = lax.dot_general(
        route_ref[...],
        normed,
        (((1,), (1,)), ((), ())),
        preferred_element_type=jnp.float32,
    )
    score = 1.0 / (1.0 + jnp.exp(-logits))
    slot_col = to_column(slot_ref[...])
    by_slot = jnp.zeros((slots, rows), jnp.float32)
    for expert in range(route_ref.shape[0]):
        by_slot = jnp.where(slot_col == expert, score[expert : expert + 1, :], by_slot)
    score_ref[...] = by_slot
    weights = pick_rows(local_ref, score_ref, steps, per_device)
    out_ref[...] = weights.T.astype(jnp.bfloat16)


def split_rows(halves, in_ref, out_ref):
    tile = 256
    kinds = 2 * halves
    per_tile = tile // kinds
    slots, length, _ = in_ref.shape
    to_row = lax.broadcasted_iota(jnp.int32, (tile, tile), 0)
    from_row = lax.broadcasted_iota(jnp.int32, (tile, tile), 1)
    column = to_row // per_tile
    source = (to_row % per_tile) * kinds + (column % halves) * 2 + column // halves
    order = jnp.where(source == from_row, 1.0, 0.0).astype(jnp.bfloat16)
    for slot in range(slots):
        for index in range(0, length // tile, 2):
            low = index * tile
            pair = [
                in_ref[slot, low + side * tile : low + (side + 1) * tile, :]
                for side in range(2)
            ]
            moved = jnp.dot(
                order,
                jnp.concatenate(pair, axis=1),
                preferred_element_type=jnp.float32,
            ).astype(jnp.bfloat16)
            for side in range(2):
                top = (index + side) * per_tile
                for kind in range(kinds):
                    left = (slot * kinds + kind) * 128
                    out_ref[top : top + per_tile, left : left + 128] = moved[
                        kind * per_tile : (kind + 1) * per_tile,
                        side * 128 : (side + 1) * 128,
                    ]


def split_first_kernel(halves, meet, in_hbm, out_ref, rest_ref, in_ref, arrived):
    first, second = out_ref.shape[0], rest_ref.shape[0]
    part = in_hbm.shape[1] // (first + second)
    group = lax.axis_index("dp")
    copies = []
    for step in range(first + second):
        base = pl.multiple_of((group ^ meet[step]) * part, part)
        target = in_ref.at[step] if step < first else rest_ref.at[step - first]
        copies.append(
            pltpu.make_async_copy(
                in_hbm.at[:, pl.ds(base, part), :], target, arrived.at[step]
            )
        )
        copies[-1].start()
    for step in range(first):
        copies[step].wait()
        split_rows(halves, in_ref.at[step], out_ref.at[step])
    for copy in copies[first:]:
        copy.wait()


def split_second_kernel(halves, down_hbm, in_ref, out_ref, down_ref, arrived):
    copy = pltpu.make_async_copy(down_hbm, down_ref, arrived)
    copy.start()
    for index in range(in_ref.shape[0]):
        split_rows(halves, in_ref.at[index], out_ref.at[index])
    copy.wait()


def slot_mask(cap_ref, per_device, units):
    first = lax.axis_index("expert") * per_device
    caps = cap_ref[...].astype(jnp.float32)
    lane = lax.broadcasted_iota(jnp.int32, caps.shape, 1)
    number = lax.broadcasted_iota(jnp.int32, (CAP_DEV, units), 0).astype(jnp.float32)
    end = jnp.zeros((1, 1), jnp.float32)
    parts = []
    for slot in range(per_device):
        begin = end
        end = begin + jnp.sum(
            jnp.where(lane == first + slot, caps, 0.0), axis=1, keepdims=True
        )
        parts.append(jnp.where((number >= begin) & (number < end), 1.0, 0.0))
    return jnp.concatenate(parts, axis=1)


def finish_rows(gate_up, cap_ref, down_ref, out_refs, per_device):
    units = down_ref.shape[0] // per_device
    mask = slot_mask(cap_ref, per_device, units)
    mask = jnp.concatenate([mask] * (gate_up.shape[0] // CAP_DEV), axis=0)
    pieces = []
    for slot in range(per_device):
        left = 2 * slot * units
        gate = gate_up[:, left : left + units]
        up = gate_up[:, left + units : left + 2 * units]
        pieces.append(gate / (1.0 + jnp.exp(-gate)) * up)
    activated = jnp.where(mask > 0.0, jnp.concatenate(pieces, axis=1), 0.0)
    activated = activated.astype(jnp.bfloat16)
    group = lax.axis_index("dp")
    for step, ref in enumerate(out_refs):
        width = ref.shape[1]
        start = pl.multiple_of((group ^ step) * width, width)
        ref[...] = jnp.dot(
            activated,
            down_ref[:, pl.ds(start, width)],
            preferred_element_type=jnp.float32,
        ).astype(ref.dtype)


def product_kernel(index, rows_ref, weight_ref, *refs):
    value = jnp.dot(
        rows_ref[...], weight_ref[index], preferred_element_type=jnp.float32
    )
    for ref in refs[:-1]:
        value = value + ref[...]
    refs[-1][...] = value


def far_kernel(per_device, sum_ref, last_ref, weight_ref, cap_ref, down_ref, *out_refs):
    gate_up = sum_ref[...] + jnp.dot(
        last_ref[...],
        weight_ref[weight_ref.shape[0] - 1],
        preferred_element_type=jnp.float32,
    )
    finish_rows(gate_up, cap_ref, down_ref, out_refs, per_device)


def near_expert_kernel(
    per_device, here_ref, chip_ref, first_ref, second_ref, cap_ref, down_ref, *out_refs
):
    rows = jnp.concatenate([here_ref[...], chip_ref[...]], axis=0)
    width = first_ref.shape[1]
    gate_up = None
    for index in range(first_ref.shape[0] + second_ref.shape[0]):
        weight = (
            first_ref[index]
            if index < first_ref.shape[0]
            else second_ref[index - first_ref.shape[0]]
        )
        term = jnp.dot(
            rows[:, index * width : (index + 1) * width],
            weight,
            preferred_element_type=jnp.float32,
        )
        gate_up = term if gate_up is None else gate_up + term
    finish_rows(gate_up, cap_ref, down_ref, out_refs, per_device)


def join_kernel(*refs):
    refs[-1][...] = load_blocks(refs[:-1]).astype(refs[-1].dtype)


def flip_kernel(*refs):
    refs[-1][...] = load_blocks(refs[:-1], 1).astype(refs[-1].dtype)


def sum_kernel(count, *refs):
    total = refs[0][...].astype(jnp.float32)
    for ref in refs[1:count]:
        total = total + ref[...].astype(jnp.float32)
    store_blocks(refs[count:], total)


def combine_kernel(weight_ref, residual_ref, *refs):
    rows = load_blocks(refs[:-1], 0).astype(jnp.bfloat16)
    mixture = jnp.dot(
        weight_ref[:, : rows.shape[0]], rows, preferred_element_type=jnp.float32
    )
    refs[-1][...] = residual_ref[...].astype(jnp.float32) + mixture


def finish_kernel(weight_ref, sum_ref, core_ref, out_ref):
    mixture = jnp.dot(
        weight_ref[:, core_ref.shape[0] :],
        core_ref[...],
        preferred_element_type=jnp.float32,
    )
    out_ref[...] = (sum_ref[...] + mixture).astype(jnp.bfloat16)


def call(kernel, name, outs, *args, scratch=(), hbm=(), after=()):
    count = len(after)
    hbm = [pltpu.with_memory_space_constraint(a, pltpu.HBM) for a in hbm]
    size = sum(a.size * a.dtype.itemsize for a in (*args, *outs))
    return pl.pallas_call(
        lambda *refs: kernel(*refs[count:]),
        in_specs=[pl.BlockSpec(memory_space=pl.ANY)] * count
        + [pl.BlockSpec(memory_space=pltpu.HBM)] * len(hbm)
        + [pl.BlockSpec(memory_space=pltpu.VMEM)] * len(args),
        out_specs=[pl.BlockSpec(memory_space=pltpu.VMEM)] * len(outs),
        out_shape=outs,
        scratch_shapes=scratch,
        compiler_params=pltpu.CompilerParams(vmem_limit_bytes=size + (8 << 20)),
        cost_estimate=pl.CostEstimate(
            flops=10**8, bytes_accessed=10**5, transcendentals=0
        ),
        name=name,
    )(*after, *hbm, *args)


def on_device(
    tokens,
    norm_gain,
    routing_projection_matrix,
    experts,
    replica_key,
    slot_expert,
    capacity,
    slot_gate_up_weight,
    down_weight,
):
    peers = lax.axis_size("expert")
    groups = lax.axis_size("dp")
    rows, width = tokens.shape
    slots = slot_expert.shape[0]
    per_device = slots // peers
    units = slot_gate_up_weight.shape[3]
    quarter = width // groups
    chips = peers // 2
    far = range(2, chips)[::-1]
    meet = [0, groups - 1, *range(1, groups - 1)]

    def blocks(count, *shape, dtype=jnp.bfloat16):
        return [jax.ShapeDtypeStruct(shape, dtype)] * count

    def to_group(value, step):
        return lax.ppermute(value, "dp", [(i, i ^ step) for i in range(groups)])

    def to_peer(value, step):
        return lax.ppermute(value, "expert", [(i, i ^ step) for i in range(peers)])

    gain = norm_gain.reshape(width // 128, 128)
    slot_row = slot_expert.reshape(1, slots)
    cap_row = capacity.reshape(1, slots)
    down = down_weight.reshape(per_device * units, width)

    core_tokens, core_experts, core_keys = (
        to_peer(value, 1) for value in (tokens, experts.T, replica_key.T)
    )
    tokens_here, gain_here, slot_here, cap_here, local = call(
        functools.partial(place_kernel, per_device),
        "place",
        blocks(1, rows, width)
        + blocks(1, *gain.shape)
        + blocks(2, 1, slots, dtype=jnp.int32)
        + blocks(1, slots, rows, dtype=jnp.float32),
        hbm=[tokens, experts.T, replica_key.T, gain, slot_row, cap_row],
        scratch=[
            pltpu.VMEM((experts.shape[1], rows), jnp.int32),
            pltpu.VMEM((experts.shape[1], rows), jnp.int32),
            pltpu.SemaphoreType.DMA((6,)),
        ],
    )
    core_local, *far_out = call(
        functools.partial(dispatch_kernel, per_device, [2 * c for c in far]),
        "dispatch",
        blocks(1, slots, rows, dtype=jnp.float32)
        + blocks(len(far), 2 * CAP_DEV, quarter),
        tokens_here,
        core_tokens,
        gain_here,
        local,
        core_experts,
        core_keys,
        slot_here,
        cap_here,
    )
    far_in = [to_peer(value, 2 * chip) for chip, value in zip(far, far_out)]
    here_rows, chip_rows = call(
        functools.partial(near_kernel, per_device, meet, (0, 2)),
        "dispatch_near",
        blocks(2, 2 * CAP_DEV, width),
        tokens_here,
        core_tokens,
        gain_here,
        local,
        core_local,
        after=(far_out[0],),
    )
    near_ready = chip_rows
    chip_rows = to_peer(chip_rows, 2)

    halves = units // 128
    split_in = slot_gate_up_weight.reshape(per_device, width, 2, halves, 128)
    split_in = split_in.transpose(0, 1, 3, 2, 4)
    split_in = split_in.reshape(per_device, width * halves * 2, 128)
    half = groups // 2

    part = (per_device, quarter * halves * 2, 128)
    out = (quarter, per_device * 2 * units)
    first_weights, rest = call(
        functools.partial(split_first_kernel, halves, meet),
        "split_first",
        blocks(1, half, *out) + blocks(1, groups - half, *part),
        hbm=[split_in],
        scratch=[
            pltpu.VMEM((half, *part), jnp.bfloat16),
            pltpu.SemaphoreType.DMA((groups,)),
        ],
        after=(near_ready,),
    )
    (far_rows,) = call(
        join_kernel,
        "join_far",
        blocks(1, (peers - NEAR) * CAP_DEV, quarter),
        *far_in,
        after=(first_weights,),
    )
    second_weights, down_here = call(
        functools.partial(split_second_kernel, halves),
        "split_second",
        blocks(1, groups - half, *out) + blocks(1, *down.shape),
        rest,
        hbm=[down],
        scratch=[pltpu.SemaphoreType.DMA],
        after=(far_rows,),
    )

    far_parts = [far_rows] + [to_group(far_rows, step) for step in meet[1:]]
    far_sum = ()
    for step in range(groups - 1):
        weights, index = (
            (first_weights, step) if step < half else (second_weights, step - half)
        )
        far_sum = call(
            functools.partial(product_kernel, index),
            "product_far",
            blocks(
                1, far_rows.shape[0], per_device * 2 * units, dtype=jnp.float32
            ),
            far_parts[step],
            weights,
            *far_sum,
        )
    far_partials = call(
        functools.partial(far_kernel, per_device),
        "expert_far",
        blocks(groups, (peers - NEAR) * CAP_DEV, quarter),
        *far_sum,
        far_parts[-1],
        second_weights,
        cap_here,
        down_here,
    )
    near_partials = call(
        functools.partial(near_expert_kernel, per_device),
        "expert_near",
        blocks(groups, NEAR * CAP_DEV, quarter),
        here_rows,
        chip_rows,
        first_weights,
        second_weights,
        cap_here,
        down_here,
        after=(far_partials[1],),
    )

    def reduce_groups(partials, name, count, after=()):
        received = [
            to_group(partials[step], step) for step in meet[1:]
        ]
        return call(
            functools.partial(sum_kernel, groups),
            name,
            blocks(count, 2 * CAP_DEV, quarter),
            partials[0],
            *received,
            after=after,
        )

    far_back = reduce_groups(far_partials, "sum_far", chips - 2)
    near_back = reduce_groups(near_partials, "sum_near", 2, far_back[:1])
    far_back = [to_peer(value, 2 * chip) for chip, value in zip(far, far_back)]
    back = [*far_back, near_back[0], to_peer(near_back[1], 2)]
    (flip_back,) = call(
        flip_kernel, "flip_back", blocks(1, chips * CAP_DEV, quarter), *back
    )
    core_back = to_peer(flip_back, 1)

    order = [2 * c for c in (*far, 0, 1)]
    order += [step + 1 for step in order]
    weights, residual = call(
        functools.partial(weight_kernel, per_device, order),
        "combine_weights",
        blocks(1, rows, peers * CAP_DEV) + blocks(1, rows, quarter),
        tokens_here,
        gain_here,
        routing_projection_matrix.T,
        slot_here,
        local,
        scratch=[pltpu.VMEM((slots, rows), jnp.float32)],
    )
    (mixed_half,) = call(
        combine_kernel,
        "combine",
        blocks(1, rows, quarter, dtype=jnp.float32),
        weights,
        residual,
        *back,
    )
    (mixed,) = call(
        finish_kernel, "finish", blocks(1, rows, quarter), weights, mixed_half, core_back
    )
    return mixed


def solution(mesh):
    in_specs = (
        P("expert", None),
        P(),
        P(),
        P("expert", None),
        P("expert", None),
        P(),
        P(),
        P("expert", None, None, "dp"),
        P("expert", "dp", None),
    )
    return jax.shard_map(
        on_device,
        mesh=mesh,
        in_specs=in_specs,
        out_specs=P("expert", "dp"),
        check_vma=False,
    )
```

```python
import functools

import jax
import jax.numpy as jnp
from jax import lax
from jax.experimental import pallas as pl
from jax.experimental.pallas import tpu as pltpu
from jax.sharding import PartitionSpec as P

CAP_DEV = 24
NEAR = 4


def to_column(row):
    n = row.shape[1]
    eye = lax.broadcasted_iota(jnp.int32, (n, n), 0) == lax.broadcasted_iota(
        jnp.int32, (n, n), 1
    )
    wide = jnp.where(eye, jnp.broadcast_to(row, (n, n)).astype(jnp.float32), 0.0)
    return jnp.sum(wide, axis=1, keepdims=True)


def place_rows(experts_t, keys_t, slot_row, cap_row, per_device):
    slots = slot_row.shape[1]
    picks, rows = experts_t.shape
    slot_f = slot_row.astype(jnp.float32)
    cap_f = cap_row.astype(jnp.float32)
    slot_col = to_column(slot_row)
    cap_col = to_column(cap_row)
    here = lax.broadcasted_iota(jnp.int32, (slots, slots), 0)
    other = lax.broadcasted_iota(jnp.int32, (slots, slots), 1)
    same = jnp.where(slot_f == slot_col, 1.0, 0.0)
    copies = jnp.sum(same, axis=1, keepdims=True)
    earlier = other < here
    place = jnp.sum(jnp.where(earlier, same, 0.0), axis=1, keepdims=True)
    together = (here // per_device) == (other // per_device)
    offset = jnp.sum(jnp.where(earlier & together, cap_f, 0.0), axis=1, keepdims=True)
    hit = jnp.zeros((slots, rows), jnp.float32)
    key = jnp.zeros((slots, rows), jnp.float32)
    experts_f = experts_t.astype(jnp.float32)
    keys_f = keys_t.astype(jnp.float32)
    for k in range(picks):
        match = experts_f[k : k + 1, :] == slot_col
        hit = jnp.where(match, 1.0, hit)
        key = jnp.where(match, keys_f[k : k + 1, :], key)
    rest = key - jnp.floor(key * (1.0 / copies)) * copies
    rest = jnp.where(rest < 0.0, rest + copies, rest)
    rest = jnp.where(rest >= copies, rest - copies, rest)
    chosen = (hit > 0.0) & (rest == place)
    before = lax.broadcasted_iota(jnp.int32, (rows, rows), 0) < lax.broadcasted_iota(
        jnp.int32, (rows, rows), 1
    )
    position = jnp.dot(
        jnp.where(chosen, 1.0, 0.0).astype(jnp.bfloat16),
        jnp.where(before, 1.0, 0.0).astype(jnp.bfloat16),
        preferred_element_type=jnp.float32,
    )
    return jnp.where(chosen & (position < cap_col), position + offset, -1.0)


def row_scale(hidden):
    return lax.rsqrt(jnp.mean(hidden * hidden, axis=-1, keepdims=True) + 1e-06)


def apply_gain(scaled, gain, first):
    number = lax.broadcasted_iota(jnp.int32, gain.shape, 0)
    parts = []
    for index in range(scaled.shape[1] // 128):
        row = jnp.sum(
            jnp.where(number == first + index, gain, 0.0), axis=0, keepdims=True
        )
        parts.append(
            (scaled[:, index * 128 : (index + 1) * 128] * row).astype(jnp.bfloat16)
        )
    return jnp.concatenate(parts, axis=1)


def pick_rows(local_ref, value_ref, steps, per_device):
    rows = local_ref.shape[1]
    me = lax.axis_index("expert")
    number = lax.broadcasted_iota(jnp.int32, (CAP_DEV, rows), 0).astype(jnp.float32)
    blocks = []
    for step in steps:
        block = jnp.zeros((CAP_DEV, rows), jnp.float32)
        for index in range(per_device):
            slot = (me ^ step) * per_device + index
            value = 1.0 if value_ref is None else value_ref[pl.ds(slot, 1), :]
            block = jnp.where(local_ref[pl.ds(slot, 1), :] == number, value, block)
        blocks.append(block)
    return jnp.concatenate(blocks, axis=0)


def pick_pairs(local_ref, core_local_ref, steps, per_device):
    own = pick_rows(local_ref, None, steps, per_device)
    core = pick_rows(core_local_ref, None, steps, per_device)
    blocks = []
    for index in range(len(steps)):
        block = slice(index * CAP_DEV, (index + 1) * CAP_DEV)
        none = jnp.zeros_like(own[block])
        blocks.append(jnp.concatenate([own[block], none], axis=1))
        blocks.append(jnp.concatenate([none, core[block]], axis=1))
    return jnp.concatenate(blocks, axis=0).astype(jnp.bfloat16)


def store_blocks(refs, value):
    top = 0
    for ref in refs:
        ref[...] = value[top : top + ref.shape[0], :].astype(ref.dtype)
        top += ref.shape[0]


def load_blocks(refs, half=None):
    values = [ref[...].astype(jnp.float32) for ref in refs]
    if half is not None:
        values = [v[half * CAP_DEV : (half + 1) * CAP_DEV, :] for v in values]
    return jnp.concatenate(values, axis=0)


def normed_part(tokens_ref, gain, start, width):
    scale = row_scale(tokens_ref[...].astype(jnp.float32))
    left = pl.multiple_of(start * width, width)
    part = tokens_ref[:, pl.ds(left, width)].astype(jnp.float32)
    return apply_gain(part * scale, gain, start * (width // 128))


def place_kernel(per_device, *refs):
    in_refs, out_refs, scratch = refs[:6], refs[6:11], refs[11:]
    tokens_ref, gain_ref, slot_ref, cap_ref, local_ref = out_refs
    experts_ref, keys_ref, arrived = scratch
    targets = (tokens_ref, experts_ref, keys_ref, gain_ref, slot_ref, cap_ref)
    copies = [
        pltpu.make_async_copy(source, target, arrived.at[index])
        for index, (source, target) in enumerate(zip(in_refs, targets))
    ]
    for copy in copies:
        copy.start()
    for copy in copies[1:]:
        copy.wait()
    local_ref[...] = place_rows(
        experts_ref[...], keys_ref[...], slot_ref[...], cap_ref[...], per_device
    )
    copies[0].wait()


def dispatch_kernel(
    per_device,
    steps,
    tokens_ref,
    core_ref,
    gain_ref,
    local_ref,
    experts_ref,
    keys_ref,
    slot_ref,
    cap_ref,
    core_local_ref,
    *out_refs,
):
    core_local_ref[...] = place_rows(
        experts_ref[...], keys_ref[...], slot_ref[...], cap_ref[...], per_device
    )
    gain = gain_ref[...].astype(jnp.float32)
    width = out_refs[0].shape[1]
    group = lax.axis_index("dp")
    pick = pick_pairs(local_ref, core_local_ref, steps, per_device)
    normed = jnp.concatenate(
        [normed_part(here, gain, group, width) for here in (tokens_ref, core_ref)],
        axis=0,
    )
    store_blocks(out_refs, jnp.dot(pick, normed, preferred_element_type=jnp.float32))


def near_kernel(
    per_device,
    meet,
    steps,
    tokens_ref,
    core_ref,
    gain_ref,
    local_ref,
    core_local_ref,
    *out_refs,
):
    gain = gain_ref[...].astype(jnp.float32)
    width = tokens_ref.shape[1] // len(meet)
    group = lax.axis_index("dp")
    pick = pick_pairs(local_ref, core_local_ref, steps, per_device)
    scales = [row_scale(here[...].astype(jnp.float32)) for here in (tokens_ref, core_ref)]
    for place, step in enumerate(meet):
        start = pl.multiple_of((group ^ step) * width, width)
        parts = []
        for here, scale in zip((tokens_ref, core_ref), scales):
            part = here[:, pl.ds(start, width)].astype(jnp.float32)
            parts.append(apply_gain(part * scale, gain, (group ^ step) * (width // 128)))
        value = jnp.dot(
            pick, jnp.concatenate(parts, axis=0), preferred_element_type=jnp.float32
        )
        top = 0
        for ref in out_refs:
            ref[:, place * width : (place + 1) * width] = value[
                top : top + ref.shape[0], :
            ].astype(ref.dtype)
            top += ref.shape[0]


def weight_kernel(
    per_device,
    steps,
    tokens_ref,
    gain_ref,
    route_ref,
    slot_ref,
    local_ref,
    out_ref,
    residual_ref,
    score_ref,
):
    quarter = residual_ref.shape[1]
    start = pl.multiple_of(lax.axis_index("dp") * quarter, quarter)
    residual_ref[...] = tokens_ref[:, pl.ds(start, quarter)]
    slots = slot_ref.shape[1]
    rows = tokens_ref.shape[0]
    hidden = tokens_ref[...].astype(jnp.float32)
    gain = gain_ref[...].astype(jnp.float32)
    normed = apply_gain(hidden * row_scale(hidden), gain, 0)
    logits = lax.dot_general(
        route_ref[...],
        normed,
        (((1,), (1,)), ((), ())),
        preferred_element_type=jnp.float32,
    )
    score = 1.0 / (1.0 + jnp.exp(-logits))
    slot_col = to_column(slot_ref[...])
    by_slot = jnp.zeros((slots, rows), jnp.float32)
    for expert in range(route_ref.shape[0]):
        by_slot = jnp.where(slot_col == expert, score[expert : expert + 1, :], by_slot)
    score_ref[...] = by_slot
    weights = pick_rows(local_ref, score_ref, steps, per_device)
    out_ref[...] = weights.T.astype(jnp.bfloat16)


def split_rows(halves, in_ref, out_ref):
    tile = 256
    kinds = 2 * halves
    per_tile = tile // kinds
    slots, length, _ = in_ref.shape
    to_row = lax.broadcasted_iota(jnp.int32, (tile, tile), 0)
    from_row = lax.broadcasted_iota(jnp.int32, (tile, tile), 1)
    column = to_row // per_tile
    source = (to_row % per_tile) * kinds + (column % halves) * 2 + column // halves
    order = jnp.where(source == from_row, 1.0, 0.0).astype(jnp.bfloat16)
    for slot in range(slots):
        for index in range(0, length // tile, 2):
            low = index * tile
            pair = [
                in_ref[slot, low + side * tile : low + (side + 1) * tile, :]
                for side in range(2)
            ]
            moved = jnp.dot(
                order,
                jnp.concatenate(pair, axis=1),
                preferred_element_type=jnp.float32,
            ).astype(jnp.bfloat16)
            for side in range(2):
                top = (index + side) * per_tile
                for kind in range(kinds):
                    left = (slot * kinds + kind) * 128
                    out_ref[top : top + per_tile, left : left + 128] = moved[
                        kind * per_tile : (kind + 1) * per_tile,
                        side * 128 : (side + 1) * 128,
                    ]


def split_first_kernel(halves, meet, in_hbm, out_ref, rest_ref, in_ref, arrived):
    first, second = out_ref.shape[0], rest_ref.shape[0]
    part = in_hbm.shape[1] // (first + second)
    group = lax.axis_index("dp")
    copies = []
    for step in range(first + second):
        base = pl.multiple_of((group ^ meet[step]) * part, part)
        target = in_ref.at[step] if step < first else rest_ref.at[step - first]
        copies.append(
            pltpu.make_async_copy(
                in_hbm.at[:, pl.ds(base, part), :], target, arrived.at[step]
            )
        )
        copies[-1].start()
    for step in range(first):
        copies[step].wait()
        split_rows(halves, in_ref.at[step], out_ref.at[step])
    for copy in copies[first:]:
        copy.wait()


def split_second_kernel(halves, down_hbm, in_ref, out_ref, down_ref, arrived):
    copy = pltpu.make_async_copy(down_hbm, down_ref, arrived)
    copy.start()
    for index in range(in_ref.shape[0]):
        split_rows(halves, in_ref.at[index], out_ref.at[index])
    copy.wait()


def slot_mask(cap_ref, per_device, units):
    first = lax.axis_index("expert") * per_device
    caps = cap_ref[...].astype(jnp.float32)
    lane = lax.broadcasted_iota(jnp.int32, caps.shape, 1)
    number = lax.broadcasted_iota(jnp.int32, (CAP_DEV, units), 0).astype(jnp.float32)
    end = jnp.zeros((1, 1), jnp.float32)
    parts = []
    for slot in range(per_device):
        begin = end
        end = begin + jnp.sum(
            jnp.where(lane == first + slot, caps, 0.0), axis=1, keepdims=True
        )
        parts.append(jnp.where((number >= begin) & (number < end), 1.0, 0.0))
    return jnp.concatenate(parts, axis=1)


def finish_rows(gate_up, cap_ref, down_ref, out_refs, per_device):
    units = down_ref.shape[0] // per_device
    mask = slot_mask(cap_ref, per_device, units)
    mask = jnp.concatenate([mask] * (gate_up.shape[0] // CAP_DEV), axis=0)
    pieces = []
    for slot in range(per_device):
        left = 2 * slot * units
        gate = gate_up[:, left : left + units]
        up = gate_up[:, left + units : left + 2 * units]
        pieces.append(gate / (1.0 + jnp.exp(-gate)) * up)
    activated = jnp.where(mask > 0.0, jnp.concatenate(pieces, axis=1), 0.0)
    activated = activated.astype(jnp.bfloat16)
    group = lax.axis_index("dp")
    for step, ref in enumerate(out_refs):
        width = ref.shape[1]
        start = pl.multiple_of((group ^ step) * width, width)
        ref[...] = jnp.dot(
            activated,
            down_ref[:, pl.ds(start, width)],
            preferred_element_type=jnp.float32,
        ).astype(ref.dtype)


def product_kernel(index, rows_ref, weight_ref, *refs):
    value = jnp.dot(
        rows_ref[...], weight_ref[index], preferred_element_type=jnp.float32
    )
    for ref in refs[:-1]:
        value = value + ref[...]
    refs[-1][...] = value


def far_kernel(per_device, sum_ref, last_ref, weight_ref, cap_ref, down_ref, *out_refs):
    gate_up = sum_ref[...] + jnp.dot(
        last_ref[...],
        weight_ref[weight_ref.shape[0] - 1],
        preferred_element_type=jnp.float32,
    )
    finish_rows(gate_up, cap_ref, down_ref, out_refs, per_device)


def near_expert_kernel(
    per_device, here_ref, chip_ref, first_ref, second_ref, cap_ref, down_ref, *out_refs
):
    rows = jnp.concatenate([here_ref[...], chip_ref[...]], axis=0)
    width = first_ref.shape[1]
    gate_up = None
    for index in range(first_ref.shape[0] + second_ref.shape[0]):
        weight = (
            first_ref[index]
            if index < first_ref.shape[0]
            else second_ref[index - first_ref.shape[0]]
        )
        term = jnp.dot(
            rows[:, index * width : (index + 1) * width],
            weight,
            preferred_element_type=jnp.float32,
        )
        gate_up = term if gate_up is None else gate_up + term
    finish_rows(gate_up, cap_ref, down_ref, out_refs, per_device)


def join_kernel(*refs):
    refs[-1][...] = load_blocks(refs[:-1]).astype(refs[-1].dtype)


def flip_kernel(*refs):
    refs[-1][...] = load_blocks(refs[:-1], 1).astype(refs[-1].dtype)


def sum_kernel(count, *refs):
    total = refs[0][...].astype(jnp.float32)
    for ref in refs[1:count]:
        total = total + ref[...].astype(jnp.float32)
    store_blocks(refs[count:], total)


def combine_kernel(weight_ref, residual_ref, *refs):
    rows = load_blocks(refs[:-1], 0).astype(jnp.bfloat16)
    mixture = jnp.dot(
        weight_ref[:, : rows.shape[0]], rows, preferred_element_type=jnp.float32
    )
    refs[-1][...] = residual_ref[...].astype(jnp.float32) + mixture


def finish_kernel(weight_ref, sum_ref, core_ref, out_ref):
    mixture = jnp.dot(
        weight_ref[:, core_ref.shape[0] :],
        core_ref[...],
        preferred_element_type=jnp.float32,
    )
    out_ref[...] = (sum_ref[...] + mixture).astype(jnp.bfloat16)


def call(kernel, name, outs, *args, scratch=(), hbm=(), after=()):
    count = len(after)
    hbm = [pltpu.with_memory_space_constraint(a, pltpu.HBM) for a in hbm]
    size = sum(a.size * a.dtype.itemsize for a in (*args, *outs))
    return pl.pallas_call(
        lambda *refs: kernel(*refs[count:]),
        in_specs=[pl.BlockSpec(memory_space=pl.ANY)] * count
        + [pl.BlockSpec(memory_space=pltpu.HBM)] * len(hbm)
        + [pl.BlockSpec(memory_space=pltpu.VMEM)] * len(args),
        out_specs=[pl.BlockSpec(memory_space=pltpu.VMEM)] * len(outs),
        out_shape=outs,
        scratch_shapes=scratch,
        compiler_params=pltpu.CompilerParams(vmem_limit_bytes=size + (8 << 20)),
        cost_estimate=pl.CostEstimate(
            flops=10**8, bytes_accessed=10**5, transcendentals=0
        ),
        name=name,
    )(*after, *hbm, *args)


def on_device(
    tokens,
    norm_gain,
    routing_projection_matrix,
    experts,
    replica_key,
    slot_expert,
    capacity,
    slot_gate_up_weight,
    down_weight,
):
    peers = lax.axis_size("expert")
    groups = lax.axis_size("dp")
    rows, width = tokens.shape
    slots = slot_expert.shape[0]
    per_device = slots // peers
    units = slot_gate_up_weight.shape[3]
    quarter = width // groups
    chips = peers // 2
    far = range(2, chips)[::-1]
    meet = [0, groups - 1, *range(1, groups - 1)]

    def blocks(count, *shape, dtype=jnp.bfloat16):
        return [jax.ShapeDtypeStruct(shape, dtype)] * count

    def to_group(value, step):
        return lax.ppermute(value, "dp", [(i, i ^ step) for i in range(groups)])

    def to_peer(value, step):
        return lax.ppermute(value, "expert", [(i, i ^ step) for i in range(peers)])

    gain = norm_gain.reshape(width // 128, 128)
    slot_row = slot_expert.reshape(1, slots)
    cap_row = capacity.reshape(1, slots)
    down = down_weight.reshape(per_device * units, width)

    core_tokens, core_experts, core_keys = (
        to_peer(value, 1) for value in (tokens, experts.T, replica_key.T)
    )
    tokens_here, gain_here, slot_here, cap_here, local = call(
        functools.partial(place_kernel, per_device),
        "place",
        blocks(1, rows, width)
        + blocks(1, *gain.shape)
        + blocks(2, 1, slots, dtype=jnp.int32)
        + blocks(1, slots, rows, dtype=jnp.float32),
        hbm=[tokens, experts.T, replica_key.T, gain, slot_row, cap_row],
        scratch=[
            pltpu.VMEM((experts.shape[1], rows), jnp.int32),
            pltpu.VMEM((experts.shape[1], rows), jnp.int32),
            pltpu.SemaphoreType.DMA((6,)),
        ],
    )
    core_local, *far_out = call(
        functools.partial(dispatch_kernel, per_device, [2 * c for c in far]),
        "dispatch",
        blocks(1, slots, rows, dtype=jnp.float32)
        + blocks(len(far), 2 * CAP_DEV, quarter),
        tokens_here,
        core_tokens,
        gain_here,
        local,
        core_experts,
        core_keys,
        slot_here,
        cap_here,
    )
    far_in = [to_peer(value, 2 * chip) for chip, value in zip(far, far_out)]
    here_rows, chip_rows = call(
        functools.partial(near_kernel, per_device, meet, (0, 2)),
        "dispatch_near",
        blocks(2, 2 * CAP_DEV, width),
        tokens_here,
        core_tokens,
        gain_here,
        local,
        core_local,
        after=(far_out[0],),
    )
    near_ready = chip_rows
    chip_rows = to_peer(chip_rows, 2)

    halves = units // 128
    split_in = slot_gate_up_weight.reshape(per_device, width, 2, halves, 128)
    split_in = split_in.transpose(0, 1, 3, 2, 4)
    split_in = split_in.reshape(per_device, width * halves * 2, 128)
    half = groups // 2

    part = (per_device, quarter * halves * 2, 128)
    out = (quarter, per_device * 2 * units)
    first_weights, rest = call(
        functools.partial(split_first_kernel, halves, meet),
        "split_first",
        blocks(1, half, *out) + blocks(1, groups - half, *part),
        hbm=[split_in],
        scratch=[
            pltpu.VMEM((half, *part), jnp.bfloat16),
            pltpu.SemaphoreType.DMA((groups,)),
        ],
        after=(near_ready,),
    )
    (far_rows,) = call(
        join_kernel,
        "join_far",
        blocks(1, (peers - NEAR) * CAP_DEV, quarter),
        *far_in,
        after=(first_weights,),
    )
    second_weights, down_here = call(
        functools.partial(split_second_kernel, halves),
        "split_second",
        blocks(1, groups - half, *out) + blocks(1, *down.shape),
        rest,
        hbm=[down],
        scratch=[pltpu.SemaphoreType.DMA],
        after=(far_rows,),
    )

    far_parts = [far_rows] + [to_group(far_rows, step) for step in meet[1:]]
    far_sum = ()
    for step in range(groups - 1):
        weights, index = (
            (first_weights, step) if step < half else (second_weights, step - half)
        )
        far_sum = call(
            functools.partial(product_kernel, index),
            "product_far",
            blocks(
                1, far_rows.shape[0], per_device * 2 * units, dtype=jnp.float32
            ),
            far_parts[step],
            weights,
            *far_sum,
        )
    far_partials = call(
        functools.partial(far_kernel, per_device),
        "expert_far",
        blocks(groups, (peers - NEAR) * CAP_DEV, quarter),
        *far_sum,
        far_parts[-1],
        second_weights,
        cap_here,
        down_here,
    )
    near_partials = call(
        functools.partial(near_expert_kernel, per_device),
        "expert_near",
        blocks(groups, NEAR * CAP_DEV, quarter),
        here_rows,
        chip_rows,
        first_weights,
        second_weights,
        cap_here,
        down_here,
        after=(far_partials[1],),
    )

    def reduce_groups(partials, name, count, after=()):
        received = [
            to_group(partials[step], step) for step in meet[1:]
        ]
        return call(
            functools.partial(sum_kernel, groups),
            name,
            blocks(count, 2 * CAP_DEV, quarter),
            partials[0],
            *received,
            after=after,
        )

    far_back = reduce_groups(far_partials, "sum_far", chips - 2)
    near_back = reduce_groups(near_partials, "sum_near", 2)
    far_back = [to_peer(value, 2 * chip) for chip, value in zip(far, far_back)]
    back = [*far_back, near_back[0], to_peer(near_back[1], 2)]
    (flip_back,) = call(
        flip_kernel, "flip_back", blocks(1, chips * CAP_DEV, quarter), *back
    )
    core_back = to_peer(flip_back, 1)

    order = [2 * c for c in (*far, 0, 1)]
    order += [step + 1 for step in order]
    weights, residual = call(
        functools.partial(weight_kernel, per_device, order),
        "combine_weights",
        blocks(1, rows, peers * CAP_DEV) + blocks(1, rows, quarter),
        tokens_here,
        gain_here,
        routing_projection_matrix.T,
        slot_here,
        local,
        scratch=[pltpu.VMEM((slots, rows), jnp.float32)],
    )
    (mixed_half,) = call(
        combine_kernel,
        "combine",
        blocks(1, rows, quarter, dtype=jnp.float32),
        weights,
        residual,
        *back,
    )
    (mixed,) = call(
        finish_kernel, "finish", blocks(1, rows, quarter), weights, mixed_half, core_back
    )
    return mixed


def solution(mesh):
    in_specs = (
        P("expert", None),
        P(),
        P(),
        P("expert", None),
        P("expert", None),
        P(),
        P(),
        P("expert", None, None, "dp"),
        P("expert", "dp", None),
    )
    return jax.shard_map(
        on_device,
        mesh=mesh,
        in_specs=in_specs,
        out_specs=P("expert", "dp"),
        check_vma=False,
    )
```
